32 devices in a mesh: seq: 4 (over x, core), fsdp: 8 (over z, y).
Axes of the slice: x: 2, y: 2, z: 4, core: 2. Of those that a mesh axis runs over, the one named last changes fastest.
Arguments:
- tokens: bfloat16 [8, 1024, 1536], P('fsdp', 'seq'), may hold values from -6 to 6
- positions: int32 [8, 1024], P('fsdp'), may hold values from 0 to 1021, as said below
- w_query: bfloat16 [1536, 1536], P('fsdp'), may hold values from -0.15625 to 0.15625
- w_key: bfloat16 [1536, 256], P('fsdp'), may hold values from -0.15625 to 0.15625
- w_value: bfloat16 [1536, 256], P('fsdp'), may hold values from -0.15625 to 0.15625
- w_output: bfloat16 [1536, 1536], P('fsdp'), may hold values from -0.625 to 0.625
- gate_up: bfloat16 [1536, 2, 8960], P('fsdp'), may hold values from -0.15625 to 0.15625
- w_down: bfloat16 [1536, 8960], P('fsdp'), may hold values from -0.0625 to 0.0625
- bias_query: bfloat16 [1536], P('fsdp'), may hold values from -3 to 3
- bias_key: bfloat16 [256], P('fsdp'), may hold values from -3 to 3
- bias_value: bfloat16 [256], P('fsdp'), may hold values from -1.1953125 to 1.1953125
- gain_attn: bfloat16 [1536], P('fsdp'), may hold values from 0.5 to 1.5
- gain_mlp: bfloat16 [1536], P('fsdp'), may hold values from 0.5 to 1.5
- cotangent: bfloat16 [8, 1024, 1536], P('fsdp', 'seq'), may hold values from -6 to 6
Outputs:
- mixed: bfloat16 [8, 1024, 1536], P('fsdp', 'seq')
- d_tokens: float32 [8, 1024, 1536], P('fsdp', 'seq')
- d_w_query: float32 [1536, 1536], P(('seq', 'fsdp'))
- d_w_key: float32 [1536, 256], P(('seq', 'fsdp'))
- d_w_value: float32 [1536, 256], P(('seq', 'fsdp'))
- d_w_output: float32 [1536, 1536], P(('seq', 'fsdp'))
- d_gate_up: float32 [1536, 2, 8960], P(('seq', 'fsdp'))
- d_w_down: float32 [1536, 8960], P(('seq', 'fsdp'))
- d_bias_query: float32 [1536], P(('seq', 'fsdp'))
- d_bias_key: float32 [256], P(('seq', 'fsdp'))
- d_bias_value: float32 [256], P(('seq', 'fsdp'))
- d_gain_attn: float32 [1536], P(('seq', 'fsdp'))
- d_gain_mlp: float32 [1536], P(('seq', 'fsdp'))
The draws below stay inside these ranges and needn't reach their ends.
Inputs may be any that keep to these rules, and one draw needn't show every extreme that they name: `positions`: each row counts up by one from 0 within each document of its sequence, and a 0 starts a new document. Every row starts with 0, and holds one document that begins at an index from 1 to 128 and whose successor begins at an index from 896 to 1023. In some row that document begins at index 1 and its successor at index 1023.
All inputs are finite; a program needn't handle non-finite values.
Results may differ from the reference program's by a relative error of at most 0.025.
Values may be sent and summed in bfloat16 or wider, within the bound.
No kernel may reach another device: no remote copies, remote signals or barrier semaphores. Data moves between devices by JAX's collectives and lax.ppermute only.
A program may use at most 640 MiB of HBM per device.

```python
import jax
import jax.numpy as jnp
from jax import lax

D = 1536
HEADS = 12
KV = 2
HD = 128
FF = 8960
LEN = 1024
SEQS = 8
HPD = 3
N_SEQ = 4


def draw_positions(key, part):
    key = jax.random.fold_in(key, 7)
    first_key, last_key, row_key = jax.random.split(key, 3)
    first_cut = jax.random.randint(first_key, (SEQS, 1), 1, LEN // 8 + 1)
    last_cut = jax.random.randint(last_key, (SEQS, 1), LEN - LEN // 8, LEN)
    chosen = jax.random.randint(row_key, (), 0, SEQS)
    row_ids = jnp.arange(SEQS, dtype=jnp.int32)[:, None]
    first_cut = jnp.where(row_ids == chosen, 1, first_cut)
    last_cut = jnp.where(row_ids == chosen, LEN - 1, last_cut)
    place_row = jnp.arange(LEN, dtype=jnp.int32)[None, :]
    doc_start = jnp.where(place_row >= last_cut, last_cut, jnp.where(place_row >= first_cut, first_cut, 0))
    return (place_row - doc_start).astype(jnp.int32)


def block_levels(own_key, dims, pieces, least, high):
    def one(dim, shards_of):
        steps = jax.random.uniform(jax.random.fold_in(jax.random.fold_in(own_key, 6), dim), (shards_of,), jnp.float32, least / len(pieces), high / len(pieces))
        return jnp.repeat(jnp.exp(steps), dims[dim] // shards_of).reshape((-1,) + (1,) * (len(dims) - dim - 1))

    gain = one(*pieces[0])
    for cut in pieces[1:]:
        gain = gain * one(*cut)
    return gain


def noise(rng, dims, spread, reach, shards=(), held_as=jnp.bfloat16):
    drawn = spread * jax.random.normal(rng, dims, jnp.float32)
    if shards:
        drawn = drawn * block_levels(rng, dims, shards, -0.22, 0.18)
    return jnp.clip(drawn, -reach, reach).astype(held_as)


def setup_inputs(seed: int = 0) -> dict:
    streams_of = jax.random.split(jax.random.key(seed), 15)
    tokens = noise(streams_of[0], (SEQS, LEN, D), 1.0, 6.0, ((0, 8), (1, 4)))
    positions = draw_positions(jax.random.fold_in(streams_of[14], 71), 0)
    w_query = noise(streams_of[2], (D, HEADS * HD), D ** -0.5, 0.15625, ((0, 8),))
    w_key = noise(streams_of[3], (D, KV * HD), D ** -0.5, 0.15625, ((0, 8),))
    w_value = noise(streams_of[4], (D, KV * HD), D ** -0.5, 0.15625, ((0, 8),))
    w_output = noise(streams_of[5], (D, HEADS * HD), (HEADS * HD // 16) ** -0.5, 0.625, ((0, 8),))
    gate_up = noise(streams_of[6], (D, 2, FF), D ** -0.5, 0.15625, ((0, 8),))
    w_down = noise(streams_of[7], (D, FF), FF ** -0.5, 0.0625, ((0, 8),))
    bias_query = noise(streams_of[8], (HEADS * HD,), 0.5, 3.0, ((0, 8),))
    bias_key = noise(streams_of[9], (KV * HD,), 0.5, 3.0, ((0, 8),))
    bias_value = noise(streams_of[10], (KV * HD,), 0.2, 1.1953125, ((0, 8),))
    gain_attn = jnp.clip(1.0 + 0.1 * jax.random.normal(streams_of[11], (D,), jnp.float32), 0.5, 1.5).astype(jnp.bfloat16)
    gain_mlp = jnp.clip(1.0 + 0.1 * jax.random.normal(streams_of[12], (D,), jnp.float32), 0.5, 1.5).astype(jnp.bfloat16)
    cotangent = noise(streams_of[13], (SEQS, LEN, D), 1.0, 6.0, ((0, 8), (1, 4)))
    return dict(tokens=tokens, positions=positions, w_query=w_query, w_key=w_key, w_value=w_value, w_output=w_output, gate_up=gate_up, w_down=w_down, bias_query=bias_query, bias_key=bias_key, bias_value=bias_value, gain_attn=gain_attn, gain_mlp=gain_mlp, cotangent=cotangent)


epsilon = 1e-06
rope_base = 1000000.0
masked_value = -1e+30
highest = lax.Precision.HIGHEST

@jax.custom_vjp
def low(v):
    return lax.optimization_barrier(v.astype(jnp.bfloat16)).astype(jnp.float32)

@jax.custom_vjp
def low_back(v):
    return v

def low_keep(v):
    return (low(v), None)

def low_pass(kept, grad):
    return (grad,)

def back_keep(v):
    return (v, None)

def back_low(kept, grad):
    return (low(grad),)
low.defvjp(low_keep, low_pass)
low_back.defvjp(back_keep, back_low)

def product(left_side, right_side):
    return jnp.dot(left_side, right_side, precision=highest, preferred_element_type=jnp.float32)

def rope_tables(positions):
    ladder = jnp.arange(HD // 2, dtype=jnp.float32)
    inverse = rope_base ** (-2.0 * ladder / HD)
    angles = positions.astype(jnp.float32)[:, None] * inverse[None, :]
    angles = jnp.concatenate([angles, angles], axis=-1)
    return (jnp.cos(angles), jnp.sin(angles))

def rotate(value, cosine, sine):
    halfway = HD // 2
    turned = jnp.concatenate([-value[..., halfway:], value[..., :halfway]], axis=-1)
    return value * cosine[:, None, :] + turned * sine[:, None, :]

def attend(queries, keys, values, documents):
    block_rows = min(512, LEN)
    key_place = jnp.arange(LEN, dtype=jnp.int32)

    def one_block(block_index):
        first_row = block_index * block_rows
        query_block = lax.dynamic_slice_in_dim(queries, first_row, block_rows, 0)
        query_place = first_row + jnp.arange(block_rows, dtype=jnp.int32)
        query_docs = lax.dynamic_slice_in_dim(documents, first_row, block_rows)
        allowed = (key_place[None, :] <= query_place[:, None]) & (documents[None, :] == query_docs[:, None])
        raw = jnp.einsum('qhd,kd->hqk', query_block, keys, precision=highest) * HD ** (-0.5)
        scores = jnp.where(allowed[None], low_back(raw), masked_value)
        row_top = lax.optimization_barrier(jnp.max(scores, axis=-1, keepdims=True))
        shifted = jnp.exp(scores - row_top)
        probability = low(shifted / lax.optimization_barrier(jnp.sum(shifted, axis=-1, keepdims=True)))
        return jnp.einsum('hqk,kd->qhd', probability, values, precision=highest)
    blocks = lax.map(jax.checkpoint(one_block), jnp.arange(LEN // block_rows, dtype=jnp.int32))
    return blocks.reshape(LEN, queries.shape[1], HD)

def block_forward(inputs, w_query, w_key, w_value, w_output, gate_up, w_down, bias_query, bias_key, bias_value, gain_attn, gain_mlp, cosine, sine, documents):
    factor_attn = lax.rsqrt(lax.optimization_barrier(jnp.mean(inputs * inputs, axis=-1, keepdims=True)) + epsilon)
    normed_attn = low(inputs * factor_attn * gain_attn)
    queries_pre = low_back(product(normed_attn, w_query) + bias_query).reshape(LEN, HEADS, HD)
    keys_pre = low_back(product(normed_attn, w_key) + bias_key).reshape(LEN, KV, HD)
    values_pre = low_back(product(normed_attn, w_value) + bias_value).reshape(LEN, KV, HD)
    queries = low_back(low(rotate(queries_pre, cosine, sine)))
    keys_dup = low_back(jnp.repeat(low(rotate(keys_pre, cosine, sine)), N_SEQ // KV, axis=1))
    values_dup = low_back(jnp.repeat(low(values_pre), N_SEQ // KV, axis=1))
    grouped = queries.reshape(LEN, N_SEQ, HPD, HD)
    outcomes = [attend(grouped[:, group], keys_dup[:, group], values_dup[:, group], documents) for group in range(N_SEQ)]
    attended = low_back(low(jnp.stack(outcomes, axis=1).reshape(LEN, HEADS * HD)))
    hidden_attn = inputs + low_back(product(attended, w_output.T))
    factor_mlp = lax.rsqrt(lax.optimization_barrier(jnp.mean(hidden_attn * hidden_attn, axis=-1, keepdims=True)) + epsilon)
    normed_mlp = low(hidden_attn * factor_mlp * gain_mlp)
    gate = low_back(product(normed_mlp, gate_up[:, 0, :]))
    upward = low_back(product(normed_mlp, gate_up[:, 1, :]))
    activated = low(jax.nn.silu(gate) * upward)
    return hidden_attn + low_back(product(activated, w_down.T))

def reference(tokens, positions, w_query, w_key, w_value, w_output, gate_up, w_down, bias_query, bias_key, bias_value, gain_attn, gain_mlp, cotangent):
    weights = tuple((weight_item.astype(jnp.float32) for weight_item in (w_query, w_key, w_value, w_output, gate_up, w_down, bias_query, bias_key, bias_value, gain_attn, gain_mlp)))

    def per_sequence(running, sequence):
        inputs, seq_positions, grad_out = sequence
        cosine, sine = rope_tables(seq_positions)
        documents = jnp.cumsum((seq_positions == 0).astype(jnp.int32)).astype(jnp.int32)

        def forward(inputs_f32, *params):
            return block_forward(inputs_f32, *params, cosine, sine, documents)
        result, pullback = jax.vjp(forward, inputs.astype(jnp.float32), *weights)
        grads = pullback(grad_out.astype(jnp.float32))
        updated = tuple((accum_value + grad_value for accum_value, grad_value in zip(running, grads[1:])))
        return (updated, (result.astype(jnp.bfloat16), grads[0]))
    zero_grads = tuple((jnp.zeros(weight_item.shape, jnp.float32) for weight_item in weights))
    totals, (mixed, d_tokens) = lax.scan(per_sequence, zero_grads, (tokens, positions, cotangent))
    return (mixed, d_tokens, totals[0], totals[1], totals[2], totals[3], totals[4], totals[5], totals[6], totals[7], totals[8], totals[9], totals[10])
```

```python
import jax
import jax.numpy as jnp
from jax import lax
from jax.sharding import PartitionSpec as P

D = 1536
HEADS = 12
KV = 2
HD = 128
FF = 8960
LANE = 128

epsilon = 1e-06
rope_base = 1000000.0
masked_value = -1e30
BF = jnp.bfloat16
F32 = jnp.float32

FF_BLOCKS = FF // LANE
CHIP_BLOCKS = -(-FF_BLOCKS // 4)
CORE_BLOCKS = CHIP_BLOCKS // 2
CORE_COLS = CORE_BLOCKS * LANE
CHIP_STARTS = (0, 18, 36, 52)
CHIP_VALID = ((0, 18), (0, 18), (0, 17), (1, 18))
CHUNKS = ((0, 768), (768, 1152))


def rope_tables(positions):
    ladder = jnp.arange(HD // 2, dtype=F32)
    inverse = rope_base ** (-2.0 * ladder / HD)
    angles = positions.astype(F32)[:, None] * inverse[None, :]
    angles = jnp.concatenate([angles, angles], axis=-1)
    return (jnp.cos(angles), jnp.sin(angles))


def rotate(value, cosine, sine):
    halfway = HD // 2
    turned = jnp.concatenate([-value[..., halfway:], value[..., :halfway]], axis=-1)
    return value * cosine[:, None, :] + turned * sine[:, None, :]


def unrotate(grad, cosine, sine):
    halfway = HD // 2
    scaled = grad * sine[:, None, :]
    turned = jnp.concatenate([scaled[..., halfway:], -scaled[..., :halfway]], axis=-1)
    return grad * cosine[:, None, :] + turned


def rms_factor(value):
    return lax.rsqrt(jnp.mean(value * value, axis=-1, keepdims=True) + epsilon)


def rms_backward(value, factor, gain, grad):
    unit = value * factor
    weighted = grad * gain
    grad_gain = jnp.sum(grad * unit, axis=0)
    inner = jnp.mean(weighted * unit, axis=-1, keepdims=True)
    return (factor * (weighted - unit * inner), grad_gain)


def masked_scores(query_block, keys, documents, first_row):
    block_rows = query_block.shape[0]
    query_place = first_row + jnp.arange(block_rows, dtype=jnp.int32)
    key_place = jnp.arange(keys.shape[0], dtype=jnp.int32)
    query_docs = lax.dynamic_slice_in_dim(documents, first_row, block_rows)
    allowed = (key_place[None, :] <= query_place[:, None]) & (
        documents[None, :] == query_docs[:, None]
    )
    raw = jnp.einsum("qhd,kd->hqk", query_block, keys, preferred_element_type=F32) * HD ** (-0.5)
    return jnp.where(allowed[None], raw, masked_value)


def attention_forward(queries, keys, values, documents):
    length = queries.shape[0]
    block_rows = min(512, length)

    def one_block(block_index):
        first_row = block_index * block_rows
        query_block = lax.dynamic_slice_in_dim(queries, first_row, block_rows, 0)
        scores = masked_scores(query_block, keys, documents, first_row)
        row_top = jnp.max(scores, axis=-1, keepdims=True)
        shifted = jnp.exp(scores - row_top)
        row_total = jnp.sum(shifted, axis=-1, keepdims=True)
        probability = (shifted / row_total).astype(BF)
        outcome = jnp.einsum("hqk,kd->qhd", probability, values, preferred_element_type=F32)
        return (outcome.astype(BF), row_top, row_total)

    outcome, tops, totals = lax.map(one_block, jnp.arange(length // block_rows, dtype=jnp.int32))
    return (outcome.reshape(queries.shape), tops, totals)


def attention_backward(queries, keys, values, documents, tops, totals, grad_attended):
    length = queries.shape[0]
    block_rows = min(512, length)
    scaling = HD ** (-0.5)

    def one_block(running, inputs_block):
        block_index, row_top, row_total = inputs_block
        first_row = block_index * block_rows
        query_block = lax.dynamic_slice_in_dim(queries, first_row, block_rows, 0)
        grad_block = lax.dynamic_slice_in_dim(grad_attended, first_row, block_rows, 0)
        scores = masked_scores(query_block, keys, documents, first_row)
        probability = jnp.exp(scores - row_top) / row_total
        prob_low = probability.astype(BF)
        grad_prob = jnp.einsum("qhd,kd->hqk", grad_block, values, preferred_element_type=F32)
        grad_scores = probability * (
            grad_prob - jnp.sum(probability * grad_prob, axis=-1, keepdims=True)
        )
        grad_low = grad_scores.astype(BF)
        grad_query = jnp.einsum("hqk,kd->qhd", grad_low, keys, preferred_element_type=F32) * scaling
        grad_keys = (
            running[0]
            + jnp.einsum("hqk,qhd->kd", grad_low, query_block, preferred_element_type=F32)
            * scaling
        )
        grad_values = running[1] + jnp.einsum(
            "hqk,qhd->kd", prob_low, grad_block, preferred_element_type=F32
        )
        return ((grad_keys, grad_values), grad_query.astype(BF))

    empty = jnp.zeros(keys.shape, F32)
    steps_in = (jnp.arange(length // block_rows, dtype=jnp.int32), tops, totals)
    (grad_keys, grad_values), grad_queries = lax.scan(one_block, (empty, empty), steps_in)
    return (grad_queries.reshape(queries.shape), grad_keys.astype(BF), grad_values.astype(BF))


def dot(left, right):
    return jnp.dot(left, right, preferred_element_type=F32)


def dot_t(left, right):
    return lax.dot_general(left, right, (((1,), (1,)), ((), ())), preferred_element_type=F32)


def t_dot(left, right):
    return lax.dot_general(left, right, (((0,), (0,)), ((), ())), preferred_element_type=F32)


def pick(array, index, axis=0):
    return lax.dynamic_index_in_dim(array, index, axis, keepdims=False)


def build(seq_count, fsdp_count):
    planes = fsdp_count // 2
    order = list(range(0, 1)) + list(range(1, planes, 2)) + list(range(2, planes, 2))[::-1]
    place = [order.index(plane) for plane in range(planes)]
    after = {order[i]: order[(i + 1) % planes] for i in range(planes)}
    ring_perm = [(2 * z + y, 2 * after[z] + y) for z in range(planes) for y in range(2)]
    y_perm = [(i, i ^ 1) for i in range(fsdp_count)]
    x_perm = [(i, i ^ 2) for i in range(seq_count)]
    c_perm = [(i, i ^ 1) for i in range(seq_count)]

    def swap_x(value):
        return lax.ppermute(value, "seq", x_perm)

    def swap_c(value):
        return lax.ppermute(value, "seq", c_perm)

    def swap_y(value):
        return lax.ppermute(value, "fsdp", y_perm)

    def ring(value):
        return lax.ppermute(value, "fsdp", ring_perm)

    def ordered(flag, first, second, axis):
        return jnp.where(
            flag == 0, jnp.stack([first, second], axis), jnp.stack([second, first], axis)
        )

    def local(
        tokens,
        positions,
        w_query,
        w_key,
        w_value,
        w_output,
        gate_up,
        w_down,
        bias_query,
        bias_key,
        bias_value,
        gain_attn,
        gain_mlp,
        cotangent,
    ):
        s = lax.axis_index("seq")
        f = lax.axis_index("fsdp")
        x, c = s // 2, s % 2
        z, y = f // 2, f % 2
        ring_order = jnp.array(order, jnp.int32)
        ring_place = jnp.array(place, jnp.int32)

        def plane_at(back):
            return ring_order[(ring_place[z] - back) % planes]

        tok_rows = tokens.shape[1]
        length = tok_rows * seq_count
        per_group = HEADS // seq_count
        group_cols = per_group * HD
        w_rows = w_query.shape[0]
        own_rows = D // (seq_count * fsdp_count)

        def ring_gather(payload):
            pieces = [payload]
            for _ in range(planes - 1):
                pieces.append(ring(pieces[-1]))
            return pieces

        def by_plane(pieces, axis):
            shape = list(pieces[0].shape)
            shape.insert(axis, planes)
            whole = jnp.zeros(shape, pieces[0].dtype)
            for back, piece in enumerate(pieces):
                whole = lax.dynamic_update_index_in_dim(whole, piece, plane_at(back), axis)
            return whole

        def gather_sequence(own):
            over_x = ordered(x, own, swap_x(own), 0)
            return ordered(c, over_x, swap_c(over_x), 1).reshape((length,) + own.shape[1:])

        def scatter_sequence(partial):
            parts = partial.reshape(2, 2, tok_rows, D)
            away = swap_c(pick(parts, 1 - c, 1).astype(BF))
            halves = pick(parts, c, 1) + away.astype(F32)
            back = swap_x(pick(halves, 1 - x).astype(BF))
            return pick(halves, x) + back.astype(F32)

        half = D // 2

        def gather_plane(own):
            first, second = own[:, :half], own[:, half:]
            a1 = swap_x(first)
            b1 = swap_y(second)
            a2 = swap_y(jnp.stack([first, a1]))
            b2 = swap_x(jnp.stack([second, b1]))
            left = jnp.concatenate([first, a2[0], a1, a2[1]], axis=0)
            right = jnp.concatenate([second, b1, b2[0], b2[1]], axis=0)
            return jnp.concatenate([left, right], axis=1)

        def scatter_plane(partial):
            parts = partial.reshape(2, 2, tok_rows, D)
            first, second = parts[..., :half], parts[..., half:]
            a1 = first[:, 0] + swap_y(first[:, 1].astype(BF)).astype(F32)
            b1 = second[0] + swap_x(second[1].astype(BF)).astype(F32)
            a2 = a1[0] + swap_x(a1[1].astype(BF)).astype(F32)
            b2 = b1[0] + swap_y(b1[1].astype(BF)).astype(F32)
            return jnp.concatenate([a2, b2], axis=1)

        kv = x
        small_row = jnp.concatenate(
            [gain_attn, gain_mlp, bias_query, bias_key, bias_value, jnp.zeros((640 - 3 * w_rows - 2 * (256 // fsdp_count),), BF)]
        )
        qkv_own = jnp.concatenate(
            [
                lax.dynamic_slice_in_dim(w_query, s * group_cols, group_cols, 1),
                lax.dynamic_slice_in_dim(w_key, kv * HD, HD, 1),
                lax.dynamic_slice_in_dim(w_value, kv * HD, HD, 1),
            ],
            axis=1,
        )
        pad_rows = jnp.zeros((15, 640), BF)
        qkv_payload = jnp.concatenate([qkv_own, small_row[None], pad_rows], axis=0)
        tokens_all = gather_sequence(tokens[0])

        def gather_attn(payload):
            mine = by_plane(ring_gather(payload), 0)
            both = ordered(y, mine, swap_y(mine), 1)
            return both.reshape((fsdp_count,) + payload.shape)

        qkv_blocks = gather_attn(qkv_payload)
        qkv_all = qkv_blocks[:, :w_rows].reshape(D, 640)
        smalls = qkv_blocks[:, w_rows]
        gain_a = smalls[:, :w_rows].reshape(D).astype(F32)
        gain_m = smalls[:, w_rows : 2 * w_rows].reshape(D).astype(F32)
        bias_q = smalls[:, 2 * w_rows : 3 * w_rows].reshape(D).astype(F32)
        kv_own = 256 // fsdp_count
        edge = 3 * w_rows
        bias_k = smalls[:, edge : edge + kv_own].reshape(KV * HD).astype(F32)
        bias_v = smalls[:, edge + kv_own : edge + 2 * kv_own].reshape(KV * HD).astype(F32)
        output_own = lax.dynamic_slice_in_dim(w_output, s * group_cols, group_cols, 1)
        output_all = gather_attn(output_own).reshape(D, group_cols)

        starts = jnp.array(CHIP_STARTS, jnp.int32)
        valid_low = jnp.array([v[0] for v in CHIP_VALID], jnp.int32)
        valid_high = jnp.array([v[1] for v in CHIP_VALID], jnp.int32)

        def columns_for(chip):
            first = (starts[chip] + c * CORE_BLOCKS) * LANE
            block = c * CORE_BLOCKS + jnp.arange(CORE_COLS, dtype=jnp.int32) // LANE
            valid = (block >= valid_low[chip]) & (block < valid_high[chip])
            both = lax.dynamic_slice_in_dim(gate_up, first, CORE_COLS, 2)
            down = lax.dynamic_slice_in_dim(w_down, first, CORE_COLS, 1)
            kinds = jnp.stack([both[:, 0], both[:, 1], down])
            return jnp.where(valid[None, None], kinds, jnp.zeros((), BF))

        chip = 2 * x + y
        kept = columns_for(chip)
        came = swap_y(columns_for(2 * x + (1 - y)))
        plane_rows = ordered(y, kept, came, 1).reshape(3, 2 * w_rows, CORE_COLS)

        mlp_weights = []
        for low, high in CHUNKS:
            mine = by_plane(ring_gather(plane_rows[:, :, low:high]), 1).reshape(3, D, high - low)
            mlp_weights.append(jnp.concatenate([mine, swap_c(mine)], axis=2))

        cot_all = gather_plane(cotangent[0])

        inputs_all = tokens_all.astype(F32)
        normed_attn = (inputs_all * rms_factor(inputs_all) * gain_a).astype(BF)
        bias_all = jnp.concatenate(
            [
                lax.dynamic_slice_in_dim(bias_q, s * group_cols, group_cols),
                lax.dynamic_slice_in_dim(bias_k, kv * HD, HD),
                lax.dynamic_slice_in_dim(bias_v, kv * HD, HD),
            ]
        )
        qkv = dot(normed_attn, qkv_all) + bias_all
        seq_positions = positions[0]
        cosine, sine = rope_tables(seq_positions)
        documents = jnp.cumsum((seq_positions == 0).astype(jnp.int32))
        turned = rotate(qkv[:, : group_cols + HD].reshape(length, per_group + 1, HD), cosine, sine)
        turned = turned.astype(BF)
        queries = turned[:, :per_group]
        keys = turned[:, per_group]
        values = qkv[:, group_cols + HD :].astype(BF)
        attended, tops, totals = attention_forward(queries, keys, values, documents)
        attended = attended.reshape(length, group_cols)
        branch_attn = scatter_sequence(dot_t(attended, output_all))

        inputs = tokens[0].astype(F32)
        hidden = inputs + branch_attn
        factor_mlp = rms_factor(hidden)
        normed_own = (hidden * factor_mlp * gain_m).astype(BF)
        normed = gather_plane(normed_own)

        grad_normed = 0.0
        branch = 0.0
        pieces = []
        for weights in mlp_weights:
            gate = dot(normed, weights[0])
            up = dot(normed, weights[1])
            grad_act = dot(cot_all, weights[2])
            sigma = jax.nn.sigmoid(gate)
            silu = gate * sigma
            activated = (silu * up).astype(BF)
            grad_gate = (grad_act * up * sigma * (1.0 + gate * (1.0 - sigma))).astype(BF)
            grad_up = (grad_act * silu).astype(BF)
            grad_normed = grad_normed + dot_t(grad_gate, weights[0]) + dot_t(grad_up, weights[1])
            branch = branch + dot_t(activated, weights[2])
            pieces.append(
                jnp.stack(
                    [
                        t_dot(normed, grad_gate).astype(BF),
                        t_dot(normed, grad_up).astype(BF),
                        t_dot(cot_all, activated).astype(BF),
                    ]
                )
            )

        def ring_scatter(block):
            running = block(plane_at(1))
            for step in range(2, planes + 1):
                running = block(plane_at(step)) + ring(running.astype(BF)).astype(F32)
            return running

        def owner_blocks(partial, cols):
            return partial.reshape(-1, 2, 2, planes, 2, own_rows, cols)

        gathered = []
        for number, (piece, (low, high)) in enumerate(zip(pieces, CHUNKS)):
            cols = 2 * (high - low)
            rows = owner_blocks(piece, cols)
            away = swap_c(pick(rows, 1 - c, 2))
            rest = pick(rows, c, 2)

            def block(plane):
                ours = pick(rest, plane, 2).astype(F32)
                theirs = pick(away, plane, 2).astype(F32)
                theirs = jnp.concatenate(
                    [theirs[..., cols // 2 :], theirs[..., : cols // 2]], axis=-1
                )
                return ours + theirs

            total = ring_scatter(block).astype(BF)
            if number % 2 == 0:
                over_x = jnp.stack([pick(total, x, 1), swap_x(pick(total, 1 - x, 1))], 1)
                both = jnp.stack([pick(over_x, y, 2), swap_y(pick(over_x, 1 - y, 2))], 2)
            else:
                over_y = jnp.stack([pick(total, y, 2), swap_y(pick(total, 1 - y, 2))], 2)
                both = jnp.stack([pick(over_y, x, 1), swap_x(pick(over_y, 1 - x, 1))], 1)
            both = jnp.where(x == 0, both, both[:, ::-1])
            both = jnp.where(y == 0, both, both[:, :, ::-1])
            halves = both.reshape(3, 4, own_rows, 2, cols // 2)
            halves = jnp.where(c == 0, halves, halves[:, :, :, ::-1])
            gathered.append(halves)
        strips = []
        for chip_index, (low, high) in enumerate(CHIP_VALID):
            whole = jnp.concatenate(
                [part[:, chip_index, :, core] for core in range(2) for part in gathered], axis=-1
            )
            strips.append(whole[..., low * LANE : high * LANE])
        d_mlp = jnp.concatenate(strips, axis=-1).astype(F32)
        d_gate_up = jnp.stack([d_mlp[0], d_mlp[1]], axis=1)
        d_w_down = d_mlp[2]

        grad_out = cotangent[0].astype(F32)
        grad_hidden_norm, grad_gain_mlp = rms_backward(
            hidden, factor_mlp, gain_m, scatter_plane(grad_normed)
        )
        result = (hidden + scatter_plane(branch)).astype(BF)
        grad_hidden = grad_out + grad_hidden_norm
        grad_hidden_low = gather_sequence(grad_hidden.astype(BF))
        grad_attended = dot(grad_hidden_low, output_all).astype(BF)
        grad_q, grad_k, grad_v = attention_backward(
            queries,
            keys,
            values,
            documents,
            tops,
            totals,
            grad_attended.reshape(length, per_group, HD),
        )
        grad_kv = jnp.stack([grad_k, grad_v])
        grad_kv = grad_kv.astype(F32) + swap_c(grad_kv).astype(F32)
        grad_k_low = unrotate(grad_kv[0][:, None], cosine, sine)[:, 0]
        grad_one = jnp.where(c == 0, grad_k_low, grad_kv[1]).astype(BF)
        grad_q_low = unrotate(grad_q.astype(F32), cosine, sine).astype(BF)
        grad_qkv = jnp.concatenate([grad_q_low.reshape(length, group_cols), grad_one], axis=1)
        one_cols = jnp.where(
            c == 0, qkv_all[:, group_cols : group_cols + HD], qkv_all[:, group_cols + HD :]
        )
        qk_all = jnp.concatenate([qkv_all[:, :group_cols], one_cols], axis=1)
        grad_normed_attn = scatter_sequence(dot_t(grad_qkv, qk_all))
        grad_input_norm, grad_gain_attn = rms_backward(
            inputs, rms_factor(inputs), gain_a, grad_normed_attn
        )
        grad_input = grad_hidden + grad_input_norm

        d_output = t_dot(grad_hidden_low, attended)
        d_qkv = t_dot(normed_attn, grad_qkv)
        bias_sums = jnp.sum(grad_qkv.astype(F32), axis=0)
        spread = jnp.zeros((2, 2, fsdp_count, own_rows), F32)
        spread_q = lax.dynamic_update_slice(
            spread, bias_sums[:group_cols].reshape(1, 1, fsdp_count, own_rows), (x, c, 0, 0)
        )
        kv_rows = KV * HD // (seq_count * fsdp_count)
        spread_kv = lax.dynamic_update_slice(
            spread, bias_sums[group_cols:].reshape(1, 2, fsdp_count, kv_rows), (x, 0, 0, 0)
        )
        smalls_out = jnp.stack(
            [grad_gain_attn, grad_gain_mlp, spread_q.reshape(D), spread_kv.reshape(D)], axis=1
        )
        smalls_out = jnp.pad(smalls_out, ((0, 0), (0, LANE - 4)))

        def to_owners(partial):
            cols = partial.shape[1]
            rows = owner_blocks(partial, cols)[0]
            away = swap_y(pick(rows, 1 - y, 3).astype(BF))
            rest = pick(rows, y, 3)

            def block(plane):
                return pick(rest, plane, 2) + pick(away, plane, 2).astype(F32)

            total = ring_scatter(block).astype(BF)
            over_x = jnp.stack([pick(total, x), swap_x(pick(total, 1 - x))], 0)
            both = jnp.stack([pick(over_x, c, 1), swap_c(pick(over_x, 1 - c, 1))], 1)
            both = jnp.where(x == 0, both, both[::-1])
            both = jnp.where(c == 0, both, both[:, ::-1])
            return both.astype(F32)

        out_blocks = to_owners(d_output)
        d_w_output = jnp.concatenate([out_blocks[i // 2, i % 2] for i in range(4)], axis=1)
        qkv_blocks_out = to_owners(jnp.concatenate([d_qkv, smalls_out], axis=1))
        d_w_query = jnp.concatenate(
            [qkv_blocks_out[i // 2, i % 2, :, :group_cols] for i in range(4)], axis=1
        )
        last = qkv_blocks_out[:, :, :, group_cols : group_cols + HD]
        d_w_key = jnp.concatenate([last[0, 0], last[1, 0]], axis=1)
        d_w_value = jnp.concatenate([last[0, 1], last[1, 1]], axis=1)
        sums = qkv_blocks_out[:, :, :, group_cols + HD :]
        d_gain_attn = jnp.sum(sums[..., 0], axis=(0, 1))
        d_gain_mlp = jnp.sum(sums[..., 1], axis=(0, 1))
        d_bias_query = jnp.sum(sums[..., 2], axis=(0, 1))
        d_bias_key = jnp.sum(sums[:, 0, :kv_rows, 3], axis=0)
        d_bias_value = jnp.sum(sums[:, 1, :kv_rows, 3], axis=0)
        return (
            result[None],
            grad_input[None],
            d_w_query,
            d_w_key,
            d_w_value,
            d_w_output,
            d_gate_up,
            d_w_down,
            d_bias_query,
            d_bias_key,
            d_bias_value,
            d_gain_attn,
            d_gain_mlp,
        )

    return local


def solution(mesh):
    rows = P("fsdp", None)
    owners = P(("seq", "fsdp"))
    return jax.shard_map(
        build(mesh.shape["seq"], mesh.shape["fsdp"]),
        mesh=mesh,
        in_specs=(
            P("fsdp", "seq", None),
            rows,
            rows,
            rows,
            rows,
            rows,
            P("fsdp", None, None),
            rows,
            P("fsdp"),
            P("fsdp"),
            P("fsdp"),
            P("fsdp"),
            P("fsdp"),
            P("fsdp", "seq", None),
        ),
        out_specs=(
            P("fsdp", "seq", None),
            P("fsdp", "seq", None),
            P(("seq", "fsdp"), None),
            P(("seq", "fsdp"), None),
            P(("seq", "fsdp"), None),
            P(("seq", "fsdp"), None),
            P(("seq", "fsdp"), None, None),
            P(("seq", "fsdp"), None),
            owners,
            owners,
            owners,
            owners,
            owners,
        ),
        check_vma=False,
    )
```

```python
import functools

import jax
import jax.numpy as jnp
from jax import lax
from jax.experimental import pallas as pl
from jax.experimental.pallas import tpu as pltpu
from jax.sharding import PartitionSpec as P

D = 1536
HEADS = 12
KV = 2
HD = 128
FF = 8960
LANE = 128

epsilon = 1e-06
rope_base = 1000000.0
masked_value = -1e30
BF = jnp.bfloat16
F32 = jnp.float32
VMEM_BYTES = 60 * 1024 * 1024

CHIP_STARTS = (0, 18, 36, 52)
CHIP_VALID = ((0, 18), (0, 18), (0, 17), (1, 18))
TILE = 256
CHUNKS = ((0, 1536), (1536, 2304))
QUERY_ROWS = 256

anywhere = pl.BlockSpec(memory_space=pl.ANY)
in_vmem = pl.BlockSpec(memory_space=pltpu.VMEM)
in_smem = pl.BlockSpec(memory_space=pltpu.SMEM)


def rope_tables(positions):
    ladder = jnp.arange(HD // 2, dtype=F32)
    inverse = rope_base ** (-2.0 * ladder / HD)
    angles = positions.astype(F32)[:, None] * inverse[None, :]
    cosine, sine = jnp.cos(angles), jnp.sin(angles)
    return (
        jnp.concatenate([cosine, cosine], axis=-1),
        jnp.concatenate([-sine, sine], axis=-1),
    )


def rms_factor(value):
    return lax.rsqrt(jnp.mean(value * value, axis=-1, keepdims=True) + epsilon)


def rms_backward(value, factor, gain, grad):
    unit = value * factor
    weighted = grad * gain
    grad_gain = jnp.sum(grad * unit, axis=0)
    inner = jnp.mean(weighted * unit, axis=-1, keepdims=True)
    return (factor * (weighted - unit * inner), grad_gain)


def dot(left, right):
    return jnp.dot(left, right, preferred_element_type=F32)


def dot_t(left, right):
    return lax.dot_general(left, right, (((1,), (1,)), ((), ())), preferred_element_type=F32)


def t_dot(left, right):
    return lax.dot_general(left, right, (((0,), (0,)), ((), ())), preferred_element_type=F32)


def pick(array, index, axis=0):
    return lax.dynamic_index_in_dim(array, index, axis, keepdims=False)


def tie(value, *others):
    return lax.optimization_barrier((value, *others))[0]


def kernel_params():
    return pltpu.CompilerParams(vmem_limit_bytes=VMEM_BYTES)


KERNEL_COST = pl.CostEstimate(flops=1_000_000, bytes_accessed=1_000_000, transcendentals=0)


def cut_body(place, gate_up, down, target, pairs, sems):
    cols = pl.ds(pl.multiple_of(place[0], LANE), target.shape[2])
    copies = [
        pltpu.make_async_copy(gate_up.at[:, :, cols], pairs, sems.at[0]),
        pltpu.make_async_copy(down.at[:, cols], target.at[2], sems.at[1]),
    ]
    for copy in copies:
        copy.start()
    copies[0].wait()
    target[0] = pairs[:, 0, :]
    target[1] = pairs[:, 1, :]
    copies[1].wait()
    empty = jnp.zeros((3, target.shape[1], LANE), BF)

    @pl.when(place[1] == 1)
    def _():
        target[:, :, 0:LANE] = empty

    @pl.when(place[1] == 2)
    def _():
        target[:, :, target.shape[2] - LANE :] = empty


def cut_columns(place, gate_up, down, cols):
    rows = down.shape[0]
    return pl.pallas_call(
        cut_body,
        out_shape=jax.ShapeDtypeStruct((3, rows, cols), BF),
        in_specs=[in_smem, anywhere, anywhere],
        out_specs=in_vmem,
        scratch_shapes=[pltpu.VMEM((rows, 2, cols), BF), pltpu.SemaphoreType.DMA((2,))],
        compiler_params=kernel_params(),
        cost_estimate=KERNEL_COST,
        name="cut_columns",
    )(place, gate_up, down)


def sequence_copies(s, sources, target, sems):
    near, far, other = sources
    rows = near.shape[0]
    x, c = s // 2, lax.rem(s, 2)
    copies = []
    for i, (source, owner) in enumerate(
        (
            (near, 2 * x + c),
            (far, 2 * (1 - x) + c),
            (other.at[0], 2 * x + 1 - c),
            (other.at[1], 2 * (1 - x) + 1 - c),
        )
    ):
        place = pl.multiple_of(owner * rows, LANE)
        copies.append(pltpu.make_async_copy(source, target.at[pl.ds(place, rows)], sems.at[i]))
    return copies


def attention_in_body(planes, rows, *refs):
    places, own = refs[0], refs[1]
    mine = refs[2 : 2 + planes]
    theirs = refs[2 + planes : 2 + 2 * planes]
    sources = refs[2 + 2 * planes : 5 + 2 * planes]
    cosine, sine, starts = refs[5 + 2 * planes : 8 + 2 * planes]
    (
        normed_t,
        queries,
        keys,
        values,
        attended,
        keep,
        send,
        weights,
        gains,
        tokens,
        small,
        sems,
        token_sems,
    ) = refs[8 + 2 * planes :]
    length = tokens.shape[0]
    group_cols = queries.shape[1]
    blocks = 2 * planes
    s, y = own[0], own[1]
    c = lax.rem(s, 2)
    copies = sequence_copies(s, sources, tokens, token_sems)
    for k in range(planes):
        for side, source in enumerate((mine[k], theirs[k])):
            block = places[k] * 2 + (y if side == 0 else 1 - y)
            first = pl.multiple_of(block * rows, 16)
            copies.append(
                pltpu.make_async_copy(
                    source.at[pl.ds(0, rows)], weights.at[pl.ds(first, rows)], sems.at[0, 2 * k + side]
                )
            )
            copies.append(
                pltpu.make_async_copy(
                    source.at[pl.ds(rows, 16)],
                    small.at[pl.ds(pl.multiple_of(block * 16, 16), 16)],
                    sems.at[1, 2 * k + side],
                )
            )
    for copy in copies:
        copy.start()
    for copy in copies:
        copy.wait()
    kv_own = KV * HD // blocks
    vectors = []
    for row, width in enumerate((rows, rows, rows, kv_own, kv_own)):
        vectors.append(
            jnp.concatenate(
                [small[pl.ds(16 * b + row, 1), 0:width].astype(F32) for b in range(blocks)], axis=1
            )
        )
    gains[0:1, :] = vectors[0]
    gains[1:2, :] = vectors[1]
    gains[2:3, :] = vectors[2]
    gains[3:4, 0 : KV * HD] = vectors[3]
    gains[4:5, 0 : KV * HD] = vectors[4]
    gain = gains[0:1, :]
    kv = s // 2
    bias = jnp.concatenate(
        [
            gains[2:3, pl.ds(pl.multiple_of(s * group_cols, LANE), group_cols)],
            gains[3:4, pl.ds(pl.multiple_of(kv * HD, LANE), HD)],
            gains[4:5, pl.ds(pl.multiple_of(kv * HD, LANE), HD)],
        ],
        axis=1,
    )
    wide = group_cols + 2 * HD
    heads = group_cols // HD
    for first in range(0, length, QUERY_ROWS):
        r = pl.ds(first, QUERY_ROWS)
        value = tokens[r, :].astype(F32)
        low = (value * rms_factor(value) * gain).astype(BF)
        normed_t[:, r] = low.T
        qkv = dot(low, weights[:, 0:wide]) + bias
        cos_rows, sin_rows = cosine[r, :], sine[r, :]
        for head in range(heads + 1):
            one = qkv[:, head * HD : (head + 1) * HD]
            turned = (one * cos_rows + pltpu.roll(one, HD // 2, 1) * sin_rows).astype(BF)
            if head < heads:
                queries[r, head * HD : (head + 1) * HD] = turned
            else:
                keys[r, :] = turned
        values[r, :] = qkv[:, group_cols + HD :].astype(BF)
    scaling = HD ** (-0.5)
    for first in range(0, length, QUERY_ROWS):
        r = pl.ds(first, QUERY_ROWS)
        reach = first + QUERY_ROWS
        query_place = first + lax.broadcasted_iota(jnp.int32, (QUERY_ROWS, reach), 0)
        key_place = lax.broadcasted_iota(jnp.int32, (QUERY_ROWS, reach), 1)
        allowed = (key_place <= query_place) & (key_place >= starts[r, :])
        for head in range(heads):
            cols = slice(head * HD, (head + 1) * HD)
            scores = dot_t(queries[r, cols], keys[0:reach, :]) * scaling
            scores = jnp.where(allowed, scores, masked_value)
            shifted = jnp.exp(scores - jnp.max(scores, axis=-1, keepdims=True))
            total = jnp.sum(shifted, axis=-1, keepdims=True)
            outcome = dot(shifted.astype(BF), values[0:reach, :])
            attended[r, cols] = (outcome / total).astype(BF)
        term = dot_t(attended[r, :], weights[:, wide:]).astype(BF)
        at = first // QUERY_ROWS

        @pl.when(c == at % 2)
        def _():
            keep[at // 2] = term

        @pl.when(c != at % 2)
        def _():
            send[at // 2] = term


def attention_in(places, own, mine, theirs, tokens, cosine, sine, starts, group_cols):
    planes = len(mine)
    rows = mine[0].shape[0] - 16
    length = cosine.shape[0]
    shapes = [
        jax.ShapeDtypeStruct((D, length), BF),
        jax.ShapeDtypeStruct((length, group_cols), BF),
        jax.ShapeDtypeStruct((length, HD), BF),
        jax.ShapeDtypeStruct((length, HD), BF),
        jax.ShapeDtypeStruct((length, group_cols), BF),
        jax.ShapeDtypeStruct((2, QUERY_ROWS, D), BF),
        jax.ShapeDtypeStruct((2, QUERY_ROWS, D), BF),
        jax.ShapeDtypeStruct((D, mine[0].shape[1]), BF),
        jax.ShapeDtypeStruct((8, D), F32),
        jax.ShapeDtypeStruct((length, D), BF),
    ]
    return pl.pallas_call(
        functools.partial(attention_in_body, planes, rows),
        out_shape=shapes,
        in_specs=[in_smem, in_smem] + [anywhere] * (2 * planes + 3) + [in_vmem] * 3,
        out_specs=[in_vmem] * len(shapes),
        scratch_shapes=[
            pltpu.VMEM((2 * planes * 16, mine[0].shape[1]), BF),
            pltpu.SemaphoreType.DMA((2, 2 * planes)),
            pltpu.SemaphoreType.DMA((4,)),
        ],
        compiler_params=kernel_params(),
        cost_estimate=KERNEL_COST,
        name="attention_in",
    )(places, own, *mine, *theirs, *tokens, cosine, sine, starts)


def attention_out_body(
    own,
    near,
    far,
    other,
    weights,
    queries,
    keys,
    values,
    cosine,
    sine,
    starts,
    grad_q,
    grad_kv,
    grad,
    grad_k,
    grad_v,
    sems,
):
    copies = sequence_copies(own[0], (near, far, other), grad, sems)
    for copy in copies:
        copy.start()
    for copy in copies:
        copy.wait()
    length = grad.shape[0]
    group_cols = queries.shape[1]
    heads = group_cols // HD
    scaling = HD ** (-0.5)
    output = weights[:, group_cols + 2 * HD :]
    grad_k[...] = jnp.zeros_like(grad_k)
    grad_v[...] = jnp.zeros_like(grad_v)
    for first in range(0, length, QUERY_ROWS):
        r = pl.ds(first, QUERY_ROWS)
        reach = first + QUERY_ROWS
        grad_heads = dot(grad[r, :], output).astype(BF)
        query_place = first + lax.broadcasted_iota(jnp.int32, (QUERY_ROWS, reach), 0)
        key_place = lax.broadcasted_iota(jnp.int32, (QUERY_ROWS, reach), 1)
        allowed = (key_place <= query_place) & (key_place >= starts[r, :])
        cos_rows, sin_rows = cosine[r, :], sine[r, :]
        for head in range(heads):
            cols = slice(head * HD, (head + 1) * HD)
            one_query = queries[r, cols]
            one_grad = grad_heads[:, cols]
            scores = dot_t(one_query, keys[0:reach, :]) * scaling
            scores = jnp.where(allowed, scores, masked_value)
            shifted = jnp.exp(scores - jnp.max(scores, axis=-1, keepdims=True))
            probability = shifted * (1.0 / jnp.sum(shifted, axis=-1, keepdims=True))
            grad_prob = dot_t(one_grad, values[0:reach, :])
            weighted = probability * grad_prob
            inner = jnp.sum(weighted, axis=-1, keepdims=True)
            grad_low = (weighted - probability * inner).astype(BF)
            turned = (dot(grad_low, keys[0:reach, :]) * scaling).astype(BF).astype(F32)
            grad_q[r, cols] = (
                turned * cos_rows - pltpu.roll(turned, HD // 2, 1) * sin_rows
            ).astype(BF)
            grad_k[0:reach, :] += t_dot(grad_low, one_query)
            grad_v[0:reach, :] += t_dot(probability.astype(BF), one_grad)
    grad_kv[0] = (grad_k[...] * scaling).astype(BF)
    grad_kv[1] = grad_v[...].astype(BF)


def attention_out(own, grad, weights, queries, keys, values, cosine, sine, starts):
    length, group_cols = queries.shape
    return pl.pallas_call(
        attention_out_body,
        out_shape=[
            jax.ShapeDtypeStruct((length, group_cols), BF),
            jax.ShapeDtypeStruct((2, length, HD), BF),
            jax.ShapeDtypeStruct((length, D), BF),
        ],
        in_specs=[in_smem] + [anywhere] * 3 + [in_vmem] * 7,
        out_specs=[in_vmem] * 3,
        scratch_shapes=[pltpu.VMEM((length, HD), F32)] * 2 + [pltpu.SemaphoreType.DMA((4,))],
        compiler_params=kernel_params(),
        cost_estimate=KERNEL_COST,
        name="attention_out",
    )(own, *grad, weights, queries, keys, values, cosine, sine, starts)


def projection_out_body(
    own_rows,
    kv_rows,
    own,
    grad_q,
    ours,
    theirs,
    weights,
    normed_t,
    cosine,
    sine,
    tokens,
    gain_mlp,
    d_qkv,
    keep,
    send,
    joined,
    sums,
):
    length, group_cols = grad_q.shape
    wide = group_cols + HD
    s = own[0]
    x, c = s // 2, lax.rem(s, 2)
    key_grad = ours[0].astype(F32) + theirs[0].astype(F32)
    key_grad = key_grad * cosine[...] - pltpu.roll(key_grad, HD // 2, 1) * sine[...]
    value_grad = ours[1].astype(F32) + theirs[1].astype(F32)
    joined[:, 0:group_cols] = grad_q[...]
    joined[:, group_cols:] = jnp.where(c == 0, key_grad, value_grad).astype(BF)
    one = jnp.where(
        c == 0,
        weights[:, group_cols : group_cols + HD],
        weights[:, group_cols + HD : group_cols + 2 * HD],
    )
    sums[...] = jnp.zeros_like(sums)
    gain_sum = jnp.zeros((1, D), F32)
    for first in range(0, length, QUERY_ROWS):
        r = pl.ds(first, QUERY_ROWS)
        term = dot_t(joined[r, 0:group_cols], weights[:, 0:group_cols]) + dot_t(
            joined[r, group_cols:], one
        )
        value = tokens[r, :].astype(F32)
        gain_sum += jnp.sum(term * (value * rms_factor(value)), axis=0, keepdims=True)
        low = term.astype(BF)
        at = first // QUERY_ROWS

        @pl.when(c == at % 2)
        def _():
            keep[at // 2] = low

        @pl.when(c != at % 2)
        def _():
            send[at // 2] = low

    bias = jnp.sum(joined[...].astype(F32), axis=0, keepdims=True)
    lane = lax.broadcasted_iota(jnp.int32, (HD, D // 2), 1)
    feature = lax.broadcasted_iota(jnp.int32, (HD, D // 2), 0)
    core, inner = lax.div(lane, D // 4), lax.rem(lane, D // 4)
    owner, row = lax.div(inner, own_rows), lax.rem(inner, own_rows)
    spot = core * (HD // 2) + owner * kv_rows + row
    chosen = jnp.where((spot == feature) & (row < kv_rows), 1.0, 0.0).astype(BF)
    spread = dot(bias[:, group_cols:].astype(BF), chosen)
    sums[0:1, :] = gain_sum
    sums[1:2, :] = gain_mlp[...]
    sums[2:3, pl.ds(pl.multiple_of(s * group_cols, LANE), group_cols)] = bias[:, 0:group_cols]
    sums[3:4, pl.ds(pl.multiple_of(x * (D // 2), LANE), D // 2)] = spread
    d_qkv[:, 0:wide] = dot(normed_t[...], joined[...]).astype(BF)
    d_qkv[:, wide:] = sums[...].T.astype(BF)


def projection_out(
    own_rows, kv_rows, own, grad_q, ours, theirs, weights, normed_t, cosine, sine, tokens, gain_mlp
):
    length, group_cols = grad_q.shape
    wide = group_cols + HD
    return pl.pallas_call(
        functools.partial(projection_out_body, own_rows, kv_rows),
        out_shape=[
            jax.ShapeDtypeStruct((D, wide + LANE), BF),
            jax.ShapeDtypeStruct((2, QUERY_ROWS, D), BF),
            jax.ShapeDtypeStruct((2, QUERY_ROWS, D), BF),
        ],
        in_specs=[in_smem] + [in_vmem] * 9,
        out_specs=[in_vmem] * 3,
        scratch_shapes=[pltpu.VMEM((length, wide), BF), pltpu.VMEM((LANE, D), F32)],
        compiler_params=kernel_params(),
        cost_estimate=KERNEL_COST,
        name="projection_out",
    )(own, grad_q, ours, theirs, weights, normed_t, cosine, sine, tokens, gain_mlp)


def plane_copies(sources, target, sems, first):
    copies = []
    rows = QUERY_ROWS
    for source, at, place, cols in sources:
        ref = source if at is None else source.at[at]
        copies.append(
            pltpu.make_async_copy(
                ref, target.at[pl.ds(place * rows, rows), cols], sems.at[first + len(copies)]
            )
        )
    return copies


def feed_forward_body(planes, rows, first, last, *refs):
    places, own = refs[0], refs[1]
    mine = refs[2 : 2 + planes]
    theirs = refs[2 + planes : 2 + 2 * planes]
    rest = list(refs[2 + 2 * planes :])
    n1, n2, na1, nb1, na2, nb2, c_own, c_x, c_y = [rest.pop(0) for _ in range(9)]
    turned_in = [] if first else [rest.pop(0) for _ in range(2)]
    totals_in = [] if first else [rest.pop(0) for _ in range(2)]
    keep, send = [rest.pop(0) for _ in range(2)]
    turned_out = [rest.pop(0) for _ in range(2)] if first else []
    totals_out = [rest.pop(0) for _ in range(8 if last else 2)]
    weights, grad_gate, grad_up, activated, grad_total, branch_total = [
        rest.pop(0) for _ in range(6)
    ]
    normed, cotangent, normed_t, cotangent_t, weight_sems, sems = [rest.pop(0) for _ in range(6)]
    low = rest
    step, steps = pl.program_id(0), pl.num_programs(0)
    tokens = normed.shape[0]
    half = D // 2
    left, right, both = pl.ds(0, half), pl.ds(half, half), pl.ds(0, D)
    c = own[0]
    normed_loads = plane_copies(
        (
            (n1, None, 0, left),
            (na2, 0, 1, left),
            (na1, None, 2, left),
            (na2, 1, 3, left),
            (n2, None, 0, right),
            (nb1, None, 1, right),
            (nb2, 0, 2, right),
            (nb2, 1, 3, right),
        ),
        normed,
        sems,
        8,
    )
    cot_loads = plane_copies(
        (
            (c_own, None, 0, both),
            (c_y, 0, 1, both),
            (c_x, None, 2, both),
            (c_y, 1, 3, both),
        ),
        cotangent,
        sems,
        16,
    )
    turned_loads = [
        pltpu.make_async_copy(source, target, sems.at[20 + i])
        for i, (source, target) in enumerate(zip(turned_in, (normed_t, cotangent_t)))
    ]
    turned_ends = [
        pltpu.make_async_copy(source, target, sems.at[20 + i])
        for i, (source, target) in enumerate(zip((normed_t, cotangent_t), turned_out))
    ]
    fills = [
        pltpu.make_async_copy(source, target, sems.at[i])
        for i, (source, target) in enumerate(zip(totals_in, (grad_total, branch_total)))
    ]
    if last:
        ends = []
        for i, source in enumerate(low):
            keep_a, send_a, keep_b, send_b = totals_out[4 * i : 4 * i + 4]
            for target, place, cols in (
                (keep_a.at[0], 0, left),
                (keep_a.at[1], 2, left),
                (send_a.at[0], 1, left),
                (send_a.at[1], 3, left),
                (keep_b.at[0], 0, right),
                (keep_b.at[1], 1, right),
                (send_b.at[0], 2, right),
                (send_b.at[1], 3, right),
            ):
                ends.append(
                    pltpu.make_async_copy(
                        source.at[pl.ds(place * QUERY_ROWS, QUERY_ROWS), cols],
                        target,
                        sems.at[len(ends)],
                    )
                )
    else:
        ends = [
            pltpu.make_async_copy(source, target, sems.at[i])
            for i, (source, target) in enumerate(zip((grad_total, branch_total), totals_out))
        ]

    def weight_copies(at, slot):
        cols = pl.ds(pl.multiple_of(at * TILE, TILE), TILE)
        copies = []
        for k in range(planes):
            base = places[k] * (2 * rows)
            for side, source in enumerate((mine[k], theirs[k])):
                start = base + (c if side == 0 else 1 - c) * rows
                copies.append(
                    pltpu.make_async_copy(
                        source.at[:, :, cols],
                        weights.at[slot, :, pl.ds(pl.multiple_of(start, 16), rows), :],
                        weight_sems.at[slot, 2 * k + side],
                    )
                )
        return copies

    slot = lax.rem(step, 2)

    @pl.when(step == 0)
    def _():
        for load in normed_loads:
            load.start()
        for copy in weight_copies(0, 0):
            copy.start()
        for load in cot_loads + turned_loads + fills:
            load.start()

    @pl.when(step + 1 < steps)
    def _():
        for copy in weight_copies(step + 1, 1 - slot):
            copy.start()

    if first:

        @pl.when(step == 0)
        def _():
            grad_total[...] = jnp.zeros_like(grad_total)
            branch_total[...] = jnp.zeros_like(branch_total)

    @pl.when(step == 0)
    def _():
        for load in normed_loads:
            load.wait()

    for copy in weight_copies(step, slot):
        copy.wait()

    @pl.when(step == 0)
    def _():
        for load in cot_loads:
            load.wait()

    block = min(256, tokens)
    for start in range(0, tokens, block):
        r = pl.ds(start, block)
        some = normed[r, :]
        gate = dot(some, weights[slot, 0])
        up = dot(some, weights[slot, 1])
        grad_act = dot(cotangent[r, :], weights[slot, 2])
        sigma = jax.nn.sigmoid(gate)
        silu = gate * sigma
        activated[r, :] = (silu * up).astype(BF)
        grad_gate[r, :] = (grad_act * up * (sigma + silu * (1.0 - sigma))).astype(BF)
        grad_up[r, :] = (grad_act * silu).astype(BF)

    @pl.when(step == 0)
    def _():
        for fill in fills:
            fill.wait()

    for start in range(0, tokens, block):
        r = pl.ds(start, block)
        grad_total[r, :] += dot_t(grad_gate[r, :], weights[slot, 0]) + dot_t(
            grad_up[r, :], weights[slot, 1]
        )
        branch_total[r, :] += dot_t(activated[r, :], weights[slot, 2])

    @pl.when(step == steps - 1)
    def _():
        if last:
            low[0][...] = grad_total[...].astype(BF)
            low[1][...] = branch_total[...].astype(BF)
        for end in ends:
            end.start()

    if first:

        @pl.when(step == 0)
        def _():
            for source, target in ((normed, normed_t), (cotangent, cotangent_t)):
                for start in range(0, D, TILE):
                    cols = pl.ds(start, TILE)
                    target[cols, :] = source[:, cols].T
            for end in turned_ends:
                end.start()

    else:

        @pl.when(step == 0)
        def _():
            for load in turned_loads:
                load.wait()

    owner_rows = D // 4
    for part in range(2):
        for target, core in ((send, 1 - c), (keep, c)):
            r = pl.ds(pl.multiple_of((2 * part + core) * owner_rows, LANE), owner_rows)
            target[0, part] = dot(normed_t[r, :], grad_gate[...]).astype(BF)
            target[1, part] = dot(normed_t[r, :], grad_up[...]).astype(BF)
            target[2, part] = dot(cotangent_t[r, :], activated[...]).astype(BF)

    @pl.when(step == steps - 1)
    def _():
        for end in ends + turned_ends:
            end.wait()


def feed_forward(places, own, mine, theirs, normed, cotangent, turned, totals, last):
    planes = len(mine)
    rows, cols = mine[0].shape[1:]
    tokens = 4 * QUERY_ROWS
    first = totals is None
    totals = () if first else totals
    owner_rows = D // 4
    piece = jax.ShapeDtypeStruct((3, 2, owner_rows, cols), BF)
    piece_spec = pl.BlockSpec((3, 2, owner_rows, TILE), lambda i, *_: (0, 0, 0, i))
    shapes = [piece, piece]
    if first:
        shapes += [jax.ShapeDtypeStruct((D, tokens), BF)] * 2
    if last:
        shapes += [jax.ShapeDtypeStruct((2, QUERY_ROWS, D // 2), BF)] * 8
    else:
        shapes += [jax.ShapeDtypeStruct((tokens, D), F32)] * 2
    scratch = [pltpu.VMEM((2, 3, D, TILE), BF)]
    scratch += [pltpu.VMEM((tokens, TILE), BF)] * 3
    scratch += [pltpu.VMEM((tokens, D), F32)] * 2
    scratch += [pltpu.VMEM((tokens, D), BF)] * 2
    scratch += [pltpu.VMEM((D, tokens), BF)] * 2
    scratch += [pltpu.SemaphoreType.DMA((2, 2 * planes)), pltpu.SemaphoreType.DMA((22,))]
    if last:
        scratch += [pltpu.VMEM((tokens, D), BF)] * 2
    inputs = [*mine, *theirs, *normed, *cotangent, *turned, *totals]
    return pl.pallas_call(
        functools.partial(feed_forward_body, planes, rows, first, last),
        grid=(cols // TILE,),
        out_shape=shapes,
        in_specs=[in_smem, in_smem] + [anywhere] * len(inputs),
        out_specs=[piece_spec, piece_spec] + [anywhere] * (len(shapes) - 2),
        scratch_shapes=scratch,
        compiler_params=kernel_params(),
        cost_estimate=KERNEL_COST,
        name="feed_forward",
    )(places, own, *inputs)


def build(seq_count, fsdp_count):
    planes = fsdp_count // 2
    order = list(range(0, 1)) + list(range(1, planes, 2)) + list(range(2, planes, 2))[::-1]
    place = [order.index(plane) for plane in range(planes)]
    after = {order[i]: order[(i + 1) % planes] for i in range(planes)}
    ring_perm = [(2 * z + y, 2 * after[z] + y) for z in range(planes) for y in range(2)]
    y_perm = [(i, i ^ 1) for i in range(fsdp_count)]
    x_perm = [(i, i ^ 2) for i in range(seq_count)]
    c_perm = [(i, i ^ 1) for i in range(seq_count)]
    rows_perm = [
        (i * fsdp_count + j, i * fsdp_count + (j ^ 1))
        for i in range(seq_count)
        for j in range(fsdp_count)
        if i % 2 == j % 2
    ]

    def swap_x(value):
        return lax.ppermute(value, "seq", x_perm)

    def swap_c(value):
        return lax.ppermute(value, "seq", c_perm)

    def swap_y(value):
        return lax.ppermute(value, "fsdp", y_perm)

    def send_rows(value):
        return lax.ppermute(value, ("seq", "fsdp"), rows_perm)

    def ring(value):
        return lax.ppermute(value, "fsdp", ring_perm)

    def ring_back(value):
        return lax.ppermute(value, "fsdp", [(j, i) for i, j in ring_perm])

    along = (planes - 1) // 2
    against = planes - 1 - along
    steps_behind = list(range(along + 1)) + [-i for i in range(1, against + 1)]

    def local(
        tokens,
        positions,
        w_query,
        w_key,
        w_value,
        w_output,
        gate_up,
        w_down,
        bias_query,
        bias_key,
        bias_value,
        gain_attn,
        gain_mlp,
        cotangent,
    ):
        s = lax.axis_index("seq")
        f = lax.axis_index("fsdp")
        x, c = s // 2, s % 2
        z, y = f // 2, f % 2
        ring_order = jnp.array(order, jnp.int32)
        ring_place = jnp.array(place, jnp.int32)
        behind = ring_order[(ring_place[z] - jnp.array(steps_behind)) % planes].astype(jnp.int32)

        def ring_gather(piece):
            ahead, back = [piece], [piece]
            for _ in range(along):
                ahead.append(ring(ahead[-1]))
            for _ in range(against):
                back.append(ring_back(back[-1]))
            return ahead + back[1:]
        core = jnp.stack([c]).astype(jnp.int32)
        own_place = jnp.stack([s, y]).astype(jnp.int32)

        tok_rows = tokens.shape[1]
        length = tok_rows * seq_count
        per_group = HEADS // seq_count
        group_cols = per_group * HD
        w_rows = w_query.shape[0]
        own_rows = D // (seq_count * fsdp_count)
        half = D // 2

        def gather_sequence(own, then=()):
            far = swap_x(own)
            return [own, far, swap_c(tie(jnp.stack([own, far]), *then))]

        def scatter_sequence(keep, send, then=()):
            halves = keep.astype(F32) + swap_c(send).astype(F32)
            back = swap_x(tie(pick(halves, 1 - x).astype(BF), *then))
            return pick(halves, x) + back.astype(F32)

        def gather_plane(own, then=()):
            first, second = own[:, :half], own[:, half:]
            a1 = swap_x(first)
            b1 = swap_y(second)
            a2 = swap_y(tie(jnp.stack([first, a1]), *then))
            b2 = swap_x(tie(jnp.stack([second, b1]), *then))
            return [first, second, a1, b1, a2, b2]

        def scatter_plane(keep_a, send_a, keep_b, send_b, then=()):
            a1 = keep_a.astype(F32) + swap_y(send_a).astype(F32)
            b1 = keep_b.astype(F32) + swap_x(send_b).astype(F32)
            a1, b1 = tie((a1, b1), *then)
            a2 = a1[0] + swap_x(a1[1].astype(BF)).astype(F32)
            b2 = b1[0] + swap_y(b1[1].astype(BF)).astype(F32)
            return jnp.concatenate([a2, b2], axis=1)

        wide = group_cols + 2 * HD
        small_rows = jnp.stack(
            [
                jnp.pad(vector, (0, wide + group_cols - vector.shape[0]))
                for vector in (gain_attn, gain_mlp, bias_query, bias_key, bias_value)
            ]
        )
        small_rows = jnp.pad(small_rows, ((0, 11), (0, 0)))
        attn_own = jnp.concatenate(
            [
                lax.dynamic_slice_in_dim(w_query, s * group_cols, group_cols, 1),
                lax.dynamic_slice_in_dim(w_key, x * HD, HD, 1),
                lax.dynamic_slice_in_dim(w_value, x * HD, HD, 1),
                lax.dynamic_slice_in_dim(w_output, s * group_cols, group_cols, 1),
            ],
            axis=1,
        )
        attn_payload = jnp.concatenate([attn_own, small_rows], axis=0)
        chunk_places = []
        for low, high in CHUNKS:
            table = []
            for start, (first, end) in zip(CHIP_STARTS, CHIP_VALID):
                edge = 1 if low == 0 and first > 0 else 0
                edge = 2 if high > end * LANE else edge
                table.append((start * LANE + low, edge))
            table = jnp.array(table, jnp.int32)
            chunk_places.append((table[2 * x + y], table[2 * x + 1 - y]))

        def cut(chunk, whose, then):
            low, high = CHUNKS[chunk]
            return cut_columns(tie(chunk_places[chunk][whose], then), gate_up, w_down, high - low)

        sent = cut(0, 1, ())
        attn_payload = tie(attn_payload, sent)
        attn_pieces = ring_gather(attn_payload)
        attn_theirs = [swap_y(piece) for piece in attn_pieces]
        token_pieces = gather_sequence(tokens[0])

        came, kept = send_rows(sent), cut(0, 0, attn_payload)
        kept, came = tie((kept, came), attn_pieces[1:], attn_theirs[0])
        payloads = [jnp.where(c == y, kept, came)]
        for chunk in range(1, len(CHUNKS)):
            sent = cut(chunk, 1, payloads[-1])
            kept, came = cut(chunk, 0, sent), send_rows(sent)
            payloads.append(jnp.where(c == y, kept, came))
        chunk_pieces = [ring_gather(payload) for payload in payloads]
        chunk_theirs = []
        for pieces in chunk_pieces:
            theirs = []
            for piece in pieces:
                theirs.append(swap_c(tie(piece, theirs[-1:])))
            chunk_theirs.append(theirs)

        cot_own = tie(cotangent[0], token_pieces[1])
        cot_far = swap_x(cot_own)
        cot_pair = tie(jnp.stack([cot_own, cot_far]), payloads[-1])
        cot_pieces = [cotangent[0], cot_far, swap_y(cot_pair)]

        seq_positions = positions[0]
        cosine, sine = rope_tables(seq_positions)
        first_keys = (jnp.arange(length, dtype=jnp.int32) - seq_positions)[:, None]
        (
            normed_attn_t,
            queries,
            keys,
            values,
            attended,
            out_keep,
            out_send,
            attn_weights,
            gains,
            tokens_all,
        ) = attention_in(
            behind,
            own_place,
            attn_pieces,
            attn_theirs,
            tie(token_pieces, sent, cot_far),
            cosine,
            sine,
            first_keys,
            group_cols,
        )
        inputs = tokens[0].astype(F32)
        out_keep, out_send, queries, keys, values, attended, gains = tie(
            (out_keep, out_send, queries, keys, values, attended, gains),
            chunk_pieces[0][along + 1],
        )
        gain_a, gain_m = gains[0], gains[1]
        hidden = inputs + scatter_sequence(out_keep, out_send)
        factor_mlp = rms_factor(hidden)
        normed_own = (hidden * factor_mlp * gain_m).astype(BF)
        normed = gather_plane(normed_own)

        def plane_ahead(steps):
            return ring_order[(ring_place[z] + steps) % planes]

        class RingScatter:
            def __init__(self, block):
                self.first, self.second, self.arrived, self.last = [], [], [], []
                self.own = block(z)
                for steps, sign, move in ((along, 1, ring), (against, -1, ring_back)):
                    if steps:
                        running = block(plane_ahead(sign * steps)).astype(BF)
                        self.first.append(running)
                        for left in range(steps - 1, 0, -1):
                            came = move(running)
                            self.arrived.append(came)
                            running = block(plane_ahead(sign * left)) + came.astype(F32)
                            running = running.astype(BF)
                            self.second.append(running)
                        came = move(running)
                        self.arrived.append(came)
                        self.last.append(came)

            def total(self, then=()):
                total = self.own
                for came in tie(self.last, then):
                    total = total + came.astype(F32)
                return total.astype(BF)

        def exchange(total, at, swap, axis):
            return jnp.stack([pick(total, at, axis), swap(pick(total, 1 - at, axis))], axis)

        def chunk_scatter(keep, send):
            away = swap_c(send)
            cols = keep.shape[-1]
            keep = keep.reshape(3, 2, planes, 2 * own_rows, cols)
            away = away.reshape(3, 2, planes, 2 * own_rows, cols)

            def block(plane):
                return pick(keep, plane, 2).astype(F32) + pick(away, plane, 2).astype(F32)

            return RingScatter(block)

        before = [(), None]
        beside = [chunk_pieces[1][1 : along + 2], None]
        turned, totals = (), None
        scatters = []
        for chunk in range(len(CHUNKS)):
            keep, send, *results = feed_forward(
                behind,
                core,
                chunk_pieces[chunk],
                chunk_theirs[chunk],
                tie(normed, before[chunk]),
                cot_pieces,
                turned,
                totals,
                chunk == len(CHUNKS) - 1,
            )
            keep, send, results = tie((keep, send, results), beside[chunk])
            if chunk == 0:
                turned, results = results[:2], results[2:]
            totals = results
            scatters.append(chunk_scatter(keep, send))
            before[1] = scatters[0].first
            beside[1] = scatters[0].arrived[along]
        grad_out = cotangent[0].astype(F32)
        grad_hidden_norm, grad_gain_mlp = rms_backward(
            hidden, factor_mlp, gain_m, scatter_plane(*totals[:4], scatters[0].second)
        )
        grad_hidden = grad_out + grad_hidden_norm
        grad_pieces = gather_sequence(
            grad_hidden.astype(BF), (scatters[1].first, scatters[0].arrived[0])
        )
        result = (hidden + scatter_plane(*tie(totals[4:], grad_pieces[1]))).astype(BF)
        grad_q, grad_kv, grad_hidden_low = attention_out(
            own_place,
            grad_pieces,
            attn_weights,
            queries,
            keys,
            values,
            cosine,
            sine,
            first_keys,
        )
        grad_q, grad_kv, grad_hidden_low = tie(
            (grad_q, grad_kv, grad_hidden_low), scatters[0].arrived[-1]
        )
        kv_rows = KV * HD // (seq_count * fsdp_count)
        d_qkv, in_keep, in_send = projection_out(
            own_rows,
            kv_rows,
            own_place,
            grad_q,
            grad_kv,
            swap_c(grad_kv),
            attn_weights,
            normed_attn_t,
            cosine,
            sine,
            tokens_all,
            grad_gain_mlp[None],
        )
        d_qkv, in_keep, in_send = tie((d_qkv, in_keep, in_send), scatters[1].arrived[along])
        in_halves = in_keep.astype(F32) + swap_c(in_send).astype(F32)
        in_leaves = tie(pick(in_halves, 1 - x).astype(BF), scatters[1].second)
        in_back = swap_x(in_leaves)
        grad_input_norm, _ = rms_backward(
            inputs,
            rms_factor(inputs),
            gain_a,
            pick(in_halves, x) + in_back.astype(F32),
        )
        grad_input = grad_hidden + grad_input_norm

        gathered = []
        for scatter, then in zip(scatters, (grad_kv, in_leaves)):
            total = scatter.total(then).reshape(3, 2, 2, own_rows, -1)
            if not gathered:
                both = exchange(tie(exchange(total, x, swap_x, 1), in_leaves), y, swap_y, 2)
            else:
                both = exchange(exchange(total, y, swap_y, 2), x, swap_x, 1)
            both = jnp.where(x == 0, both, both[:, ::-1])
            both = jnp.where(y == 0, both, both[:, :, ::-1])
            gathered.append(both)
        strips = []
        for chip_index, (low, high) in enumerate(CHIP_VALID):
            whole = jnp.concatenate(
                [part[:, chip_index // 2, chip_index % 2] for part in gathered], axis=-1
            )
            strips.append(whole[..., low * LANE : high * LANE])
        d_mlp = jnp.concatenate(strips, axis=-1).astype(F32)
        d_gate_up = jnp.stack([d_mlp[0], d_mlp[1]], axis=1)
        d_w_down = d_mlp[2]

        d_output = t_dot(grad_hidden_low, attended).astype(BF)

        def to_owners(partial, middle=(), last=()):
            cols = partial.shape[1]
            rows = partial.reshape(2, 2, planes, 2, own_rows, cols)
            away = tie(swap_y(pick(rows, 1 - y, 3)), middle)
            rest = pick(rows, y, 3)

            def block(plane):
                return pick(rest, plane, 2).astype(F32) + pick(away, plane, 2).astype(F32)

            total = tie(RingScatter(block).total(), last)
            both = exchange(exchange(total, x, swap_x, 0), c, swap_c, 1)
            both = jnp.where(x == 0, both, both[::-1])
            both = jnp.where(c == 0, both, both[:, ::-1])
            return both.astype(F32)

        out_blocks = to_owners(d_output)
        d_w_output = jnp.concatenate([out_blocks[i // 2, i % 2] for i in range(4)], axis=1)
        qkv_out = to_owners(d_qkv, in_leaves, in_back)
        d_w_query = jnp.concatenate(
            [qkv_out[i // 2, i % 2, :, :group_cols] for i in range(4)], axis=1
        )
        last = qkv_out[:, :, :, group_cols : group_cols + HD]
        d_w_key = jnp.concatenate([last[0, 0], last[1, 0]], axis=1)
        d_w_value = jnp.concatenate([last[0, 1], last[1, 1]], axis=1)
        sums = qkv_out[:, :, :, group_cols + HD :]
        d_gain_attn = jnp.sum(sums[..., 0], axis=(0, 1))
        d_gain_mlp = jnp.sum(sums[..., 1], axis=(0, 1))
        d_bias_query = jnp.sum(sums[..., 2], axis=(0, 1))
        d_bias_key = jnp.sum(sums[:, 0, :kv_rows, 3], axis=0)
        d_bias_value = jnp.sum(sums[:, 1, :kv_rows, 3], axis=0)
        return (
            result[None],
            grad_input[None],
            d_w_query,
            d_w_key,
            d_w_value,
            d_w_output,
            d_gate_up,
            d_w_down,
            d_bias_query,
            d_bias_key,
            d_bias_value,
            d_gain_attn,
            d_gain_mlp,
        )

    return local


def solution(mesh):
    rows = P("fsdp", None)
    owners = P(("seq", "fsdp"))
    return jax.shard_map(
        build(mesh.shape["seq"], mesh.shape["fsdp"]),
        mesh=mesh,
        in_specs=(
            P("fsdp", "seq", None),
            rows,
            rows,
            rows,
            rows,
            rows,
            P("fsdp", None, None),
            rows,
            P("fsdp"),
            P("fsdp"),
            P("fsdp"),
            P("fsdp"),
            P("fsdp"),
            P("fsdp", "seq", None),
        ),
        out_specs=(
            P("fsdp", "seq", None),
            P("fsdp", "seq", None),
            P(("seq", "fsdp"), None),
            P(("seq", "fsdp"), None),
            P(("seq", "fsdp"), None),
            P(("seq", "fsdp"), None),
            P(("seq", "fsdp"), None, None),
            P(("seq", "fsdp"), None),
            owners,
            owners,
            owners,
            owners,
            owners,
        ),
        check_vma=False,
    )
```

```python
import functools

import jax
import jax.numpy as jnp
from jax import lax
from jax.experimental import pallas as pl
from jax.experimental.pallas import tpu as pltpu
from jax.sharding import PartitionSpec as P

D = 1536
HEADS = 12
KV = 2
HD = 128
FF = 8960
LANE = 128

epsilon = 1e-06
rope_base = 1000000.0
masked_value = -1e30
BF = jnp.bfloat16
F32 = jnp.float32
VMEM_BYTES = 60 * 1024 * 1024

CHIP_STARTS = (0, 18, 36, 52)
CHIP_VALID = ((0, 18), (0, 18), (0, 17), (1, 18))
TILE = 256
CHUNKS = ((0, 1280), (1280, 2304))
QUERY_ROWS = 256

anywhere = pl.BlockSpec(memory_space=pl.ANY)
in_vmem = pl.BlockSpec(memory_space=pltpu.VMEM)
in_smem = pl.BlockSpec(memory_space=pltpu.SMEM)


def rope_tables(positions):
    ladder = jnp.arange(HD // 2, dtype=F32)
    inverse = rope_base ** (-2.0 * ladder / HD)
    angles = positions.astype(F32)[:, None] * inverse[None, :]
    cosine, sine = jnp.cos(angles), jnp.sin(angles)
    return (
        jnp.concatenate([cosine, cosine], axis=-1),
        jnp.concatenate([-sine, sine], axis=-1),
    )


def rms_factor(value):
    return lax.rsqrt(jnp.mean(value * value, axis=-1, keepdims=True) + epsilon)


def rms_backward(value, factor, gain, grad):
    unit = value * factor
    weighted = grad * gain
    grad_gain = jnp.sum(grad * unit, axis=0)
    inner = jnp.mean(weighted * unit, axis=-1, keepdims=True)
    return (factor * (weighted - unit * inner), grad_gain)


def dot(left, right):
    return jnp.dot(left, right, preferred_element_type=F32)


def dot_t(left, right):
    return lax.dot_general(left, right, (((1,), (1,)), ((), ())), preferred_element_type=F32)


def t_dot(left, right):
    return lax.dot_general(left, right, (((0,), (0,)), ((), ())), preferred_element_type=F32)


def pick(array, index, axis=0):
    return lax.dynamic_index_in_dim(array, index, axis, keepdims=False)


def tie(value, *others):
    return lax.optimization_barrier((value, *others))[0] if jax.tree.leaves(others) else value


def kernel_params():
    return pltpu.CompilerParams(vmem_limit_bytes=VMEM_BYTES)


KERNEL_COST = pl.CostEstimate(flops=1_000_000, bytes_accessed=1_000_000, transcendentals=0)


def cut_body(place, gate_up, down, target, pairs, sems):
    cols = pl.ds(pl.multiple_of(place[0], LANE), target.shape[2])
    copies = [
        pltpu.make_async_copy(gate_up.at[:, :, cols], pairs, sems.at[0]),
        pltpu.make_async_copy(down.at[:, cols], target.at[2], sems.at[1]),
    ]
    for copy in copies:
        copy.start()
    copies[0].wait()
    target[0] = pairs[:, 0, :]
    target[1] = pairs[:, 1, :]
    copies[1].wait()
    empty = jnp.zeros((3, target.shape[1], LANE), BF)

    @pl.when(place[1] == 1)
    def _():
        target[:, :, 0:LANE] = empty

    @pl.when(place[1] == 2)
    def _():
        target[:, :, target.shape[2] - LANE :] = empty


def cut_columns(place, gate_up, down, cols):
    rows = down.shape[0]
    return pl.pallas_call(
        cut_body,
        out_shape=jax.ShapeDtypeStruct((3, rows, cols), BF),
        in_specs=[in_smem, anywhere, anywhere],
        out_specs=in_vmem,
        scratch_shapes=[pltpu.VMEM((rows, 2, cols), BF), pltpu.SemaphoreType.DMA((2,))],
        compiler_params=kernel_params(),
        cost_estimate=KERNEL_COST,
        name="cut_columns",
    )(place, gate_up, down)


def sequence_copies(s, sources, target, sems):
    near, far, other_near, other_far = sources
    rows = near.shape[0]
    x, c = s // 2, lax.rem(s, 2)
    copies = []
    for i, (source, owner) in enumerate(
        (
            (near, 2 * x + c),
            (far, 2 * (1 - x) + c),
            (other_near, 2 * x + 1 - c),
            (other_far, 2 * (1 - x) + 1 - c),
        )
    ):
        place = pl.multiple_of(owner * rows, LANE)
        copies.append(pltpu.make_async_copy(source, target.at[pl.ds(place, rows)], sems.at[i]))
    return copies


def split_store(s, block, value, targets):
    x, c = s // 2, lax.rem(s, 2)
    for i, target in enumerate(targets):
        far, away = i % 2, i // 2
        owner = 2 * (1 - x if far else x) + (1 - c if away else c)

        @pl.when(owner == block)
        def _():
            target[...] = value


def attention_in_body(planes, rows, *refs):
    places, own = refs[0], refs[1]
    mine = refs[2 : 2 + planes]
    theirs = refs[2 + planes : 2 + 2 * planes]
    sources = refs[2 + 2 * planes : 6 + 2 * planes]
    cosine, sine, starts = refs[6 + 2 * planes : 9 + 2 * planes]
    normed_t, queries, keys, values, attended_t = refs[9 + 2 * planes : 14 + 2 * planes]
    targets = refs[14 + 2 * planes : 18 + 2 * planes]
    weights, gains, tokens, small, sems, token_sems = refs[18 + 2 * planes :]
    length = tokens.shape[0]
    group_cols = queries.shape[1]
    blocks = 2 * planes
    s, y = own[0], own[1]
    copies = sequence_copies(s, sources, tokens, token_sems)
    for k in range(planes):
        for side, source in enumerate((mine[k], theirs[k])):
            block = places[k] * 2 + (y if side == 0 else 1 - y)
            first = pl.multiple_of(block * rows, 16)
            copies.append(
                pltpu.make_async_copy(
                    source.at[pl.ds(0, rows)], weights.at[pl.ds(first, rows)], sems.at[0, 2 * k + side]
                )
            )
            copies.append(
                pltpu.make_async_copy(
                    source.at[pl.ds(rows, 16)],
                    small.at[pl.ds(pl.multiple_of(block * 16, 16), 16)],
                    sems.at[1, 2 * k + side],
                )
            )
    for copy in copies:
        copy.start()
    for copy in copies:
        copy.wait()
    kv_own = KV * HD // blocks
    vectors = []
    for row, width in enumerate((rows, rows, rows, kv_own, kv_own)):
        vectors.append(
            jnp.concatenate(
                [small[pl.ds(16 * b + row, 1), 0:width].astype(F32) for b in range(blocks)], axis=1
            )
        )
    gains[0:1, :] = vectors[0]
    gains[1:2, :] = vectors[1]
    gains[2:3, :] = vectors[2]
    gains[3:4, 0 : KV * HD] = vectors[3]
    gains[4:5, 0 : KV * HD] = vectors[4]
    gain = gains[0:1, :]
    kv = s // 2
    bias = jnp.concatenate(
        [
            gains[2:3, pl.ds(pl.multiple_of(s * group_cols, LANE), group_cols)],
            gains[3:4, pl.ds(pl.multiple_of(kv * HD, LANE), HD)],
            gains[4:5, pl.ds(pl.multiple_of(kv * HD, LANE), HD)],
        ],
        axis=1,
    )
    wide = group_cols + 2 * HD
    heads = group_cols // HD
    for first in range(0, length, QUERY_ROWS):
        r = pl.ds(first, QUERY_ROWS)
        value = tokens[r, :].astype(F32)
        low = (value * rms_factor(value) * gain).astype(BF)
        normed_t[:, r] = low.T
        qkv = dot(low, weights[:, 0:wide]) + bias
        cos_rows, sin_rows = cosine[r, :], sine[r, :]
        for head in range(heads + 1):
            one = qkv[:, head * HD : (head + 1) * HD]
            turned = (one * cos_rows + pltpu.roll(one, HD // 2, 1) * sin_rows).astype(BF)
            if head < heads:
                queries[r, head * HD : (head + 1) * HD] = turned
            else:
                keys[r, :] = turned
        values[r, :] = qkv[:, group_cols + HD :].astype(BF)
    scaling = HD ** (-0.5)
    for first in range(0, length, QUERY_ROWS):
        r = pl.ds(first, QUERY_ROWS)
        reach = first + QUERY_ROWS
        query_place = first + lax.broadcasted_iota(jnp.int32, (QUERY_ROWS, reach), 0)
        key_place = lax.broadcasted_iota(jnp.int32, (QUERY_ROWS, reach), 1)
        allowed = (key_place <= query_place) & (key_place >= starts[r, :])
        outcomes = []
        for head in range(heads):
            cols = slice(head * HD, (head + 1) * HD)
            scores = dot_t(queries[r, cols], keys[0:reach, :]) * scaling
            scores = jnp.where(allowed, scores, masked_value)
            shifted = jnp.exp(scores - jnp.max(scores, axis=-1, keepdims=True))
            total = jnp.sum(shifted, axis=-1, keepdims=True)
            outcome = dot(shifted.astype(BF), values[0:reach, :])
            outcomes.append((outcome / total).astype(BF))
        attended = jnp.concatenate(outcomes, axis=1)
        attended_t[:, r] = attended.T
        term = dot_t(attended, weights[:, wide:]).astype(BF)
        split_store(s, first // QUERY_ROWS, term, targets)


def attention_in(places, own, mine, theirs, tokens, cosine, sine, starts, group_cols):
    planes = len(mine)
    rows = mine[0].shape[0] - 16
    length = cosine.shape[0]
    shapes = [
        jax.ShapeDtypeStruct((D, length), BF),
        jax.ShapeDtypeStruct((length, group_cols), BF),
        jax.ShapeDtypeStruct((length, HD), BF),
        jax.ShapeDtypeStruct((length, HD), BF),
        jax.ShapeDtypeStruct((group_cols, length), BF),
        *[jax.ShapeDtypeStruct((QUERY_ROWS, D), BF)] * 4,
        jax.ShapeDtypeStruct((D, mine[0].shape[1]), BF),
        jax.ShapeDtypeStruct((8, D), F32),
        jax.ShapeDtypeStruct((length, D), BF),
    ]
    return pl.pallas_call(
        functools.partial(attention_in_body, planes, rows),
        out_shape=shapes,
        in_specs=[in_smem, in_smem] + [anywhere] * (2 * planes + 4) + [in_vmem] * 3,
        out_specs=[in_vmem] * len(shapes),
        scratch_shapes=[
            pltpu.VMEM((2 * planes * 16, mine[0].shape[1]), BF),
            pltpu.SemaphoreType.DMA((2, 2 * planes)),
            pltpu.SemaphoreType.DMA((4,)),
        ],
        compiler_params=kernel_params(),
        cost_estimate=KERNEL_COST,
        name="attention_in",
    )(places, own, *mine, *theirs, *tokens, cosine, sine, starts)


def attention_out_body(
    own,
    near,
    far,
    other_near,
    other_far,
    weights,
    queries,
    keys,
    values,
    cosine,
    sine,
    starts,
    normed_t,
    attended_t,
    grad_q,
    grad_kv,
    d_early,
    grad,
    grad_k,
    grad_v,
    sems,
):
    copies = sequence_copies(own[0], (near, far, other_near, other_far), grad, sems)
    for copy in copies:
        copy.start()
    for copy in copies:
        copy.wait()
    length = grad.shape[0]
    group_cols = queries.shape[1]
    heads = group_cols // HD
    scaling = HD ** (-0.5)
    output = weights[:, group_cols + 2 * HD :]
    grad_k[...] = jnp.zeros_like(grad_k)
    grad_v[...] = jnp.zeros_like(grad_v)
    for first in range(0, length, QUERY_ROWS):
        r = pl.ds(first, QUERY_ROWS)
        reach = first + QUERY_ROWS
        grad_heads = dot(grad[r, :], output).astype(BF)
        query_place = first + lax.broadcasted_iota(jnp.int32, (QUERY_ROWS, reach), 0)
        key_place = lax.broadcasted_iota(jnp.int32, (QUERY_ROWS, reach), 1)
        allowed = (key_place <= query_place) & (key_place >= starts[r, :])
        cos_rows, sin_rows = cosine[r, :], sine[r, :]
        for head in range(heads):
            cols = slice(head * HD, (head + 1) * HD)
            one_query = queries[r, cols]
            one_grad = grad_heads[:, cols]
            scores = dot_t(one_query, keys[0:reach, :]) * scaling
            scores = jnp.where(allowed, scores, masked_value)
            shifted = jnp.exp(scores - jnp.max(scores, axis=-1, keepdims=True))
            probability = shifted * (1.0 / jnp.sum(shifted, axis=-1, keepdims=True))
            grad_prob = dot_t(one_grad, values[0:reach, :])
            weighted = probability * grad_prob
            inner = jnp.sum(weighted, axis=-1, keepdims=True)
            grad_low = (weighted - probability * inner).astype(BF)
            turned = (dot(grad_low, keys[0:reach, :]) * scaling).astype(BF).astype(F32)
            grad_q[r, cols] = (
                turned * cos_rows - pltpu.roll(turned, HD // 2, 1) * sin_rows
            ).astype(BF)
            grad_k[0:reach, :] += t_dot(grad_low, one_query)
            grad_v[0:reach, :] += t_dot(probability.astype(BF), one_grad)
    grad_kv[0] = (grad_k[...] * scaling).astype(BF)
    grad_kv[1] = grad_v[...].astype(BF)
    d_early[:, 0:group_cols] = dot(attended_t[...], grad[...]).astype(BF).T
    d_early[:, group_cols:] = dot(normed_t[...], grad_q[...]).astype(BF)


def attention_out(
    own, grad, weights, queries, keys, values, cosine, sine, starts, normed_t, attended_t
):
    length, group_cols = queries.shape
    return pl.pallas_call(
        attention_out_body,
        out_shape=[
            jax.ShapeDtypeStruct((length, group_cols), BF),
            jax.ShapeDtypeStruct((2, length, HD), BF),
            jax.ShapeDtypeStruct((D, 2 * group_cols), BF),
        ],
        in_specs=[in_smem] + [anywhere] * 4 + [in_vmem] * 9,
        out_specs=[in_vmem] * 3,
        scratch_shapes=[
            pltpu.VMEM((length, D), BF),
            pltpu.VMEM((length, HD), F32),
            pltpu.VMEM((length, HD), F32),
            pltpu.SemaphoreType.DMA((4,)),
        ],
        compiler_params=kernel_params(),
        cost_estimate=KERNEL_COST,
        name="attention_out",
    )(
        own,
        *grad,
        weights,
        queries,
        keys,
        values,
        cosine,
        sine,
        starts,
        normed_t,
        attended_t,
    )


def projection_out_body(
    own_rows,
    kv_rows,
    own,
    grad_q,
    ours,
    theirs,
    weights,
    normed_t,
    cosine,
    sine,
    tokens,
    gain_mlp,
    d_late,
    near,
    far,
    other_near,
    other_far,
    joined,
    sums,
):
    length, group_cols = grad_q.shape
    wide = group_cols + HD
    s = own[0]
    x, c = s // 2, lax.rem(s, 2)
    key_grad = ours[0].astype(F32) + theirs[0].astype(F32)
    key_grad = key_grad * cosine[...] - pltpu.roll(key_grad, HD // 2, 1) * sine[...]
    value_grad = ours[1].astype(F32) + theirs[1].astype(F32)
    joined[:, 0:group_cols] = grad_q[...]
    joined[:, group_cols:] = jnp.where(c == 0, key_grad, value_grad).astype(BF)
    one = jnp.where(
        c == 0,
        weights[:, group_cols : group_cols + HD],
        weights[:, group_cols + HD : group_cols + 2 * HD],
    )
    sums[...] = jnp.zeros_like(sums)
    gain_sum = jnp.zeros((1, D), F32)
    for first in range(0, length, QUERY_ROWS):
        r = pl.ds(first, QUERY_ROWS)
        term = dot_t(joined[r, 0:group_cols], weights[:, 0:group_cols]) + dot_t(
            joined[r, group_cols:], one
        )
        value = tokens[r, :].astype(F32)
        gain_sum += jnp.sum(term * (value * rms_factor(value)), axis=0, keepdims=True)
        split_store(
            s, first // QUERY_ROWS, term.astype(BF), (near, far, other_near, other_far)
        )

    bias = jnp.sum(joined[...].astype(F32), axis=0, keepdims=True)
    lane = lax.broadcasted_iota(jnp.int32, (HD, D // 2), 1)
    feature = lax.broadcasted_iota(jnp.int32, (HD, D // 2), 0)
    core, inner = lax.div(lane, D // 4), lax.rem(lane, D // 4)
    owner, row = lax.div(inner, own_rows), lax.rem(inner, own_rows)
    spot = core * (HD // 2) + owner * kv_rows + row
    chosen = jnp.where((spot == feature) & (row < kv_rows), 1.0, 0.0).astype(BF)
    spread = dot(bias[:, group_cols:].astype(BF), chosen)
    sums[0:1, :] = gain_sum
    sums[1:2, :] = gain_mlp[...]
    sums[2:3, pl.ds(pl.multiple_of(s * group_cols, LANE), group_cols)] = bias[:, 0:group_cols]
    sums[3:4, pl.ds(pl.multiple_of(x * (D // 2), LANE), D // 2)] = spread
    d_late[:, 0:HD] = dot(normed_t[...], joined[:, group_cols:]).astype(BF)
    d_late[:, HD:] = sums[...].T.astype(BF)


def projection_out(
    own_rows,
    kv_rows,
    own,
    grad_q,
    ours,
    theirs,
    weights,
    normed_t,
    cosine,
    sine,
    tokens,
    gain_mlp,
):
    length, group_cols = grad_q.shape
    wide = group_cols + HD
    return pl.pallas_call(
        functools.partial(projection_out_body, own_rows, kv_rows),
        out_shape=[
            jax.ShapeDtypeStruct((D, HD + LANE), BF),
            *[jax.ShapeDtypeStruct((QUERY_ROWS, D), BF)] * 4,
        ],
        in_specs=[in_smem] + [in_vmem] * 9,
        out_specs=[in_vmem] * 5,
        scratch_shapes=[pltpu.VMEM((length, wide), BF), pltpu.VMEM((LANE, D), F32)],
        compiler_params=kernel_params(),
        cost_estimate=KERNEL_COST,
        name="projection_out",
    )(own, grad_q, ours, theirs, weights, normed_t, cosine, sine, tokens, gain_mlp)


def plane_copies(chip, parts, target, sems, first):
    x, y = lax.div(chip, 2), lax.rem(chip, 2)
    copies = []
    for i, part in enumerate(parts):
        owner = 2 * (1 - x if i % 2 else x) + (1 - y if i // 2 else y)
        r = pl.ds(pl.multiple_of(owner * QUERY_ROWS, QUERY_ROWS), QUERY_ROWS)
        copies.append(pltpu.make_async_copy(part, target.at[r], sems.at[first + i]))
    return copies


def weight_terms(c, normed_t, cotangent_t, grad_gate, grad_up, activated, keep, send):
    owner_rows = D // 4
    for part in range(2):
        for targets, core in ((send, 1 - c), (keep, c)):
            r = pl.ds(pl.multiple_of((2 * part + core) * owner_rows, LANE), owner_rows)
            targets[0][part] = dot(normed_t[r, :], grad_gate[...]).astype(BF)
            targets[1][part] = dot(normed_t[r, :], grad_up[...]).astype(BF)
            targets[2][part] = dot(cotangent_t[r, :], activated[...]).astype(BF)


def last_weights_body(
    own, normed_t, cotangent_t, grad_gate, grad_up, activated, *targets
):
    weight_terms(
        own[0], normed_t, cotangent_t, grad_gate, grad_up, activated, targets[:3], targets[3:]
    )


def last_weights(own, turned, parts):
    tokens, cols = parts[0].shape
    owner_rows = D // 4
    piece = jax.ShapeDtypeStruct((2, owner_rows, cols), BF)
    piece_spec = pl.BlockSpec((2, owner_rows, TILE), lambda i: (0, 0, i))
    whole = pl.BlockSpec((D, tokens), lambda i: (0, 0), pipeline_mode=pl.Buffered(1))
    part = pl.BlockSpec((tokens, TILE), lambda i: (0, i))
    return pl.pallas_call(
        last_weights_body,
        grid=(cols // TILE,),
        out_shape=[piece] * 6,
        in_specs=[in_smem, whole, whole, part, part, part],
        out_specs=[piece_spec] * 6,
        compiler_params=kernel_params(),
        cost_estimate=KERNEL_COST,
        name="last_weights",
    )(own, *turned, *parts)


def feed_forward_body(planes, rows, first, last, *refs):
    places, own = refs[0], refs[1]
    mine = refs[2 : 2 + planes]
    theirs = refs[2 + planes : 2 + 2 * planes]
    rest = list(refs[2 + 2 * planes :])
    normed_parts, cot_parts = [[rest.pop(0) for _ in range(4)] for _ in range(2)]
    totals_in = [] if first else [rest.pop(0) for _ in range(2)]
    if last:
        grad_gate, grad_up, activated = [rest.pop(0) for _ in range(3)]
    else:
        keep, send = [rest.pop(0) for _ in range(2)]
    turned_out = [rest.pop(0) for _ in range(2)] if first else []
    totals_out = [rest.pop(0) for _ in range(2)]
    weights, grad_total, branch_total = [rest.pop(0) for _ in range(3)]
    normed, cotangent, weight_sems, sems = [rest.pop(0) for _ in range(4)]
    if last:
        low = rest
    else:
        grad_gate, grad_up, activated, normed_t, cotangent_t = rest
    step, steps = pl.program_id(0), pl.num_programs(0)
    tokens = normed.shape[0]
    c = own[0]
    normed_loads = plane_copies(own[1], normed_parts, normed, sems, 8)
    cot_loads = plane_copies(own[1], cot_parts, cotangent, sems, 12)
    turned_ends = [
        pltpu.make_async_copy(source, target, sems.at[16 + i])
        for i, (source, target) in enumerate(
            zip((normed_t, cotangent_t) if first else (), turned_out)
        )
    ]
    fills = [
        pltpu.make_async_copy(source, target, sems.at[i])
        for i, (source, target) in enumerate(zip(totals_in, (grad_total, branch_total)))
    ]
    if last:
        ends = [
            pltpu.make_async_copy(low[i], target, sems.at[i]) for i, target in enumerate(totals_out)
        ]
    else:
        ends = [
            pltpu.make_async_copy(source, target, sems.at[i])
            for i, (source, target) in enumerate(zip((grad_total, branch_total), totals_out))
        ]

    def weight_copies(at, slot):
        cols = pl.ds(pl.multiple_of(at * TILE, TILE), TILE)
        copies = []
        for k in range(planes):
            base = places[k] * (2 * rows)
            for side, source in enumerate((mine[k], theirs[k])):
                start = base + (c if side == 0 else 1 - c) * rows
                copies.append(
                    pltpu.make_async_copy(
                        source.at[:, :, cols],
                        weights.at[slot, :, pl.ds(pl.multiple_of(start, 16), rows), :],
                        weight_sems.at[slot, 2 * k + side],
                    )
                )
        return copies

    slot = lax.rem(step, 2)

    @pl.when(step == 0)
    def _():
        for load in normed_loads:
            load.start()
        for copy in weight_copies(0, 0):
            copy.start()
        for load in cot_loads + fills:
            load.start()

    @pl.when(step + 1 < steps)
    def _():
        for copy in weight_copies(step + 1, 1 - slot):
            copy.start()

    if first:

        @pl.when(step == 0)
        def _():
            grad_total[...] = jnp.zeros_like(grad_total)
            branch_total[...] = jnp.zeros_like(branch_total)

    @pl.when(step == 0)
    def _():
        for load in normed_loads:
            load.wait()

    for copy in weight_copies(step, slot):
        copy.wait()

    @pl.when(step == 0)
    def _():
        for load in cot_loads:
            load.wait()

    block = min(256, tokens)
    for start in range(0, tokens, block):
        r = pl.ds(start, block)
        some = normed[r, :]
        gate = dot(some, weights[slot, 0])
        up = dot(some, weights[slot, 1])
        grad_act = dot(cotangent[r, :], weights[slot, 2])
        sigma = jax.nn.sigmoid(gate)
        silu = gate * sigma
        activated[r, :] = (silu * up).astype(BF)
        grad_gate[r, :] = (grad_act * up * (sigma + silu * (1.0 - sigma))).astype(BF)
        grad_up[r, :] = (grad_act * silu).astype(BF)

    @pl.when(step == 0)
    def _():
        for fill in fills:
            fill.wait()

    for start in range(0, tokens, block):
        r = pl.ds(start, block)
        grad_total[r, :] += dot_t(grad_gate[r, :], weights[slot, 0]) + dot_t(
            grad_up[r, :], weights[slot, 1]
        )
        branch_total[r, :] += dot_t(activated[r, :], weights[slot, 2])

    @pl.when(step == steps - 1)
    def _():
        if last:
            low[0][...] = grad_total[...].astype(BF)
            low[1][...] = branch_total[...].astype(BF)
        for end in ends:
            end.start()

    if not last:

        @pl.when(step == 0)
        def _():
            for source, target in ((normed, normed_t), (cotangent, cotangent_t)):
                for start in range(0, D, TILE):
                    cols = pl.ds(start, TILE)
                    target[cols, :] = source[:, cols].T
            for end in turned_ends:
                end.start()

        keep, send = [[piece.at[kind] for kind in range(3)] for piece in (keep, send)]
        weight_terms(c, normed_t, cotangent_t, grad_gate, grad_up, activated, keep, send)

    @pl.when(step == steps - 1)
    def _():
        for end in ends + turned_ends:
            end.wait()


def feed_forward(places, own, mine, theirs, normed, cotangent, totals, last):
    planes = len(mine)
    rows, cols = mine[0].shape[1:]
    tokens = 4 * QUERY_ROWS
    first = totals is None
    totals = () if first else totals
    if last:
        shapes = [jax.ShapeDtypeStruct((tokens, cols), BF)] * 3
        specs = [pl.BlockSpec((tokens, TILE), lambda i, *_: (0, i))] * 3
    else:
        owner_rows = D // 4
        shapes = [jax.ShapeDtypeStruct((3, 2, owner_rows, cols), BF)] * 2
        specs = [pl.BlockSpec((3, 2, owner_rows, TILE), lambda i, *_: (0, 0, 0, i))] * 2
    blocks = len(shapes)
    if first:
        shapes += [jax.ShapeDtypeStruct((D, tokens), BF)] * 2
    if last:
        shapes += [jax.ShapeDtypeStruct((tokens, D), BF)] * 2
    else:
        shapes += [jax.ShapeDtypeStruct((tokens, D), F32)] * 2
    scratch = [pltpu.VMEM((2, 3, D, TILE), BF)]
    scratch += [pltpu.VMEM((tokens, D), F32)] * 2
    scratch += [pltpu.VMEM((tokens, D), BF)] * 2
    scratch += [pltpu.SemaphoreType.DMA((2, 2 * planes)), pltpu.SemaphoreType.DMA((18,))]
    if last:
        scratch += [pltpu.VMEM((tokens, D), BF)] * 2
    else:
        scratch += [pltpu.VMEM((tokens, TILE), BF)] * 3 + [pltpu.VMEM((D, tokens), BF)] * 2
    inputs = [*mine, *theirs, *normed, *cotangent, *totals]
    return pl.pallas_call(
        functools.partial(feed_forward_body, planes, rows, first, last),
        grid=(cols // TILE,),
        out_shape=shapes,
        in_specs=[in_smem, in_smem] + [anywhere] * len(inputs),
        out_specs=specs + [anywhere] * (len(shapes) - blocks),
        scratch_shapes=scratch,
        compiler_params=kernel_params(),
        cost_estimate=KERNEL_COST,
        name="feed_forward",
    )(places, own, *inputs)


def assemble_body(*refs):
    parts, gate_up, down = refs[:-2], refs[-2], refs[-1]
    for chip, (start, (first, end)) in enumerate(zip(CHIP_STARTS, CHIP_VALID)):
        for part, (low, high) in zip(parts, CHUNKS):
            from_col = max(first * LANE, low)
            to_col = min(end * LANE, high)
            here = slice(from_col - low, to_col - low)
            there = slice(start * LANE + from_col, start * LANE + to_col)
            for kind in range(2):
                gate_up[:, kind, there] = part[chip, kind, :, here].astype(F32)
            down[:, there] = part[chip, 2, :, here].astype(F32)


def assemble(parts):
    rows = parts[0].shape[2]
    return pl.pallas_call(
        assemble_body,
        out_shape=[
            jax.ShapeDtypeStruct((rows, 2, FF), F32),
            jax.ShapeDtypeStruct((rows, FF), F32),
        ],
        in_specs=[in_vmem] * len(parts),
        out_specs=[in_vmem] * 2,
        compiler_params=kernel_params(),
        cost_estimate=KERNEL_COST,
        name="assemble",
    )(*parts)


def build(seq_count, fsdp_count):
    planes = fsdp_count // 2
    order = list(range(0, 1)) + list(range(1, planes, 2)) + list(range(2, planes, 2))[::-1]
    place = [order.index(plane) for plane in range(planes)]
    after = {order[i]: order[(i + 1) % planes] for i in range(planes)}
    ring_perm = [(z, after[z]) for z in range(planes)]
    other = [(0, 1), (1, 0)]
    rows_perm = [(0, 1), (3, 2)]

    def swap_x(value):
        return lax.ppermute(value, "x", other)

    def swap_c(value):
        return lax.ppermute(value, "c", other)

    def swap_y(value):
        return lax.ppermute(value, "y", other)

    def swap_xy(value):
        return lax.ppermute(value, ("x", "y"), [(i, 3 - i) for i in range(4)])

    def send_rows(value):
        return lax.ppermute(value, ("c", "y"), rows_perm)

    def ring(value):
        return lax.ppermute(value, "z", ring_perm)

    def ring_back(value):
        return lax.ppermute(value, "z", [(j, i) for i, j in ring_perm])

    def trade(blocks, axes):
        return lax.all_to_all(blocks, axes, split_axis=0, concat_axis=0, tiled=True)

    along = (planes - 1) // 2
    against = planes - 1 - along
    steps_behind = list(range(along + 1)) + [-i for i in range(1, against + 1)]

    def local(
        tokens,
        positions,
        w_query,
        w_key,
        w_value,
        w_output,
        gate_up,
        w_down,
        bias_query,
        bias_key,
        bias_value,
        gain_attn,
        gain_mlp,
        cotangent,
    ):
        x, c, z, y = [lax.axis_index(axis) for axis in ("x", "c", "z", "y")]
        s = 2 * x + c
        ring_order = jnp.array(order, jnp.int32)
        ring_place = jnp.array(place, jnp.int32)
        behind = ring_order[(ring_place[z] - jnp.array(steps_behind)) % planes].astype(jnp.int32)

        def ring_gather(piece, then=()):
            ahead, back = [piece], [piece]
            for _ in range(along):
                ahead.append(ring(ahead[-1]))
            for step in range(against):
                back.append(ring_back(tie(back[-1], then) if step else back[-1]))
            return ahead + back[1:]
        core = jnp.stack([c, 2 * x + y]).astype(jnp.int32)
        own_place = jnp.stack([s, y]).astype(jnp.int32)

        tok_rows = tokens.shape[1]
        length = tok_rows * seq_count
        per_group = HEADS // seq_count
        group_cols = per_group * HD
        w_rows = w_query.shape[0]
        own_rows = D // (seq_count * fsdp_count)

        def gather_sequence(own, then=()):
            far = swap_x(own)
            theirs = swap_c(own)
            return [own, far, theirs, swap_c(tie(far, theirs, then))]

        def gather_plane(own):
            return [own, swap_x(own), swap_y(own), swap_xy(own)]

        def scatter_plane(terms, then=()):
            came = trade(terms.reshape(4, tok_rows, D), ("x", "y"))
            return jnp.sum(tie(came, then).astype(F32), axis=0)

        wide = group_cols + 2 * HD
        small_rows = jnp.stack(
            [
                jnp.pad(vector, (0, wide + group_cols - vector.shape[0]))
                for vector in (gain_attn, gain_mlp, bias_query, bias_key, bias_value)
            ]
        )
        small_rows = jnp.pad(small_rows, ((0, 11), (0, 0)))
        attn_own = jnp.concatenate(
            [
                lax.dynamic_slice_in_dim(w_query, s * group_cols, group_cols, 1),
                lax.dynamic_slice_in_dim(w_key, x * HD, HD, 1),
                lax.dynamic_slice_in_dim(w_value, x * HD, HD, 1),
                lax.dynamic_slice_in_dim(w_output, s * group_cols, group_cols, 1),
            ],
            axis=1,
        )
        attn_payload = jnp.concatenate([attn_own, small_rows], axis=0)
        chunk_places = []
        for low, high in CHUNKS:
            table = []
            for start, (first, end) in zip(CHIP_STARTS, CHIP_VALID):
                edge = 1 if low == 0 and first > 0 else 0
                edge = 2 if high > end * LANE else edge
                table.append((start * LANE + low, edge))
            table = jnp.array(table, jnp.int32)
            chunk_places.append((table[2 * x + y], table[2 * x + 1 - y]))

        def cut(chunk, whose, then):
            low, high = CHUNKS[chunk]
            return cut_columns(tie(chunk_places[chunk][whose], then), gate_up, w_down, high - low)

        sent = cut(0, 1, ())
        attn_payload = tie(attn_payload, sent)
        token_far = swap_x(tokens[0])
        token_pieces = [tokens[0], token_far, swap_c(tokens[0])]
        attn_pieces = ring_gather(attn_payload, token_pieces[2])
        first_back = along + 1
        attn_theirs = [swap_y(tie(attn_pieces[0], attn_pieces[1]))]
        attn_theirs += [swap_y(piece) for piece in attn_pieces[1:-1]]

        came, kept = send_rows(sent), cut(0, 0, attn_payload)
        kept, came = tie((kept, came), attn_pieces[1:], attn_theirs[first_back], token_pieces[1:3])
        payloads = [jnp.where(c == y, kept, came)]
        token_pieces.append(swap_c(tie(token_far, payloads[0])))
        after = (payloads[0], token_pieces[3])
        cuts = [(cut(1, 1, after), cut(1, 0, after))]
        attn_theirs.append(swap_y(tie(attn_pieces[-1], cuts)))
        own_swapped = swap_c(tie(payloads[0], attn_theirs))
        for sent, kept in cuts:
            came = send_rows(tie(sent, attn_theirs))
            payloads.append(jnp.where(c == y, kept, came))
        chunk_pieces = [ring_gather(payloads[0])]
        cot_x = swap_x(tie(cotangent[0], cuts))
        cot_y = swap_y(tie(cotangent[0], attn_theirs))

        seq_positions = positions[0]
        cosine, sine = rope_tables(seq_positions)
        first_keys = (jnp.arange(length, dtype=jnp.int32) - seq_positions)[:, None]
        (
            normed_attn_t,
            queries,
            keys,
            values,
            attended_t,
            *out_terms,
            attn_weights,
            gains,
            tokens_all,
        ) = attention_in(
            behind,
            own_place,
            attn_pieces,
            attn_theirs,
            tie(token_pieces, cot_x),
            cosine,
            sine,
            first_keys,
            group_cols,
        )
        inputs = tokens[0].astype(F32)
        out_terms, queries, keys, values, attended_t, gains = tie(
            (out_terms, queries, keys, values, attended_t, gains),
            chunk_pieces[0][1 : along + 2],
            came,
            cot_y,
            own_swapped,
        )

        def scatter_sequence(near, far, other_near, other_far, then=()):
            leaves = (far.astype(F32) + swap_c(other_far).astype(F32)).astype(BF)
            leaves = tie(leaves, *then)
            back = swap_x(leaves)
            stays = near.astype(F32) + swap_c(other_near).astype(F32)
            return stays + back.astype(F32), leaves, back

        gain_a, gain_m = gains[0], gains[1]
        branch_attn, out_leaves, _ = scatter_sequence(*out_terms)
        cot_pieces = [cotangent[0], cot_x, cot_y, swap_y(tie(cot_x, out_terms))]
        hidden = inputs + tie(branch_attn, cot_pieces[3])
        factor_mlp = rms_factor(hidden)
        normed_own = (hidden * factor_mlp * gain_m).astype(BF)
        normed = gather_plane(normed_own)
        chunk_theirs = [[own_swapped] + [swap_c(piece) for piece in chunk_pieces[0][1:-1]], []]
        chunk_theirs[0].append(swap_c(tie(chunk_pieces[0][-1], normed[1:])))
        chunk_pieces.append(ring_gather(tie(payloads[1], normed_own)))

        def plane_ahead(steps):
            return ring_order[(ring_place[z] + steps) % planes]

        class RingScatter:
            def __init__(self, block):
                self.block = block
                self.own = block(z)
                self.first = [
                    block(plane_ahead(sign * steps)).astype(BF)
                    for steps, sign in ((along, 1), (against, -1))
                    if steps
                ]

            def go(self, then=()):
                self.arrived, self.second, self.last = [], [], []
                firsts = list(self.first)
                for steps, sign, move in ((along, 1, ring), (against, -1, ring_back)):
                    if steps:
                        running = firsts.pop(0)
                        for left in range(steps - 1, 0, -1):
                            came = tie(move(running), then)
                            self.arrived.append(came)
                            running = self.block(plane_ahead(sign * left)) + came.astype(F32)
                            running = running.astype(BF)
                            self.second.append(running)
                        came = move(running)
                        self.arrived.append(came)
                        self.last.append(came)
                return self

            def total(self, then=()):
                total = self.own
                for came in tie(self.last, then):
                    total = total + came.astype(F32)
                return total.astype(BF)

        def chunk_scatter(keep, send, then):
            def by_plane(piece):
                return piece.reshape(piece.shape[:-2] + (planes, 2 * own_rows, piece.shape[-1]))

            if isinstance(send, (list, tuple)):
                away = [by_plane(swap_c(piece)) for piece in send]
                keep = [by_plane(piece) for piece in keep]

                def block(plane):
                    return jnp.stack(
                        [
                            pick(ours, plane, 1).astype(F32) + pick(theirs, plane, 1).astype(F32)
                            for ours, theirs in zip(keep, away)
                        ]
                    )

            else:
                away = by_plane(tie(swap_c(send), then))
                keep = by_plane(keep)

                def block(plane):
                    return pick(keep, plane, 2).astype(F32) + pick(away, plane, 2).astype(F32)

            return RingScatter(block)

        before = [(), None]
        beside = [chunk_pieces[1][1 : along + 2]]
        totals = None
        scatters = []
        for chunk in range(len(CHUNKS)):
            last = chunk == len(CHUNKS) - 1
            results = feed_forward(
                behind,
                core,
                chunk_pieces[chunk],
                chunk_theirs[chunk],
                tie(normed, before[chunk]),
                cot_pieces,
                totals,
                last,
            )
            if last:
                results = tie(results, scatters[0].arrived[along])
                totals = results[3:]
                pieces = last_weights(core, turned, results[:3])
                keep, send = pieces[:3], pieces[3:]
            else:
                results = tie(results, beside[chunk])
                keep, send = results[:2]
                turned, totals = results[2:4], results[4:]
                own = tie(chunk_pieces[1][0], send)
                chunk_theirs[1] = [swap_c(piece) for piece in [own] + chunk_pieces[1][1:]]
            then = () if last else chunk_theirs[1][:-1]
            scatters.append(chunk_scatter(keep, send, then))
            if not last:
                scatters[0].go()
                before[1] = scatters[0].first
        last_sent = (keep, send)

        grad_out = cotangent[0].astype(F32)
        grad_hidden_norm, grad_gain_mlp = rms_backward(
            hidden, factor_mlp, gain_m, scatter_plane(totals[0], (last_sent, scatters[0].last[0], scatters[0].second))
        )
        grad_hidden = grad_out + grad_hidden_norm
        grad_pieces = gather_sequence(
            grad_hidden.astype(BF)
        )
        grad_q, grad_kv, d_early = attention_out(
            own_place,
            tie(grad_pieces, scatters[1].first),
            attn_weights,
            queries,
            keys,
            values,
            cosine,
            sine,
            first_keys,
            normed_attn_t,
            attended_t,
        )
        scatters[1].go()
        grad_q, grad_kv, d_early = tie(
            (grad_q, grad_kv, d_early), scatters[1].arrived[along], scatters[0].last[-1]
        )

        branch = trade(tie(totals[1], grad_pieces[1]).reshape(4, tok_rows, D), ("x", "y"))

        def owner_rows(partial):
            rows = partial.reshape(2, 2, planes, 2, own_rows, partial.shape[1])
            return pick(rows, 1 - y, 3), pick(rows, y, 3)

        grad_kv_theirs = swap_c(grad_kv)
        early_rows = owner_rows(d_early)
        kv_rows = KV * HD // (seq_count * fsdp_count)
        d_late, *in_terms = projection_out(
            own_rows,
            kv_rows,
            own_place,
            tie(grad_q, early_rows[0], scatters[1].second, branch),
            grad_kv,
            grad_kv_theirs,
            attn_weights,
            normed_attn_t,
            cosine,
            sine,
            tokens_all,
            grad_gain_mlp[None],
        )
        def owner_scatter(away, stays, then=()):
            def block(plane):
                return pick(stays, plane, 2).astype(F32) + pick(away, plane, 2).astype(F32)

            return RingScatter(block).go(then)

        def chunk_sum(scatter, then):
            total = scatter.total(then).reshape(3, 2, 2, own_rows, -1)
            return total.transpose(1, 2, 0, 3, 4).reshape(4, 3, own_rows, -1)

        early_away = tie(swap_y(early_rows[0]), d_late)
        late_leaves, late_stays = owner_rows(d_late)
        grad_normed_attn, in_leaves, in_back = scatter_sequence(*in_terms, (early_away, late_leaves))
        grad_input_norm, _ = rms_backward(
            inputs,
            rms_factor(inputs),
            gain_a,
            grad_normed_attn,
        )
        grad_input = grad_hidden + grad_input_norm
        result = hidden + jnp.sum(tie(branch, in_leaves).astype(F32), axis=0)
        result = result.astype(BF)
        first_sum = chunk_sum(scatters[0], in_leaves)
        gathered = [trade(first_sum, ("x", "y"))]

        late_away = tie(swap_y(late_leaves), in_back)
        early = owner_scatter(early_away, early_rows[1], (in_back, gathered))
        late = owner_scatter(late_away, late_stays)
        second_sum = chunk_sum(scatters[1], (early.first, late.first))
        gathered.append(trade(second_sum, ("x", "y")))
        d_gate_up, d_w_down = assemble(gathered)
        owned = [early.total(second_sum), late.total(second_sum)]
        owned = jnp.concatenate(owned, axis=-1).reshape(4, own_rows, -1)
        owned = trade(owned, ("x", "c")).astype(F32)
        early, late = owned[..., : 2 * group_cols], owned[..., 2 * group_cols :]
        d_w_output = jnp.concatenate([early[i, :, :group_cols] for i in range(4)], axis=1)
        d_w_query = jnp.concatenate([early[i, :, group_cols:] for i in range(4)], axis=1)
        d_w_key = jnp.concatenate([late[0, :, :HD], late[2, :, :HD]], axis=1)
        d_w_value = jnp.concatenate([late[1, :, :HD], late[3, :, :HD]], axis=1)
        sums = jnp.sum(late[:, :, HD:], axis=0)
        d_gain_attn, d_gain_mlp, d_bias_query = sums[:, 0], sums[:, 1], sums[:, 2]
        kv_sums = late[:, :kv_rows, HD + 3]
        d_bias_key = kv_sums[0] + kv_sums[2]
        d_bias_value = kv_sums[1] + kv_sums[3]
        return (
            result[None],
            grad_input[None],
            d_w_query,
            d_w_key,
            d_w_value,
            d_w_output,
            d_gate_up,
            d_w_down,
            d_bias_query,
            d_bias_key,
            d_bias_value,
            d_gain_attn,
            d_gain_mlp,
        )

    return local


def solution(mesh):
    seq, fsdp = mesh.shape["seq"], mesh.shape["fsdp"]
    grid = jax.sharding.Mesh(mesh.devices.reshape(seq // 2, 2, fsdp // 2, 2), ("x", "c", "z", "y"))
    by_rows, by_owner = ("z", "y"), ("x", "c", "z", "y")
    tokens = P(by_rows, ("x", "c"), None)
    rows, vector = P(by_rows, None), P(by_rows)
    owner, owner_vector = P(by_owner, None), P(by_owner)
    return jax.shard_map(
        build(seq, fsdp),
        mesh=grid,
        in_specs=(
            tokens,
            rows,
            rows,
            rows,
            rows,
            rows,
            P(by_rows, None, None),
            rows,
            vector,
            vector,
            vector,
            vector,
            vector,
            tokens,
        ),
        out_specs=(
            tokens,
            tokens,
            owner,
            owner,
            owner,
            owner,
            P(by_owner, None, None),
            owner,
            owner_vector,
            owner_vector,
            owner_vector,
            owner_vector,
            owner_vector,
        ),
        check_vma=False,
    )
```

```python
import functools

import jax
import jax.numpy as jnp
from jax import lax
from jax.experimental import pallas as pl
from jax.experimental.pallas import tpu as pltpu
from jax.sharding import PartitionSpec as P

D = 1536
HEADS = 12
KV = 2
HD = 128
FF = 8960
LANE = 128

epsilon = 1e-06
rope_base = 1000000.0
masked_value = -1e30
BF = jnp.bfloat16
F32 = jnp.float32
VMEM_BYTES = 60 * 1024 * 1024

CHIP_STARTS = (0, 18, 36, 52)
CHIP_VALID = ((0, 18), (0, 18), (0, 17), (1, 18))
TILE = 256
CHUNKS = ((0, 1280), (1280, 2304))
QUERY_ROWS = 256

anywhere = pl.BlockSpec(memory_space=pl.ANY)
in_vmem = pl.BlockSpec(memory_space=pltpu.VMEM)
in_smem = pl.BlockSpec(memory_space=pltpu.SMEM)


def rope_tables(positions):
    ladder = jnp.arange(HD // 2, dtype=F32)
    inverse = rope_base ** (-2.0 * ladder / HD)
    angles = positions.astype(F32)[:, None] * inverse[None, :]
    cosine, sine = jnp.cos(angles), jnp.sin(angles)
    return (
        jnp.concatenate([cosine, cosine], axis=-1),
        jnp.concatenate([-sine, sine], axis=-1),
    )


def rms_factor(value):
    return lax.rsqrt(jnp.mean(value * value, axis=-1, keepdims=True) + epsilon)


def rms_backward(value, factor, gain, grad):
    unit = value * factor
    weighted = grad * gain
    grad_gain = jnp.sum(grad * unit, axis=0)
    inner = jnp.mean(weighted * unit, axis=-1, keepdims=True)
    return (factor * (weighted - unit * inner), grad_gain)


def dot(left, right):
    return jnp.dot(left, right, preferred_element_type=F32)


def dot_t(left, right):
    return lax.dot_general(left, right, (((1,), (1,)), ((), ())), preferred_element_type=F32)


def t_dot(left, right):
    return lax.dot_general(left, right, (((0,), (0,)), ((), ())), preferred_element_type=F32)


def pick(array, index, axis=0):
    return lax.dynamic_index_in_dim(array, index, axis, keepdims=False)


def tie(value, *others):
    return lax.optimization_barrier((value, *others))[0] if jax.tree.leaves(others) else value


def kernel_params():
    return pltpu.CompilerParams(vmem_limit_bytes=VMEM_BYTES)


KERNEL_COST = pl.CostEstimate(flops=1_000_000, bytes_accessed=1_000_000, transcendentals=0)


def cut_body(place, gate_up, down, target, pairs, sems):
    cols = pl.ds(pl.multiple_of(place[0], LANE), target.shape[2])
    copies = [
        pltpu.make_async_copy(gate_up.at[:, :, cols], pairs, sems.at[0]),
        pltpu.make_async_copy(down.at[:, cols], target.at[2], sems.at[1]),
    ]
    for copy in copies:
        copy.start()
    copies[0].wait()
    target[0] = pairs[:, 0, :]
    target[1] = pairs[:, 1, :]
    copies[1].wait()
    empty = jnp.zeros((3, target.shape[1], LANE), BF)

    @pl.when(place[1] == 1)
    def _():
        target[:, :, 0:LANE] = empty

    @pl.when(place[1] == 2)
    def _():
        target[:, :, target.shape[2] - LANE :] = empty


def cut_columns(place, gate_up, down, cols):
    rows = down.shape[0]
    return pl.pallas_call(
        cut_body,
        out_shape=jax.ShapeDtypeStruct((3, rows, cols), BF),
        in_specs=[in_smem, anywhere, anywhere],
        out_specs=in_vmem,
        scratch_shapes=[pltpu.VMEM((rows, 2, cols), BF), pltpu.SemaphoreType.DMA((2,))],
        compiler_params=kernel_params(),
        cost_estimate=KERNEL_COST,
        name="cut_columns",
    )(place, gate_up, down)


def sequence_copies(s, sources, target, sems):
    near, far, other_near, other_far = sources
    rows = near.shape[0]
    x, c = s // 2, lax.rem(s, 2)
    copies = []
    for i, (source, owner) in enumerate(
        (
            (near, 2 * x + c),
            (far, 2 * (1 - x) + c),
            (other_near, 2 * x + 1 - c),
            (other_far, 2 * (1 - x) + 1 - c),
        )
    ):
        place = pl.multiple_of(owner * rows, LANE)
        copies.append(pltpu.make_async_copy(source, target.at[pl.ds(place, rows)], sems.at[i]))
    return copies


def split_store(s, block, value, targets):
    x, c = s // 2, lax.rem(s, 2)
    for i, target in enumerate(targets):
        far, away = i % 2, i // 2
        owner = 2 * (1 - x if far else x) + (1 - c if away else c)

        @pl.when(owner == block)
        def _():
            target[...] = value


def attention_in_body(planes, rows, *refs):
    places, own = refs[0], refs[1]
    mine = refs[2 : 2 + planes]
    theirs = refs[2 + planes : 2 + 2 * planes]
    sources = refs[2 + 2 * planes : 6 + 2 * planes]
    cosine, sine, starts = refs[6 + 2 * planes : 9 + 2 * planes]
    normed_t, queries, keys, values, attended_t = refs[9 + 2 * planes : 14 + 2 * planes]
    targets = refs[14 + 2 * planes : 18 + 2 * planes]
    weights, gains, tokens, small, attended, sems = refs[18 + 2 * planes :]
    length = tokens.shape[0]
    group_cols = queries.shape[1]
    blocks = 2 * planes
    s, y = own[0], own[1]
    copies = []
    for k in range(planes):
        for side, source in enumerate((mine[k], theirs[k])):
            block = places[k] * 2 + (y if side == 0 else 1 - y)
            first = pl.multiple_of(block * rows, 16)
            copies.append(
                pltpu.make_async_copy(
                    source.at[pl.ds(0, rows)], weights.at[pl.ds(first, rows)], sems.at[0, 2 * k + side]
                )
            )
            copies.append(
                pltpu.make_async_copy(
                    source.at[pl.ds(rows, 16)],
                    small.at[pl.ds(pl.multiple_of(block * 16, 16), 16)],
                    sems.at[1, 2 * k + side],
                )
            )
    for copy in copies:
        copy.start()
    for copy in copies:
        copy.wait()
    kv_own = KV * HD // blocks
    vectors = []
    for row, width in enumerate((rows, rows, rows, kv_own, kv_own)):
        vectors.append(
            jnp.concatenate(
                [small[pl.ds(16 * b + row, 1), 0:width].astype(F32) for b in range(blocks)], axis=1
            )
        )
    gains[0:1, :] = vectors[0]
    gains[1:2, :] = vectors[1]
    gains[2:3, :] = vectors[2]
    gains[3:4, 0 : KV * HD] = vectors[3]
    gains[4:5, 0 : KV * HD] = vectors[4]
    gain = gains[0:1, :]
    kv = s // 2
    bias = jnp.concatenate(
        [
            gains[2:3, pl.ds(pl.multiple_of(s * group_cols, LANE), group_cols)],
            gains[3:4, pl.ds(pl.multiple_of(kv * HD, LANE), HD)],
            gains[4:5, pl.ds(pl.multiple_of(kv * HD, LANE), HD)],
        ],
        axis=1,
    )
    wide = group_cols + 2 * HD
    heads = group_cols // HD
    x, c = s // 2, lax.rem(s, 2)
    owners = (2 * x + c, 2 * (1 - x) + c, 2 * x + 1 - c, 2 * (1 - x) + 1 - c)
    for source, owner in zip(sources, owners):
        r = pl.ds(pl.multiple_of(owner * QUERY_ROWS, QUERY_ROWS), QUERY_ROWS)
        tokens[r, :] = source[...]

    def project(at, carry):
        r = pl.ds(pl.multiple_of(at * QUERY_ROWS, QUERY_ROWS), QUERY_ROWS)
        value = tokens[r, :].astype(F32)
        low = (value * rms_factor(value) * gain).astype(BF)
        normed_t[:, r] = low.T
        qkv = dot(low, weights[:, 0:wide]) + bias
        cos_rows, sin_rows = cosine[r, :], sine[r, :]
        for head in range(heads + 1):
            one = qkv[:, head * HD : (head + 1) * HD]
            turned = (one * cos_rows + pltpu.roll(one, HD // 2, 1) * sin_rows).astype(BF)
            if head < heads:
                queries[r, head * HD : (head + 1) * HD] = turned
            else:
                keys[r, :] = turned
        values[r, :] = qkv[:, group_cols + HD :].astype(BF)
        return carry

    lax.fori_loop(0, length // QUERY_ROWS, project, 0)
    scaling = HD ** (-0.5)
    for first in range(0, length, QUERY_ROWS):
        r = pl.ds(first, QUERY_ROWS)
        reach = first + QUERY_ROWS
        query_place = first + lax.broadcasted_iota(jnp.int32, (QUERY_ROWS, reach), 0)
        key_place = lax.broadcasted_iota(jnp.int32, (QUERY_ROWS, reach), 1)
        allowed = (key_place <= query_place) & (key_place >= starts[r, :])
        hidden_keys = jnp.where(allowed, 0.0, masked_value)

        def attend(head, carry):
            cols = pl.ds(pl.multiple_of(head * HD, HD), HD)
            scores = dot_t(queries[r, cols], keys[0:reach, :]) * scaling + hidden_keys
            shifted = jnp.exp(scores - jnp.max(scores, axis=-1, keepdims=True))
            total = jnp.sum(shifted, axis=-1, keepdims=True)
            outcome = dot(shifted.astype(BF), values[0:reach, :])
            attended[:, cols] = (outcome / total).astype(BF)
            return carry

        lax.fori_loop(0, heads, attend, 0)
        attended_t[:, r] = attended[...].T
        term = dot_t(attended[...], weights[:, wide:]).astype(BF)
        split_store(s, first // QUERY_ROWS, term, targets)


def attention_in(places, own, mine, theirs, tokens, cosine, sine, starts, group_cols):
    planes = len(mine)
    rows = mine[0].shape[0] - 16
    length = cosine.shape[0]
    shapes = [
        jax.ShapeDtypeStruct((D, length), BF),
        jax.ShapeDtypeStruct((length, group_cols), BF),
        jax.ShapeDtypeStruct((length, HD), BF),
        jax.ShapeDtypeStruct((length, HD), BF),
        jax.ShapeDtypeStruct((group_cols, length), BF),
        *[jax.ShapeDtypeStruct((QUERY_ROWS, D), BF)] * 4,
        jax.ShapeDtypeStruct((D, mine[0].shape[1]), BF),
        jax.ShapeDtypeStruct((8, D), F32),
        jax.ShapeDtypeStruct((length, D), BF),
    ]
    return pl.pallas_call(
        functools.partial(attention_in_body, planes, rows),
        out_shape=shapes,
        in_specs=[in_smem, in_smem] + [anywhere] * (2 * planes) + [in_vmem] * 7,
        out_specs=[in_vmem] * len(shapes),
        scratch_shapes=[
            pltpu.VMEM((2 * planes * 16, mine[0].shape[1]), BF),
            pltpu.VMEM((QUERY_ROWS, group_cols), BF),
            pltpu.SemaphoreType.DMA((2, 2 * planes)),
        ],
        compiler_params=kernel_params(),
        cost_estimate=KERNEL_COST,
        name="attention_in",
    )(places, own, *mine, *theirs, *tokens, cosine, sine, starts)


def attention_out_body(
    own,
    near,
    far,
    other_near,
    other_far,
    weights,
    queries,
    keys,
    values,
    cosine,
    sine,
    starts,
    normed_t,
    attended_t,
    grad_q,
    grad_kv,
    d_early,
    grad,
    grad_k,
    grad_v,
    sems,
):
    copies = sequence_copies(own[0], (near, far, other_near, other_far), grad, sems)
    for copy in copies:
        copy.start()
    for copy in copies:
        copy.wait()
    length = grad.shape[0]
    group_cols = queries.shape[1]
    heads = group_cols // HD
    scaling = HD ** (-0.5)
    output = weights[:, group_cols + 2 * HD :]
    grad_k[...] = jnp.zeros_like(grad_k)
    grad_v[...] = jnp.zeros_like(grad_v)
    for first in range(0, length, QUERY_ROWS):
        r = pl.ds(first, QUERY_ROWS)
        reach = first + QUERY_ROWS
        grad_heads = dot(grad[r, :], output).astype(BF)
        query_place = first + lax.broadcasted_iota(jnp.int32, (QUERY_ROWS, reach), 0)
        key_place = lax.broadcasted_iota(jnp.int32, (QUERY_ROWS, reach), 1)
        allowed = (key_place <= query_place) & (key_place >= starts[r, :])
        cos_rows, sin_rows = cosine[r, :], sine[r, :]
        for head in range(heads):
            cols = slice(head * HD, (head + 1) * HD)
            one_query = queries[r, cols]
            one_grad = grad_heads[:, cols]
            scores = dot_t(one_query, keys[0:reach, :]) * scaling
            scores = jnp.where(allowed, scores, masked_value)
            shifted = jnp.exp(scores - jnp.max(scores, axis=-1, keepdims=True))
            probability = shifted * (1.0 / jnp.sum(shifted, axis=-1, keepdims=True))
            grad_prob = dot_t(one_grad, values[0:reach, :])
            weighted = probability * grad_prob
            inner = jnp.sum(weighted, axis=-1, keepdims=True)
            grad_low = (weighted - probability * inner).astype(BF)
            turned = (dot(grad_low, keys[0:reach, :]) * scaling).astype(BF).astype(F32)
            grad_q[r, cols] = (
                turned * cos_rows - pltpu.roll(turned, HD // 2, 1) * sin_rows
            ).astype(BF)
            grad_k[0:reach, :] += t_dot(grad_low, one_query)
            grad_v[0:reach, :] += t_dot(probability.astype(BF), one_grad)
    grad_kv[0] = (grad_k[...] * scaling).astype(BF)
    grad_kv[1] = grad_v[...].astype(BF)
    d_early[:, 0:group_cols] = dot(attended_t[...], grad[...]).astype(BF).T
    d_early[:, group_cols:] = dot(normed_t[...], grad_q[...]).astype(BF)


def attention_out(
    own, grad, weights, queries, keys, values, cosine, sine, starts, normed_t, attended_t
):
    length, group_cols = queries.shape
    return pl.pallas_call(
        attention_out_body,
        out_shape=[
            jax.ShapeDtypeStruct((length, group_cols), BF),
            jax.ShapeDtypeStruct((2, length, HD), BF),
            jax.ShapeDtypeStruct((D, 2 * group_cols), BF),
        ],
        in_specs=[in_smem] + [anywhere] * 4 + [in_vmem] * 9,
        out_specs=[in_vmem] * 3,
        scratch_shapes=[
            pltpu.VMEM((length, D), BF),
            pltpu.VMEM((length, HD), F32),
            pltpu.VMEM((length, HD), F32),
            pltpu.SemaphoreType.DMA((4,)),
        ],
        compiler_params=kernel_params(),
        cost_estimate=KERNEL_COST,
        name="attention_out",
    )(
        own,
        *grad,
        weights,
        queries,
        keys,
        values,
        cosine,
        sine,
        starts,
        normed_t,
        attended_t,
    )


def projection_out_body(
    own_rows,
    kv_rows,
    own,
    grad_q,
    ours,
    theirs,
    weights,
    normed_t,
    cosine,
    sine,
    tokens,
    gain_mlp,
    d_late,
    near,
    far,
    other_near,
    other_far,
    joined,
    sums,
):
    length, group_cols = grad_q.shape
    wide = group_cols + HD
    s = own[0]
    x, c = s // 2, lax.rem(s, 2)
    key_grad = ours[0].astype(F32) + theirs[0].astype(F32)
    key_grad = key_grad * cosine[...] - pltpu.roll(key_grad, HD // 2, 1) * sine[...]
    value_grad = ours[1].astype(F32) + theirs[1].astype(F32)
    joined[:, 0:group_cols] = grad_q[...]
    joined[:, group_cols:] = jnp.where(c == 0, key_grad, value_grad).astype(BF)
    one = jnp.where(
        c == 0,
        weights[:, group_cols : group_cols + HD],
        weights[:, group_cols + HD : group_cols + 2 * HD],
    )
    sums[...] = jnp.zeros_like(sums)
    gain_sum = jnp.zeros((1, D), F32)
    for first in range(0, length, QUERY_ROWS):
        r = pl.ds(first, QUERY_ROWS)
        term = dot_t(joined[r, 0:group_cols], weights[:, 0:group_cols]) + dot_t(
            joined[r, group_cols:], one
        )
        value = tokens[r, :].astype(F32)
        gain_sum += jnp.sum(term * (value * rms_factor(value)), axis=0, keepdims=True)
        split_store(
            s, first // QUERY_ROWS, term.astype(BF), (near, far, other_near, other_far)
        )

    bias = jnp.sum(joined[...].astype(F32), axis=0, keepdims=True)
    lane = lax.broadcasted_iota(jnp.int32, (HD, D // 2), 1)
    feature = lax.broadcasted_iota(jnp.int32, (HD, D // 2), 0)
    core, inner = lax.div(lane, D // 4), lax.rem(lane, D // 4)
    owner, row = lax.div(inner, own_rows), lax.rem(inner, own_rows)
    spot = core * (HD // 2) + owner * kv_rows + row
    chosen = jnp.where((spot == feature) & (row < kv_rows), 1.0, 0.0).astype(BF)
    spread = dot(bias[:, group_cols:].astype(BF), chosen)
    sums[0:1, :] = gain_sum
    sums[1:2, :] = gain_mlp[...]
    sums[2:3, pl.ds(pl.multiple_of(s * group_cols, LANE), group_cols)] = bias[:, 0:group_cols]
    sums[3:4, pl.ds(pl.multiple_of(x * (D // 2), LANE), D // 2)] = spread
    d_late[:, 0:HD] = dot(normed_t[...], joined[:, group_cols:]).astype(BF)
    d_late[:, HD:] = sums[...].T.astype(BF)


def projection_out(
    own_rows,
    kv_rows,
    own,
    grad_q,
    ours,
    theirs,
    weights,
    normed_t,
    cosine,
    sine,
    tokens,
    gain_mlp,
):
    length, group_cols = grad_q.shape
    wide = group_cols + HD
    return pl.pallas_call(
        functools.partial(projection_out_body, own_rows, kv_rows),
        out_shape=[
            jax.ShapeDtypeStruct((D, HD + LANE), BF),
            *[jax.ShapeDtypeStruct((QUERY_ROWS, D), BF)] * 4,
        ],
        in_specs=[in_smem] + [in_vmem] * 9,
        out_specs=[in_vmem] * 5,
        scratch_shapes=[pltpu.VMEM((length, wide), BF), pltpu.VMEM((LANE, D), F32)],
        compiler_params=kernel_params(),
        cost_estimate=KERNEL_COST,
        name="projection_out",
    )(own, grad_q, ours, theirs, weights, normed_t, cosine, sine, tokens, gain_mlp)


def plane_copies(chip, parts, target, sems, first):
    x, y = lax.div(chip, 2), lax.rem(chip, 2)
    copies = []
    for i, part in enumerate(parts):
        owner = 2 * (1 - x if i % 2 else x) + (1 - y if i // 2 else y)
        r = pl.ds(pl.multiple_of(owner * QUERY_ROWS, QUERY_ROWS), QUERY_ROWS)
        copies.append(pltpu.make_async_copy(part, target.at[r], sems.at[first + i]))
    return copies


def weight_terms(c, normed_t, cotangent_t, grad_gate, grad_up, activated, keep, send):
    owner_rows = D // 4
    for part in range(2):
        for targets, core in ((send, 1 - c), (keep, c)):
            r = pl.ds(pl.multiple_of((2 * part + core) * owner_rows, LANE), owner_rows)
            targets[0][part] = dot(normed_t[r, :], grad_gate[...]).astype(BF)
            targets[1][part] = dot(normed_t[r, :], grad_up[...]).astype(BF)
            targets[2][part] = dot(cotangent_t[r, :], activated[...]).astype(BF)


def last_weights_body(
    own, normed_t, cotangent_t, grad_gate, grad_up, activated, *targets
):
    weight_terms(
        own[0], normed_t, cotangent_t, grad_gate, grad_up, activated, targets[:3], targets[3:]
    )


def last_weights(own, turned, parts):
    tokens, cols = parts[0].shape
    owner_rows = D // 4
    piece = jax.ShapeDtypeStruct((2, owner_rows, cols), BF)
    piece_spec = pl.BlockSpec((2, owner_rows, TILE), lambda i: (0, 0, i))
    whole = pl.BlockSpec((D, tokens), lambda i: (0, 0), pipeline_mode=pl.Buffered(1))
    part = pl.BlockSpec((tokens, TILE), lambda i: (0, i))
    return pl.pallas_call(
        last_weights_body,
        grid=(cols // TILE,),
        out_shape=[piece] * 6,
        in_specs=[in_smem, whole, whole, part, part, part],
        out_specs=[piece_spec] * 6,
        compiler_params=kernel_params(),
        cost_estimate=KERNEL_COST,
        name="last_weights",
    )(own, *turned, *parts)


def feed_forward_body(planes, rows, first, last, *refs):
    places, own = refs[0], refs[1]
    mine = refs[2 : 2 + planes]
    theirs = refs[2 + planes : 2 + 2 * planes]
    rest = list(refs[2 + 2 * planes :])
    normed_parts, cot_parts = [[rest.pop(0) for _ in range(4)] for _ in range(2)]
    totals_in = [] if first else [rest.pop(0) for _ in range(2)]
    if last:
        grad_gate, grad_up, activated = [rest.pop(0) for _ in range(3)]
    else:
        keep, send = [rest.pop(0) for _ in range(2)]
    turned_out = [rest.pop(0) for _ in range(2)] if first else []
    totals_out = [rest.pop(0) for _ in range(2)]
    weights, grad_total, branch_total = [rest.pop(0) for _ in range(3)]
    normed, cotangent, weight_sems, sems = [rest.pop(0) for _ in range(4)]
    low = [rest.pop(0) for _ in range(2)]
    if not last:
        grad_gate, grad_up, activated, normed_t, cotangent_t = rest
    step, steps = pl.program_id(0), pl.num_programs(0)
    tokens = normed.shape[0]
    c, chip = own[0], own[1]
    normed_loads = plane_copies(chip, normed_parts, normed, sems, 8)
    cot_loads = plane_copies(chip, cot_parts, cotangent, sems, 12)
    turned_ends = [
        pltpu.make_async_copy(source, target, sems.at[16 + i])
        for i, (source, target) in enumerate(
            zip((normed_t, cotangent_t) if first else (), turned_out)
        )
    ]
    fills = [
        pltpu.make_async_copy(source, target, sems.at[i])
        for i, (source, target) in enumerate(zip(totals_in, low))
    ]
    ends = [
        pltpu.make_async_copy(source, target, sems.at[2 + i])
        for i, (source, target) in enumerate(zip(low, totals_out))
    ]

    def weight_copies(at, slot):
        cols = pl.ds(pl.multiple_of(at * TILE, TILE), TILE)
        copies = []
        for k in range(planes):
            base = places[k] * (2 * rows)
            for side, source in enumerate((mine[k], theirs[k])):
                start = base + (c if side == 0 else 1 - c) * rows
                copies.append(
                    pltpu.make_async_copy(
                        source.at[:, :, cols],
                        weights.at[slot, :, pl.ds(pl.multiple_of(start, 16), rows), :],
                        weight_sems.at[slot, 2 * k + side],
                    )
                )
        return copies

    slot = lax.rem(step, 2)

    @pl.when(step == 0)
    def _():
        for load in normed_loads:
            load.start()
        for copy in weight_copies(0, 0):
            copy.start()
        for load in cot_loads + fills:
            load.start()

    @pl.when(step + 1 < steps)
    def _():
        for copy in weight_copies(step + 1, 1 - slot):
            copy.start()

    @pl.when(step == 0)
    def _():
        grad_total[...] = jnp.zeros_like(grad_total)
        branch_total[...] = jnp.zeros_like(branch_total)
        for load in normed_loads:
            load.wait()

    for copy in weight_copies(step, slot):
        copy.wait()

    block = min(256, tokens)
    for start in range(0, tokens, block):
        r = pl.ds(start, block)
        some = normed[r, :]
        gate = dot(some, weights[slot, 0])
        up = dot(some, weights[slot, 1])
        if start == 0:

            @pl.when(step == 0)
            def _():
                for load in cot_loads:
                    load.wait()

        grad_act = dot(cotangent[r, :], weights[slot, 2])
        sigma = jax.nn.sigmoid(gate)
        silu = gate * sigma
        activated[r, :] = (silu * up).astype(BF)
        grad_gate[r, :] = (grad_act * up * (sigma + silu * (1.0 - sigma))).astype(BF)
        grad_up[r, :] = (grad_act * silu).astype(BF)

    for start in range(0, tokens, block):
        r = pl.ds(start, block)
        grad_total[r, :] += dot_t(grad_gate[r, :], weights[slot, 0]) + dot_t(
            grad_up[r, :], weights[slot, 1]
        )
        branch_total[r, :] += dot_t(activated[r, :], weights[slot, 2])

    @pl.when(step == steps - 1)
    def _():
        for fill in fills:
            fill.wait()
        for target, total in zip(low, (grad_total, branch_total)):
            value = total[...]
            target[...] = (value if first else value + target[...].astype(F32)).astype(BF)
        for end in ends:
            end.start()

    if not last:

        @pl.when(step == 0)
        def _():
            for source, target in ((normed, normed_t), (cotangent, cotangent_t)):
                for start in range(0, D, TILE):
                    cols = pl.ds(start, TILE)
                    target[cols, :] = source[:, cols].T
            for end in turned_ends:
                end.start()

        keep, send = [[piece.at[kind] for kind in range(3)] for piece in (keep, send)]
        weight_terms(c, normed_t, cotangent_t, grad_gate, grad_up, activated, keep, send)

    @pl.when(step == steps - 1)
    def _():
        for end in ends + turned_ends:
            end.wait()


def feed_forward(places, own, mine, theirs, normed, cotangent, totals, last):
    planes = len(mine)
    rows, cols = mine[0].shape[1:]
    tokens = 4 * QUERY_ROWS
    first = totals is None
    totals = () if first else totals
    if last:
        shapes = [jax.ShapeDtypeStruct((tokens, cols), BF)] * 3
        specs = [pl.BlockSpec((tokens, TILE), lambda i, *_: (0, i))] * 3
    else:
        owner_rows = D // 4
        shapes = [jax.ShapeDtypeStruct((3, 2, owner_rows, cols), BF)] * 2
        specs = [pl.BlockSpec((3, 2, owner_rows, TILE), lambda i, *_: (0, 0, 0, i))] * 2
    blocks = len(shapes)
    if first:
        shapes += [jax.ShapeDtypeStruct((D, tokens), BF)] * 2
    shapes += [jax.ShapeDtypeStruct((tokens, D), BF)] * 2
    scratch = [pltpu.VMEM((2, 3, D, TILE), BF)]
    scratch += [pltpu.VMEM((tokens, D), F32)] * 2
    scratch += [pltpu.VMEM((tokens, D), BF)] * 2
    scratch += [pltpu.SemaphoreType.DMA((2, 2 * planes)), pltpu.SemaphoreType.DMA((18,))]
    scratch += [pltpu.VMEM((tokens, D), BF)] * 2
    if not last:
        scratch += [pltpu.VMEM((tokens, TILE), BF)] * 3 + [pltpu.VMEM((D, tokens), BF)] * 2
    inputs = [*mine, *theirs, *normed, *cotangent, *totals]
    return pl.pallas_call(
        functools.partial(feed_forward_body, planes, rows, first, last),
        grid=(cols // TILE,),
        out_shape=shapes,
        in_specs=[in_smem, in_smem] + [anywhere] * len(inputs),
        out_specs=specs + [anywhere] * (len(shapes) - blocks),
        scratch_shapes=scratch,
        compiler_params=kernel_params(),
        cost_estimate=KERNEL_COST,
        name="feed_forward",
    )(places, own, *inputs)


def add_planes_body(kinds, count, rows, where, *refs):
    ours, theirs = refs[:kinds], refs[kinds : 2 * kinds]
    targets = refs[2 * kinds : 2 * kinds + count]
    held, sems = refs[2 * kinds + count :]
    copies = []
    for i in range(count):
        r = pl.ds(pl.multiple_of(where[i] * rows, 16), rows)
        for kind in range(3):
            for side, sources in enumerate((ours, theirs)):
                source = sources[kind] if kinds == 3 else sources[0].at[kind]
                copies.append(
                    pltpu.make_async_copy(
                        source.at[:, r, :], held.at[i, kind, side], sems.at[i, kind, side]
                    )
                )
    for copy in copies:
        copy.start()
    for i in range(count):
        for kind in range(3):
            for side in range(2):
                copies[(i * 3 + kind) * 2 + side].wait()
            total = held[i, kind, 0].astype(F32) + held[i, kind, 1].astype(F32)
            targets[i][kind] = total.astype(BF)


def add_planes(ours, theirs, rows, where):
    count, cols = where.shape[0], ours[0].shape[-1]
    return pl.pallas_call(
        functools.partial(add_planes_body, len(ours), count, rows),
        out_shape=[jax.ShapeDtypeStruct((3, 2, rows, cols), BF)] * count,
        in_specs=[in_smem] + [anywhere] * (2 * len(ours)),
        out_specs=[in_vmem] * count,
        scratch_shapes=[
            pltpu.VMEM((count, 3, 2, 2, rows, cols), BF),
            pltpu.SemaphoreType.DMA((count, 3, 2)),
        ],
        compiler_params=kernel_params(),
        cost_estimate=KERNEL_COST,
        name="add_planes",
    )(where, *ours, *theirs)


def assemble_body(*refs):
    parts, gate_up, down = refs[:-2], refs[-2], refs[-1]
    for chip, (start, (first, end)) in enumerate(zip(CHIP_STARTS, CHIP_VALID)):
        for part, (low, high) in zip(parts, CHUNKS):
            from_col = max(first * LANE, low)
            to_col = min(end * LANE, high)
            here = slice(from_col - low, to_col - low)
            there = slice(start * LANE + from_col, start * LANE + to_col)
            for kind in range(2):
                gate_up[:, kind, there] = part[chip, kind, :, here].astype(F32)
            down[:, there] = part[chip, 2, :, here].astype(F32)


def assemble(parts):
    rows = parts[0].shape[2]
    return pl.pallas_call(
        assemble_body,
        out_shape=[
            jax.ShapeDtypeStruct((rows, 2, FF), F32),
            jax.ShapeDtypeStruct((rows, FF), F32),
        ],
        in_specs=[in_vmem] * len(parts),
        out_specs=[in_vmem] * 2,
        compiler_params=kernel_params(),
        cost_estimate=KERNEL_COST,
        name="assemble",
    )(*parts)


def build(seq_count, fsdp_count):
    planes = fsdp_count // 2
    order = list(range(0, 1)) + list(range(1, planes, 2)) + list(range(2, planes, 2))[::-1]
    place = [order.index(plane) for plane in range(planes)]
    after = {order[i]: order[(i + 1) % planes] for i in range(planes)}
    ring_perm = [(z, after[z]) for z in range(planes)]
    other = [(0, 1), (1, 0)]
    rows_perm = [(0, 1), (3, 2)]

    def swap_x(value):
        return lax.ppermute(value, "x", other)

    def swap_c(value):
        return lax.ppermute(value, "c", other)

    def swap_y(value):
        return lax.ppermute(value, "y", other)

    def swap_xy(value):
        return lax.ppermute(value, ("x", "y"), [(i, 3 - i) for i in range(4)])

    def send_rows(value):
        return lax.ppermute(value, ("c", "y"), rows_perm)

    def ring(value):
        return lax.ppermute(value, "z", ring_perm)

    def ring_back(value):
        return lax.ppermute(value, "z", [(j, i) for i, j in ring_perm])

    def trade(blocks, axes):
        return lax.all_to_all(blocks, axes, split_axis=0, concat_axis=0, tiled=True)

    along = (planes - 1) // 2
    against = planes - 1 - along
    steps_behind = list(range(along + 1)) + [-i for i in range(1, against + 1)]

    def local(
        tokens,
        positions,
        w_query,
        w_key,
        w_value,
        w_output,
        gate_up,
        w_down,
        bias_query,
        bias_key,
        bias_value,
        gain_attn,
        gain_mlp,
        cotangent,
    ):
        x, c, z, y = [lax.axis_index(axis) for axis in ("x", "c", "z", "y")]
        s = 2 * x + c
        ring_order = jnp.array(order, jnp.int32)
        ring_place = jnp.array(place, jnp.int32)
        behind = ring_order[(ring_place[z] - jnp.array(steps_behind)) % planes].astype(jnp.int32)

        def ring_gather(piece, then=()):
            ahead, back = [piece], [piece]
            for _ in range(along):
                ahead.append(ring(ahead[-1]))
            for step in range(against):
                back.append(ring_back(tie(back[-1], then) if step else back[-1]))
            return ahead + back[1:]
        core = jnp.stack([c, 2 * x + y]).astype(jnp.int32)
        own_place = jnp.stack([s, y]).astype(jnp.int32)

        tok_rows = tokens.shape[1]
        length = tok_rows * seq_count
        per_group = HEADS // seq_count
        group_cols = per_group * HD
        w_rows = w_query.shape[0]
        own_rows = D // (seq_count * fsdp_count)

        def gather_sequence(own, then=()):
            far = swap_x(own)
            theirs = swap_c(own)
            return [own, far, theirs, swap_c(tie(far, theirs, then))]

        def gather_plane(own):
            return [own, swap_x(own), swap_y(own), swap_xy(own)]

        def scatter_plane(terms, then=()):
            came = trade(terms.reshape(4, tok_rows, D), ("x", "y"))
            return jnp.sum(tie(came, then).astype(F32), axis=0)

        wide = group_cols + 2 * HD
        small_rows = jnp.stack(
            [
                jnp.pad(vector, (0, wide + group_cols - vector.shape[0]))
                for vector in (gain_attn, gain_mlp, bias_query, bias_key, bias_value)
            ]
        )
        small_rows = jnp.pad(small_rows, ((0, 11), (0, 0)))
        attn_own = jnp.concatenate(
            [
                lax.dynamic_slice_in_dim(w_query, s * group_cols, group_cols, 1),
                lax.dynamic_slice_in_dim(w_key, x * HD, HD, 1),
                lax.dynamic_slice_in_dim(w_value, x * HD, HD, 1),
                lax.dynamic_slice_in_dim(w_output, s * group_cols, group_cols, 1),
            ],
            axis=1,
        )
        attn_payload = jnp.concatenate([attn_own, small_rows], axis=0)
        chunk_places = []
        for low, high in CHUNKS:
            table = []
            for start, (first, end) in zip(CHIP_STARTS, CHIP_VALID):
                edge = 1 if low == 0 and first > 0 else 0
                edge = 2 if high > end * LANE else edge
                table.append((start * LANE + low, edge))
            table = jnp.array(table, jnp.int32)
            chunk_places.append((table[2 * x + y], table[2 * x + 1 - y]))

        def cut(chunk, whose, then):
            low, high = CHUNKS[chunk]
            return cut_columns(tie(chunk_places[chunk][whose], then), gate_up, w_down, high - low)

        sent = cut(0, 1, ())
        attn_payload = tie(attn_payload, sent)
        token_far = swap_x(tokens[0])
        token_pieces = [tokens[0], token_far, swap_c(tokens[0])]
        attn_pieces = ring_gather(attn_payload, token_pieces[2])
        first_back = along + 1
        attn_theirs = [swap_y(tie(attn_pieces[0], attn_pieces[1]))]
        attn_theirs += [swap_y(piece) for piece in attn_pieces[1:-1]]

        came, kept = send_rows(sent), cut(0, 0, attn_payload)
        cuts = [(cut(1, 1, kept), cut(1, 0, kept))]
        kept, came = tie(
            (kept, came), attn_pieces[1:], attn_theirs[first_back], token_pieces[1:3], cuts
        )
        payloads = [jnp.where(c == y, kept, came)]
        token_pieces.append(swap_c(tie(token_far, payloads[0])))
        attn_theirs.append(swap_y(tie(attn_pieces[-1], payloads[0])))
        own_swapped = swap_c(tie(payloads[0], attn_theirs))
        for sent, kept in cuts:
            came = send_rows(tie(sent, attn_theirs))
            payloads.append(jnp.where(c == y, kept, came))
        chunk_pieces = [ring_gather(payloads[0])]
        cot_x = swap_x(tie(cotangent[0], cuts))
        cot_y = swap_y(tie(cotangent[0], attn_theirs))

        seq_positions = positions[0]
        cosine, sine = rope_tables(seq_positions)
        first_keys = (jnp.arange(length, dtype=jnp.int32) - seq_positions)[:, None]
        (
            normed_attn_t,
            queries,
            keys,
            values,
            attended_t,
            *out_terms,
            attn_weights,
            gains,
            tokens_all,
        ) = attention_in(
            behind,
            own_place,
            attn_pieces,
            attn_theirs,
            tie(token_pieces, cot_x),
            cosine,
            sine,
            first_keys,
            group_cols,
        )
        inputs = tokens[0].astype(F32)
        out_terms, queries, keys, values, attended_t, gains = tie(
            (out_terms, queries, keys, values, attended_t, gains),
            chunk_pieces[0][1 : along + 2],
            came,
            cot_y,
            own_swapped,
        )

        def scatter_sequence(near, far, other_near, other_far, then=()):
            leaves = (far.astype(F32) + swap_c(other_far).astype(F32)).astype(BF)
            leaves = tie(leaves, *then)
            back = swap_x(leaves)
            stays = near.astype(F32) + swap_c(other_near).astype(F32)
            return stays + back.astype(F32), leaves, back

        gain_a, gain_m = gains[0], gains[1]
        branch_attn, out_leaves, _ = scatter_sequence(*out_terms)
        cot_pieces = [cotangent[0], cot_x, cot_y, swap_y(tie(cot_x, out_terms))]
        hidden = inputs + tie(branch_attn, cot_pieces[3])
        factor_mlp = rms_factor(hidden)
        normed_own = (hidden * factor_mlp * gain_m).astype(BF)
        normed = gather_plane(normed_own)
        chunk_theirs = [[own_swapped] + [swap_c(piece) for piece in chunk_pieces[0][1:-1]], []]
        chunk_theirs[0].append(swap_c(tie(chunk_pieces[0][-1], normed[1:])))
        chunk_pieces.append(ring_gather(tie(payloads[1], normed_own)))

        def plane_ahead(steps):
            return ring_order[(ring_place[z] + steps) % planes]

        class RingScatter:
            def __init__(self, block, first=None):
                self.block = block
                self.own = block(z)
                self.first = first or [
                    block(plane_ahead(sign * steps)).astype(BF)
                    for steps, sign in ((along, 1), (against, -1))
                    if steps
                ]

            def go(self, then=(), together=False):
                self.arrived, self.second, self.last = [], [], []
                firsts = list(self.first)
                for steps, sign, move in ((along, 1, ring), (against, -1, ring_back)):
                    then = (then, self.last) if together else then
                    if steps:
                        running = firsts.pop(0)
                        for left in range(steps - 1, 0, -1):
                            came = tie(move(running), then)
                            self.arrived.append(came)
                            running = self.block(plane_ahead(sign * left)) + came.astype(F32)
                            running = running.astype(BF)
                            self.second.append(running)
                        came = move(running)
                        self.arrived.append(came)
                        self.last.append(came)
                return self

            def total(self, then=()):
                total = self.own
                for came in tie(self.last, then):
                    total = total + came.astype(F32)
                return total.astype(BF)

        def chunk_scatter(keep, send, then):
            def by_plane(piece):
                return piece.reshape(piece.shape[:-2] + (planes, 2 * own_rows, piece.shape[-1]))

            if isinstance(send, (list, tuple)):
                away = [swap_c(piece) for piece in send]
                first = None
                if along and against and 2 * own_rows % 16 == 0:
                    where = jnp.stack([plane_ahead(along), plane_ahead(-against)]).astype(jnp.int32)
                    first = add_planes(keep, away, 2 * own_rows, where)
                away = [by_plane(piece) for piece in away]
                keep = [by_plane(piece) for piece in keep]

                def block(plane):
                    return jnp.stack(
                        [
                            pick(ours, plane, 1).astype(F32) + pick(theirs, plane, 1).astype(F32)
                            for ours, theirs in zip(keep, away)
                        ]
                    )

            else:
                first = None
                away = by_plane(tie(swap_c(send), then))
                keep = by_plane(keep)

                def block(plane):
                    return pick(keep, plane, 2).astype(F32) + pick(away, plane, 2).astype(F32)

            return RingScatter(block, first)

        before = [(), None]
        beside = [chunk_pieces[1][1 : along + 2]]
        totals = None
        scatters = []
        for chunk in range(len(CHUNKS)):
            last = chunk == len(CHUNKS) - 1
            results = feed_forward(
                behind,
                core,
                chunk_pieces[chunk],
                chunk_theirs[chunk],
                tie(normed, before[chunk]),
                cot_pieces,
                totals,
                last,
            )
            if last:
                results = tie(results, scatters[0].arrived[along])
                totals = results[3:]
                pieces = last_weights(core, turned, results[:3])
                keep, send = pieces[:3], pieces[3:]
            else:
                results = tie(results, beside[chunk])
                keep, send = results[:2]
                turned, totals = results[2:4], results[4:]
                own = tie(chunk_pieces[1][0], send)
                chunk_theirs[1] = [swap_c(piece) for piece in [own] + chunk_pieces[1][1:]]
            then = () if last else chunk_theirs[1][:-1]
            scatters.append(chunk_scatter(keep, send, then))
            if not last:
                scatters[0].go()
                before[1] = scatters[0].first
        last_sent = (keep, send)

        grad_out = cotangent[0].astype(F32)
        grad_hidden_norm, grad_gain_mlp = rms_backward(
            hidden, factor_mlp, gain_m, scatter_plane(totals[0], (last_sent, scatters[0].last[0], scatters[0].second))
        )
        grad_hidden = grad_out + grad_hidden_norm
        grad_pieces = gather_sequence(
            grad_hidden.astype(BF)
        )
        grad_q, grad_kv, d_early = attention_out(
            own_place,
            tie(grad_pieces, scatters[1].first),
            attn_weights,
            queries,
            keys,
            values,
            cosine,
            sine,
            first_keys,
            normed_attn_t,
            attended_t,
        )
        scatters[1].go()
        d_early = tie(d_early, scatters[0].last[-1])

        branch = trade(tie(totals[1], grad_pieces[1]).reshape(4, tok_rows, D), ("x", "y"))

        def owner_rows(partial):
            rows = partial.reshape(2, 2, planes, 2, own_rows, partial.shape[1])
            return pick(rows, 1 - y, 3), pick(rows, y, 3)

        grad_kv_theirs = swap_c(grad_kv)
        early_rows = owner_rows(d_early)
        kv_rows = KV * HD // (seq_count * fsdp_count)
        d_late, *in_terms = projection_out(
            own_rows,
            kv_rows,
            own_place,
            tie(grad_q, branch),
            grad_kv,
            grad_kv_theirs,
            attn_weights,
            normed_attn_t,
            cosine,
            sine,
            tokens_all,
            grad_gain_mlp[None],
        )
        def owner_scatter(away, stays, then=()):
            def block(plane):
                return pick(stays, plane, 2).astype(F32) + pick(away, plane, 2).astype(F32)

            return RingScatter(block).go(then, True)

        def chunk_sum(scatter, then):
            total = scatter.total(then).reshape(3, 2, 2, own_rows, -1)
            return total.transpose(1, 2, 0, 3, 4).reshape(4, 3, own_rows, -1)

        early_away = tie(swap_y(early_rows[0]), d_late)
        d_late, in_terms = tie((d_late, in_terms), scatters[1].arrived[along])
        late_leaves, late_stays = owner_rows(d_late)
        grad_normed_attn, in_leaves, in_back = scatter_sequence(*in_terms, (early_away, late_leaves))
        grad_input_norm, _ = rms_backward(
            inputs,
            rms_factor(inputs),
            gain_a,
            grad_normed_attn,
        )
        grad_input = grad_hidden + grad_input_norm
        result = hidden + jnp.sum(tie(branch, in_leaves).astype(F32), axis=0)
        result = result.astype(BF)
        first_sum = chunk_sum(scatters[0], in_leaves)
        gathered = [trade(first_sum, ("x", "y"))]

        late_away = tie(swap_y(late_leaves), in_back, scatters[1].last[-1])
        early = owner_scatter(early_away, early_rows[1], (in_back, gathered[0], scatters[1].last[0]))
        late = owner_scatter(late_away, late_stays)
        second_sum = chunk_sum(scatters[1], (early.first, late.first))
        gathered.append(trade(second_sum, ("x", "y")))
        d_gate_up, d_w_down = assemble(gathered)
        owned = [early.total(gathered), late.total(gathered)]
        owned = jnp.concatenate(owned, axis=-1).reshape(4, own_rows, -1)
        owned = trade(owned, ("x", "c")).astype(F32)
        early, late = owned[..., : 2 * group_cols], owned[..., 2 * group_cols :]
        d_w_output = jnp.concatenate([early[i, :, :group_cols] for i in range(4)], axis=1)
        d_w_query = jnp.concatenate([early[i, :, group_cols:] for i in range(4)], axis=1)
        d_w_key = jnp.concatenate([late[0, :, :HD], late[2, :, :HD]], axis=1)
        d_w_value = jnp.concatenate([late[1, :, :HD], late[3, :, :HD]], axis=1)
        sums = jnp.sum(late[:, :, HD:], axis=0)
        d_gain_attn, d_gain_mlp, d_bias_query = sums[:, 0], sums[:, 1], sums[:, 2]
        kv_sums = late[:, :kv_rows, HD + 3]
        d_bias_key = kv_sums[0] + kv_sums[2]
        d_bias_value = kv_sums[1] + kv_sums[3]
        return (
            result[None],
            grad_input[None],
            d_w_query,
            d_w_key,
            d_w_value,
            d_w_output,
            d_gate_up,
            d_w_down,
            d_bias_query,
            d_bias_key,
            d_bias_value,
            d_gain_attn,
            d_gain_mlp,
        )

    return local


def solution(mesh):
    seq, fsdp = mesh.shape["seq"], mesh.shape["fsdp"]
    grid = jax.sharding.Mesh(mesh.devices.reshape(seq // 2, 2, fsdp // 2, 2), ("x", "c", "z", "y"))
    by_rows, by_owner = ("z", "y"), ("x", "c", "z", "y")
    tokens = P(by_rows, ("x", "c"), None)
    rows, vector = P(by_rows, None), P(by_rows)
    owner, owner_vector = P(by_owner, None), P(by_owner)
    return jax.shard_map(
        build(seq, fsdp),
        mesh=grid,
        in_specs=(
            tokens,
            rows,
            rows,
            rows,
            rows,
            rows,
            P(by_rows, None, None),
            rows,
            vector,
            vector,
            vector,
            vector,
            vector,
            tokens,
        ),
        out_specs=(
            tokens,
            tokens,
            owner,
            owner,
            owner,
            owner,
            P(by_owner, None, None),
            owner,
            owner_vector,
            owner_vector,
            owner_vector,
            owner_vector,
            owner_vector,
        ),
        check_vma=False,
    )
```

```python
import functools

import jax
import jax.numpy as jnp
from jax import lax
from jax.experimental import pallas as pl
from jax.experimental.pallas import tpu as pltpu
from jax.sharding import PartitionSpec as P

D = 1536
HEADS = 12
KV = 2
HD = 128
FF = 8960
LANE = 128

epsilon = 1e-06
rope_base = 1000000.0
masked_value = -1e30
BF = jnp.bfloat16
F32 = jnp.float32
VMEM_BYTES = 60 * 1024 * 1024

CHIP_STARTS = (0, 18, 36, 52)
CHIP_VALID = ((0, 18), (0, 18), (0, 17), (1, 18))
TILE = 256
CHUNKS = ((0, 1280), (1280, 2304))
QUERY_ROWS = 256

anywhere = pl.BlockSpec(memory_space=pl.ANY)
in_vmem = pl.BlockSpec(memory_space=pltpu.VMEM)
in_smem = pl.BlockSpec(memory_space=pltpu.SMEM)


def rope_tables(positions):
    ladder = jnp.arange(HD // 2, dtype=F32)
    inverse = rope_base ** (-2.0 * ladder / HD)
    angles = positions.astype(F32)[:, None] * inverse[None, :]
    cosine, sine = jnp.cos(angles), jnp.sin(angles)
    return (
        jnp.concatenate([cosine, cosine], axis=-1),
        jnp.concatenate([-sine, sine], axis=-1),
    )


def rms_factor(value):
    return lax.rsqrt(jnp.mean(value * value, axis=-1, keepdims=True) + epsilon)


def rms_backward(value, factor, gain, grad):
    unit = value * factor
    weighted = grad * gain
    grad_gain = jnp.sum(grad * unit, axis=0)
    inner = jnp.mean(weighted * unit, axis=-1, keepdims=True)
    return (factor * (weighted - unit * inner), grad_gain)


def dot(left, right):
    return jnp.dot(left, right, preferred_element_type=F32)


def dot_t(left, right):
    return lax.dot_general(left, right, (((1,), (1,)), ((), ())), preferred_element_type=F32)


def t_dot(left, right):
    return lax.dot_general(left, right, (((0,), (0,)), ((), ())), preferred_element_type=F32)


def pick(array, index, axis=0):
    return lax.dynamic_index_in_dim(array, index, axis, keepdims=False)


def tie(value, *others):
    return lax.optimization_barrier((value, *others))[0] if jax.tree.leaves(others) else value


def kernel_params():
    return pltpu.CompilerParams(vmem_limit_bytes=VMEM_BYTES)


KERNEL_COST = pl.CostEstimate(flops=1_000_000, bytes_accessed=1_000_000, transcendentals=0)


def cut_body(place, gate_up, down, target, pairs, sems):
    cols = pl.ds(pl.multiple_of(place[0], LANE), target.shape[2])
    copies = [
        pltpu.make_async_copy(gate_up.at[:, :, cols], pairs, sems.at[0]),
        pltpu.make_async_copy(down.at[:, cols], target.at[2], sems.at[1]),
    ]
    for copy in copies:
        copy.start()
    copies[0].wait()
    target[0] = pairs[:, 0, :]
    target[1] = pairs[:, 1, :]
    copies[1].wait()
    empty = jnp.zeros((3, target.shape[1], LANE), BF)

    @pl.when(place[1] == 1)
    def _():
        target[:, :, 0:LANE] = empty

    @pl.when(place[1] == 2)
    def _():
        target[:, :, target.shape[2] - LANE :] = empty


def cut_columns(place, gate_up, down, cols):
    rows = down.shape[0]
    return pl.pallas_call(
        cut_body,
        out_shape=jax.ShapeDtypeStruct((3, rows, cols), BF),
        in_specs=[in_smem, anywhere, anywhere],
        out_specs=in_vmem,
        scratch_shapes=[pltpu.VMEM((rows, 2, cols), BF), pltpu.SemaphoreType.DMA((2,))],
        compiler_params=kernel_params(),
        cost_estimate=KERNEL_COST,
        name="cut_columns",
    )(place, gate_up, down)


def sequence_copies(s, sources, target, sems):
    near, far, other_near, other_far = sources
    rows = near.shape[0]
    x, c = s // 2, lax.rem(s, 2)
    copies = []
    for i, (source, owner) in enumerate(
        (
            (near, 2 * x + c),
            (far, 2 * (1 - x) + c),
            (other_near, 2 * x + 1 - c),
            (other_far, 2 * (1 - x) + 1 - c),
        )
    ):
        place = pl.multiple_of(owner * rows, LANE)
        copies.append(pltpu.make_async_copy(source, target.at[pl.ds(place, rows)], sems.at[i]))
    return copies


def split_store(s, block, value, targets):
    x, c = s // 2, lax.rem(s, 2)
    for i, target in enumerate(targets):
        far, away = i % 2, i // 2
        owner = 2 * (1 - x if far else x) + (1 - c if away else c)

        @pl.when(owner == block)
        def _():
            target[...] = value


def attention_in_body(planes, rows, *refs):
    places, own = refs[0], refs[1]
    mine = refs[2 : 2 + planes]
    theirs = refs[2 + planes : 2 + 2 * planes]
    sources = refs[2 + 2 * planes : 6 + 2 * planes]
    cosine, sine, starts = refs[6 + 2 * planes : 9 + 2 * planes]
    normed_t, queries, keys, values, attended_t = refs[9 + 2 * planes : 14 + 2 * planes]
    targets = refs[14 + 2 * planes : 18 + 2 * planes]
    weights, gains, tokens, small, attended, sems = refs[18 + 2 * planes :]
    length = tokens.shape[0]
    group_cols = queries.shape[1]
    blocks = 2 * planes
    s, y = own[0], own[1]
    copies = []
    for k in range(planes):
        for side, source in enumerate((mine[k], theirs[k])):
            block = places[k] * 2 + (y if side == 0 else 1 - y)
            first = pl.multiple_of(block * rows, 16)
            copies.append(
                pltpu.make_async_copy(
                    source.at[pl.ds(0, rows)], weights.at[pl.ds(first, rows)], sems.at[0, 2 * k + side]
                )
            )
            copies.append(
                pltpu.make_async_copy(
                    source.at[pl.ds(rows, 16)],
                    small.at[pl.ds(pl.multiple_of(block * 16, 16), 16)],
                    sems.at[1, 2 * k + side],
                )
            )
    for copy in copies:
        copy.start()
    for copy in copies:
        copy.wait()
    kv_own = KV * HD // blocks
    vectors = []
    for row, width in enumerate((rows, rows, rows, kv_own, kv_own)):
        vectors.append(
            jnp.concatenate(
                [small[pl.ds(16 * b + row, 1), 0:width].astype(F32) for b in range(blocks)], axis=1
            )
        )
    gains[0:1, :] = vectors[0]
    gains[1:2, :] = vectors[1]
    gains[2:3, :] = vectors[2]
    gains[3:4, 0 : KV * HD] = vectors[3]
    gains[4:5, 0 : KV * HD] = vectors[4]
    gain = gains[0:1, :]
    kv = s // 2
    bias = jnp.concatenate(
        [
            gains[2:3, pl.ds(pl.multiple_of(s * group_cols, LANE), group_cols)],
            gains[3:4, pl.ds(pl.multiple_of(kv * HD, LANE), HD)],
            gains[4:5, pl.ds(pl.multiple_of(kv * HD, LANE), HD)],
        ],
        axis=1,
    )
    wide = group_cols + 2 * HD
    heads = group_cols // HD
    x, c = s // 2, lax.rem(s, 2)
    owners = (2 * x + c, 2 * (1 - x) + c, 2 * x + 1 - c, 2 * (1 - x) + 1 - c)
    for source, owner in zip(sources, owners):
        r = pl.ds(pl.multiple_of(owner * QUERY_ROWS, QUERY_ROWS), QUERY_ROWS)
        tokens[r, :] = source[...]

    def project(at, carry):
        r = pl.ds(pl.multiple_of(at * QUERY_ROWS, QUERY_ROWS), QUERY_ROWS)
        value = tokens[r, :].astype(F32)
        low = (value * rms_factor(value) * gain).astype(BF)
        normed_t[:, r] = low.T
        qkv = dot(low, weights[:, 0:wide]) + bias
        cos_rows, sin_rows = cosine[r, :], sine[r, :]
        for head in range(heads + 1):
            one = qkv[:, head * HD : (head + 1) * HD]
            turned = (one * cos_rows + pltpu.roll(one, HD // 2, 1) * sin_rows).astype(BF)
            if head < heads:
                queries[r, head * HD : (head + 1) * HD] = turned
            else:
                keys[r, :] = turned
        values[r, :] = qkv[:, group_cols + HD :].astype(BF)
        return carry

    lax.fori_loop(0, length // QUERY_ROWS, project, 0)
    scaling = HD ** (-0.5)
    for first in range(0, length, QUERY_ROWS):
        r = pl.ds(first, QUERY_ROWS)
        reach = first + QUERY_ROWS
        query_place = first + lax.broadcasted_iota(jnp.int32, (QUERY_ROWS, reach), 0)
        key_place = lax.broadcasted_iota(jnp.int32, (QUERY_ROWS, reach), 1)
        allowed = (key_place <= query_place) & (key_place >= starts[r, :])
        hidden_keys = jnp.where(allowed, 0.0, masked_value)

        def attend(head, carry):
            cols = pl.ds(pl.multiple_of(head * HD, HD), HD)
            scores = dot_t(queries[r, cols], keys[0:reach, :]) * scaling + hidden_keys
            shifted = jnp.exp(scores - jnp.max(scores, axis=-1, keepdims=True))
            total = jnp.sum(shifted, axis=-1, keepdims=True)
            outcome = dot(shifted.astype(BF), values[0:reach, :])
            attended[:, cols] = (outcome / total).astype(BF)
            return carry

        lax.fori_loop(0, heads, attend, 0)
        attended_t[:, r] = attended[...].T
        term = dot_t(attended[...], weights[:, wide:]).astype(BF)
        split_store(s, first // QUERY_ROWS, term, targets)


def attention_in(places, own, mine, theirs, tokens, cosine, sine, starts, group_cols):
    planes = len(mine)
    rows = mine[0].shape[0] - 16
    length = cosine.shape[0]
    shapes = [
        jax.ShapeDtypeStruct((D, length), BF),
        jax.ShapeDtypeStruct((length, group_cols), BF),
        jax.ShapeDtypeStruct((length, HD), BF),
        jax.ShapeDtypeStruct((length, HD), BF),
        jax.ShapeDtypeStruct((group_cols, length), BF),
        *[jax.ShapeDtypeStruct((QUERY_ROWS, D), BF)] * 4,
        jax.ShapeDtypeStruct((D, mine[0].shape[1]), BF),
        jax.ShapeDtypeStruct((8, D), F32),
        jax.ShapeDtypeStruct((length, D), BF),
    ]
    return pl.pallas_call(
        functools.partial(attention_in_body, planes, rows),
        out_shape=shapes,
        in_specs=[in_smem, in_smem] + [anywhere] * (2 * planes) + [in_vmem] * 7,
        out_specs=[in_vmem] * len(shapes),
        scratch_shapes=[
            pltpu.VMEM((2 * planes * 16, mine[0].shape[1]), BF),
            pltpu.VMEM((QUERY_ROWS, group_cols), BF),
            pltpu.SemaphoreType.DMA((2, 2 * planes)),
        ],
        compiler_params=kernel_params(),
        cost_estimate=KERNEL_COST,
        name="attention_in",
    )(places, own, *mine, *theirs, *tokens, cosine, sine, starts)


def attention_out_body(
    own,
    near,
    far,
    other_near,
    other_far,
    weights,
    queries,
    keys,
    values,
    cosine,
    sine,
    starts,
    normed_t,
    attended_t,
    grad_q,
    grad_kv,
    d_early,
    grad,
    grad_k,
    grad_v,
    sems,
):
    copies = sequence_copies(own[0], (near, far, other_near, other_far), grad, sems)
    for copy in copies:
        copy.start()
    for copy in copies:
        copy.wait()
    length = grad.shape[0]
    group_cols = queries.shape[1]
    heads = group_cols // HD
    scaling = HD ** (-0.5)
    output = weights[:, group_cols + 2 * HD :]
    grad_k[...] = jnp.zeros_like(grad_k)
    grad_v[...] = jnp.zeros_like(grad_v)
    for first in range(0, length, QUERY_ROWS):
        r = pl.ds(first, QUERY_ROWS)
        reach = first + QUERY_ROWS
        grad_heads = dot(grad[r, :], output).astype(BF)
        query_place = first + lax.broadcasted_iota(jnp.int32, (QUERY_ROWS, reach), 0)
        key_place = lax.broadcasted_iota(jnp.int32, (QUERY_ROWS, reach), 1)
        allowed = (key_place <= query_place) & (key_place >= starts[r, :])
        cos_rows, sin_rows = cosine[r, :], sine[r, :]
        for head in range(heads):
            cols = slice(head * HD, (head + 1) * HD)
            one_query = queries[r, cols]
            one_grad = grad_heads[:, cols]
            scores = dot_t(one_query, keys[0:reach, :]) * scaling
            scores = jnp.where(allowed, scores, masked_value)
            shifted = jnp.exp(scores - jnp.max(scores, axis=-1, keepdims=True))
            probability = shifted * (1.0 / jnp.sum(shifted, axis=-1, keepdims=True))
            grad_prob = dot_t(one_grad, values[0:reach, :])
            weighted = probability * grad_prob
            inner = jnp.sum(weighted, axis=-1, keepdims=True)
            grad_low = (weighted - probability * inner).astype(BF)
            turned = (dot(grad_low, keys[0:reach, :]) * scaling).astype(BF).astype(F32)
            grad_q[r, cols] = (
                turned * cos_rows - pltpu.roll(turned, HD // 2, 1) * sin_rows
            ).astype(BF)
            grad_k[0:reach, :] += t_dot(grad_low, one_query)
            grad_v[0:reach, :] += t_dot(probability.astype(BF), one_grad)
    grad_kv[0] = (grad_k[...] * scaling).astype(BF)
    grad_kv[1] = grad_v[...].astype(BF)
    d_early[:, 0:group_cols] = dot(attended_t[...], grad[...]).astype(BF).T
    d_early[:, group_cols:] = dot(normed_t[...], grad_q[...]).astype(BF)


def attention_out(
    own, grad, weights, queries, keys, values, cosine, sine, starts, normed_t, attended_t
):
    length, group_cols = queries.shape
    return pl.pallas_call(
        attention_out_body,
        out_shape=[
            jax.ShapeDtypeStruct((length, group_cols), BF),
            jax.ShapeDtypeStruct((2, length, HD), BF),
            jax.ShapeDtypeStruct((D, 2 * group_cols), BF),
        ],
        in_specs=[in_smem] + [anywhere] * 4 + [in_vmem] * 9,
        out_specs=[in_vmem] * 3,
        scratch_shapes=[
            pltpu.VMEM((length, D), BF),
            pltpu.VMEM((length, HD), F32),
            pltpu.VMEM((length, HD), F32),
            pltpu.SemaphoreType.DMA((4,)),
        ],
        compiler_params=kernel_params(),
        cost_estimate=KERNEL_COST,
        name="attention_out",
    )(
        own,
        *grad,
        weights,
        queries,
        keys,
        values,
        cosine,
        sine,
        starts,
        normed_t,
        attended_t,
    )


def projection_out_body(
    own_rows,
    kv_rows,
    own,
    grad_q,
    ours,
    theirs,
    weights,
    normed_t,
    cosine,
    sine,
    tokens,
    gain_mlp,
    d_late,
    near,
    far,
    other_near,
    other_far,
    joined,
    sums,
):
    length, group_cols = grad_q.shape
    wide = group_cols + HD
    s = own[0]
    x, c = s // 2, lax.rem(s, 2)
    key_grad = ours[0].astype(F32) + theirs[0].astype(F32)
    key_grad = key_grad * cosine[...] - pltpu.roll(key_grad, HD // 2, 1) * sine[...]
    value_grad = ours[1].astype(F32) + theirs[1].astype(F32)
    joined[:, 0:group_cols] = grad_q[...]
    joined[:, group_cols:] = jnp.where(c == 0, key_grad, value_grad).astype(BF)
    one = jnp.where(
        c == 0,
        weights[:, group_cols : group_cols + HD],
        weights[:, group_cols + HD : group_cols + 2 * HD],
    )
    sums[...] = jnp.zeros_like(sums)
    gain_sum = jnp.zeros((1, D), F32)
    for first in range(0, length, QUERY_ROWS):
        r = pl.ds(first, QUERY_ROWS)
        term = dot_t(joined[r, 0:group_cols], weights[:, 0:group_cols]) + dot_t(
            joined[r, group_cols:], one
        )
        value = tokens[r, :].astype(F32)
        gain_sum += jnp.sum(term * (value * rms_factor(value)), axis=0, keepdims=True)
        split_store(
            s, first // QUERY_ROWS, term.astype(BF), (near, far, other_near, other_far)
        )

    bias = jnp.sum(joined[...].astype(F32), axis=0, keepdims=True)
    lane = lax.broadcasted_iota(jnp.int32, (HD, D // 2), 1)
    feature = lax.broadcasted_iota(jnp.int32, (HD, D // 2), 0)
    core, inner = lax.div(lane, D // 4), lax.rem(lane, D // 4)
    owner, row = lax.div(inner, own_rows), lax.rem(inner, own_rows)
    spot = core * (HD // 2) + owner * kv_rows + row
    chosen = jnp.where((spot == feature) & (row < kv_rows), 1.0, 0.0).astype(BF)
    spread = dot(bias[:, group_cols:].astype(BF), chosen)
    sums[0:1, :] = gain_sum
    sums[1:2, :] = gain_mlp[...]
    sums[2:3, pl.ds(pl.multiple_of(s * group_cols, LANE), group_cols)] = bias[:, 0:group_cols]
    sums[3:4, pl.ds(pl.multiple_of(x * (D // 2), LANE), D // 2)] = spread
    d_late[:, 0:HD] = dot(normed_t[...], joined[:, group_cols:]).astype(BF)
    d_late[:, HD:] = sums[...].T.astype(BF)


def projection_out(
    own_rows,
    kv_rows,
    own,
    grad_q,
    ours,
    theirs,
    weights,
    normed_t,
    cosine,
    sine,
    tokens,
    gain_mlp,
):
    length, group_cols = grad_q.shape
    wide = group_cols + HD
    return pl.pallas_call(
        functools.partial(projection_out_body, own_rows, kv_rows),
        out_shape=[
            jax.ShapeDtypeStruct((D, HD + LANE), BF),
            *[jax.ShapeDtypeStruct((QUERY_ROWS, D), BF)] * 4,
        ],
        in_specs=[in_smem] + [in_vmem] * 9,
        out_specs=[in_vmem] * 5,
        scratch_shapes=[pltpu.VMEM((length, wide), BF), pltpu.VMEM((LANE, D), F32)],
        compiler_params=kernel_params(),
        cost_estimate=KERNEL_COST,
        name="projection_out",
    )(own, grad_q, ours, theirs, weights, normed_t, cosine, sine, tokens, gain_mlp)


def plane_copies(chip, parts, target, sems, first):
    x, y = lax.div(chip, 2), lax.rem(chip, 2)
    copies = []
    for i, part in enumerate(parts):
        owner = 2 * (1 - x if i % 2 else x) + (1 - y if i // 2 else y)
        r = pl.ds(pl.multiple_of(owner * QUERY_ROWS, QUERY_ROWS), QUERY_ROWS)
        copies.append(pltpu.make_async_copy(part, target.at[r], sems.at[first + i]))
    return copies


def weight_terms(c, normed_t, cotangent_t, grad_gate, grad_up, activated, keep, send):
    owner_rows = D // 4
    for part in range(2):
        for targets, core in ((send, 1 - c), (keep, c)):
            r = pl.ds(pl.multiple_of((2 * part + core) * owner_rows, LANE), owner_rows)
            targets[0][part] = dot(normed_t[r, :], grad_gate[...]).astype(BF)
            targets[1][part] = dot(normed_t[r, :], grad_up[...]).astype(BF)
            targets[2][part] = dot(cotangent_t[r, :], activated[...]).astype(BF)


def last_weights_body(
    own, normed_t, cotangent_t, grad_gate, grad_up, activated, *targets
):
    weight_terms(
        own[0], normed_t, cotangent_t, grad_gate, grad_up, activated, targets[:3], targets[3:]
    )


def last_weights(own, turned, parts):
    tokens, cols = parts[0].shape
    owner_rows = D // 4
    piece = jax.ShapeDtypeStruct((2, owner_rows, cols), BF)
    piece_spec = pl.BlockSpec((2, owner_rows, TILE), lambda i: (0, 0, i))
    whole = pl.BlockSpec((D, tokens), lambda i: (0, 0), pipeline_mode=pl.Buffered(1))
    part = pl.BlockSpec((tokens, TILE), lambda i: (0, i))
    return pl.pallas_call(
        last_weights_body,
        grid=(cols // TILE,),
        out_shape=[piece] * 6,
        in_specs=[in_smem, whole, whole, part, part, part],
        out_specs=[piece_spec] * 6,
        compiler_params=kernel_params(),
        cost_estimate=KERNEL_COST,
        name="last_weights",
    )(own, *turned, *parts)


def feed_forward_body(planes, rows, first, last, *refs):
    places, own = refs[0], refs[1]
    mine = refs[2 : 2 + planes]
    theirs = refs[2 + planes : 2 + 2 * planes]
    rest = list(refs[2 + 2 * planes :])
    normed_parts, cot_parts = [[rest.pop(0) for _ in range(4)] for _ in range(2)]
    totals_in = [] if first else [rest.pop(0) for _ in range(2)]
    if last:
        grad_gate, grad_up, activated = [rest.pop(0) for _ in range(3)]
    else:
        keep, send = [rest.pop(0) for _ in range(2)]
    turned_out = [rest.pop(0) for _ in range(2)] if first else []
    totals_out = [rest.pop(0) for _ in range(2)]
    weights, grad_total, branch_total = [rest.pop(0) for _ in range(3)]
    normed, cotangent, weight_sems, sems = [rest.pop(0) for _ in range(4)]
    low = [rest.pop(0) for _ in range(2)]
    if not last:
        grad_gate, grad_up, activated, normed_t, cotangent_t = rest
    step, steps = pl.program_id(0), pl.num_programs(0)
    tokens = normed.shape[0]
    c, chip = own[0], own[1]
    normed_loads = plane_copies(chip, normed_parts, normed, sems, 8)
    cot_loads = plane_copies(chip, cot_parts, cotangent, sems, 12)
    turned_ends = [
        pltpu.make_async_copy(source, target, sems.at[16 + i])
        for i, (source, target) in enumerate(
            zip((normed_t, cotangent_t) if first else (), turned_out)
        )
    ]
    fills = [
        pltpu.make_async_copy(source, target, sems.at[i])
        for i, (source, target) in enumerate(zip(totals_in, low))
    ]
    ends = [
        pltpu.make_async_copy(source, target, sems.at[2 + i])
        for i, (source, target) in enumerate(zip(low, totals_out))
    ]

    def weight_copies(at, slot):
        cols = pl.ds(pl.multiple_of(at * TILE, TILE), TILE)
        copies = []
        for k in range(planes):
            base = places[k] * (2 * rows)
            for side, source in enumerate((mine[k], theirs[k])):
                start = base + (c if side == 0 else 1 - c) * rows
                copies.append(
                    pltpu.make_async_copy(
                        source.at[:, :, cols],
                        weights.at[slot, :, pl.ds(pl.multiple_of(start, 16), rows), :],
                        weight_sems.at[slot, 2 * k + side],
                    )
                )
        return copies

    slot = lax.rem(step, 2)

    @pl.when(step == 0)
    def _():
        for load in normed_loads:
            load.start()
        for copy in weight_copies(0, 0):
            copy.start()
        for load in cot_loads + fills:
            load.start()

    @pl.when(step + 1 < steps)
    def _():
        for copy in weight_copies(step + 1, 1 - slot):
            copy.start()

    @pl.when(step == 0)
    def _():
        grad_total[...] = jnp.zeros_like(grad_total)
        branch_total[...] = jnp.zeros_like(branch_total)
        for load in normed_loads:
            load.wait()

    for copy in weight_copies(step, slot):
        copy.wait()

    block = min(256, tokens)
    for start in range(0, tokens, block):
        r = pl.ds(start, block)
        some = normed[r, :]
        gate = dot(some, weights[slot, 0])
        up = dot(some, weights[slot, 1])
        if start == 0:

            @pl.when(step == 0)
            def _():
                for load in cot_loads:
                    load.wait()

        grad_act = dot(cotangent[r, :], weights[slot, 2])
        sigma = jax.nn.sigmoid(gate)
        silu = gate * sigma
        activated[r, :] = (silu * up).astype(BF)
        grad_gate[r, :] = (grad_act * up * (sigma + silu * (1.0 - sigma))).astype(BF)
        grad_up[r, :] = (grad_act * silu).astype(BF)

    for start in range(0, tokens, block):
        r = pl.ds(start, block)
        grad_total[r, :] += dot_t(grad_gate[r, :], weights[slot, 0]) + dot_t(
            grad_up[r, :], weights[slot, 1]
        )
        branch_total[r, :] += dot_t(activated[r, :], weights[slot, 2])

    @pl.when(step == steps - 1)
    def _():
        for fill in fills:
            fill.wait()
        for target, total in zip(low, (grad_total, branch_total)):
            value = total[...]
            target[...] = (value if first else value + target[...].astype(F32)).astype(BF)
        for end in ends:
            end.start()

    if not last:

        @pl.when(step == 0)
        def _():
            for source, target in ((normed, normed_t), (cotangent, cotangent_t)):
                for start in range(0, D, TILE):
                    cols = pl.ds(start, TILE)
                    target[cols, :] = source[:, cols].T
            for end in turned_ends:
                end.start()

        keep, send = [[piece.at[kind] for kind in range(3)] for piece in (keep, send)]
        weight_terms(c, normed_t, cotangent_t, grad_gate, grad_up, activated, keep, send)

    @pl.when(step == steps - 1)
    def _():
        for end in ends + turned_ends:
            end.wait()


def feed_forward(places, own, mine, theirs, normed, cotangent, totals, last):
    planes = len(mine)
    rows, cols = mine[0].shape[1:]
    tokens = 4 * QUERY_ROWS
    first = totals is None
    totals = () if first else totals
    if last:
        shapes = [jax.ShapeDtypeStruct((tokens, cols), BF)] * 3
        specs = [pl.BlockSpec((tokens, TILE), lambda i, *_: (0, i))] * 3
    else:
        owner_rows = D // 4
        shapes = [jax.ShapeDtypeStruct((3, 2, owner_rows, cols), BF)] * 2
        specs = [pl.BlockSpec((3, 2, owner_rows, TILE), lambda i, *_: (0, 0, 0, i))] * 2
    blocks = len(shapes)
    if first:
        shapes += [jax.ShapeDtypeStruct((D, tokens), BF)] * 2
    shapes += [jax.ShapeDtypeStruct((tokens, D), BF)] * 2
    scratch = [pltpu.VMEM((2, 3, D, TILE), BF)]
    scratch += [pltpu.VMEM((tokens, D), F32)] * 2
    scratch += [pltpu.VMEM((tokens, D), BF)] * 2
    scratch += [pltpu.SemaphoreType.DMA((2, 2 * planes)), pltpu.SemaphoreType.DMA((18,))]
    scratch += [pltpu.VMEM((tokens, D), BF)] * 2
    if not last:
        scratch += [pltpu.VMEM((tokens, TILE), BF)] * 3 + [pltpu.VMEM((D, tokens), BF)] * 2
    inputs = [*mine, *theirs, *normed, *cotangent, *totals]
    return pl.pallas_call(
        functools.partial(feed_forward_body, planes, rows, first, last),
        grid=(cols // TILE,),
        out_shape=shapes,
        in_specs=[in_smem, in_smem] + [anywhere] * len(inputs),
        out_specs=specs + [anywhere] * (len(shapes) - blocks),
        scratch_shapes=scratch,
        compiler_params=kernel_params(),
        cost_estimate=KERNEL_COST,
        name="feed_forward",
    )(places, own, *inputs)


def add_planes_body(kinds, count, rows, where, *refs):
    ours, theirs = refs[:kinds], refs[kinds : 2 * kinds]
    targets = refs[2 * kinds : 2 * kinds + count]
    held, sems = refs[2 * kinds + count :]
    copies = []
    for i in range(count):
        r = pl.ds(pl.multiple_of(where[i] * rows, 16), rows)
        for kind in range(3):
            for side, sources in enumerate((ours, theirs)):
                source = sources[kind] if kinds == 3 else sources[0].at[kind]
                copies.append(
                    pltpu.make_async_copy(
                        source.at[:, r, :], held.at[i, kind, side], sems.at[i, kind, side]
                    )
                )
    for copy in copies:
        copy.start()
    for i in range(count):
        for kind in range(3):
            for side in range(2):
                copies[(i * 3 + kind) * 2 + side].wait()
            total = held[i, kind, 0].astype(F32) + held[i, kind, 1].astype(F32)
            targets[i][kind] = total.astype(BF)


def add_planes(ours, theirs, rows, where):
    count, cols = where.shape[0], ours[0].shape[-1]
    return pl.pallas_call(
        functools.partial(add_planes_body, len(ours), count, rows),
        out_shape=[jax.ShapeDtypeStruct((3, 2, rows, cols), BF)] * count,
        in_specs=[in_smem] + [anywhere] * (2 * len(ours)),
        out_specs=[in_vmem] * count,
        scratch_shapes=[
            pltpu.VMEM((count, 3, 2, 2, rows, cols), BF),
            pltpu.SemaphoreType.DMA((count, 3, 2)),
        ],
        compiler_params=kernel_params(),
        cost_estimate=KERNEL_COST,
        name="add_planes",
    )(where, *ours, *theirs)


def assemble_body(*refs):
    parts, gate_up, down = refs[:-2], refs[-2], refs[-1]
    for chip, (start, (first, end)) in enumerate(zip(CHIP_STARTS, CHIP_VALID)):
        for part, (low, high) in zip(parts, CHUNKS):
            from_col = max(first * LANE, low)
            to_col = min(end * LANE, high)
            here = slice(from_col - low, to_col - low)
            there = slice(start * LANE + from_col, start * LANE + to_col)
            for kind in range(2):
                gate_up[:, kind, there] = part[chip, kind, :, here].astype(F32)
            down[:, there] = part[chip, 2, :, here].astype(F32)


def assemble(parts):
    rows = parts[0].shape[2]
    return pl.pallas_call(
        assemble_body,
        out_shape=[
            jax.ShapeDtypeStruct((rows, 2, FF), F32),
            jax.ShapeDtypeStruct((rows, FF), F32),
        ],
        in_specs=[in_vmem] * len(parts),
        out_specs=[in_vmem] * 2,
        compiler_params=kernel_params(),
        cost_estimate=KERNEL_COST,
        name="assemble",
    )(*parts)


def build(seq_count, fsdp_count):
    planes = fsdp_count // 2
    order = list(range(0, 1)) + list(range(1, planes, 2)) + list(range(2, planes, 2))[::-1]
    place = [order.index(plane) for plane in range(planes)]
    after = {order[i]: order[(i + 1) % planes] for i in range(planes)}
    ring_perm = [(z, after[z]) for z in range(planes)]
    other = [(0, 1), (1, 0)]
    rows_perm = [(0, 1), (3, 2)]

    def swap_x(value):
        return lax.ppermute(value, "x", other)

    def swap_c(value):
        return lax.ppermute(value, "c", other)

    def swap_y(value):
        return lax.ppermute(value, "y", other)

    def swap_xy(value):
        return lax.ppermute(value, ("x", "y"), [(i, 3 - i) for i in range(4)])

    def send_rows(value):
        return lax.ppermute(value, ("c", "y"), rows_perm)

    def ring(value):
        return lax.ppermute(value, "z", ring_perm)

    def ring_back(value):
        return lax.ppermute(value, "z", [(j, i) for i, j in ring_perm])

    def trade(blocks, axes):
        return lax.all_to_all(blocks, axes, split_axis=0, concat_axis=0, tiled=True)

    along = (planes - 1) // 2
    against = planes - 1 - along
    steps_behind = list(range(along + 1)) + [-i for i in range(1, against + 1)]

    def local(
        tokens,
        positions,
        w_query,
        w_key,
        w_value,
        w_output,
        gate_up,
        w_down,
        bias_query,
        bias_key,
        bias_value,
        gain_attn,
        gain_mlp,
        cotangent,
    ):
        x, c, z, y = [lax.axis_index(axis) for axis in ("x", "c", "z", "y")]
        s = 2 * x + c
        ring_order = jnp.array(order, jnp.int32)
        ring_place = jnp.array(place, jnp.int32)
        behind = ring_order[(ring_place[z] - jnp.array(steps_behind)) % planes].astype(jnp.int32)

        def ring_gather(piece, then=()):
            ahead, back = [piece], [piece]
            for _ in range(along):
                ahead.append(ring(ahead[-1]))
            for step in range(against):
                back.append(ring_back(tie(back[-1], then) if step else back[-1]))
            return ahead + back[1:]
        core = jnp.stack([c, 2 * x + y]).astype(jnp.int32)
        own_place = jnp.stack([s, y]).astype(jnp.int32)

        tok_rows = tokens.shape[1]
        length = tok_rows * seq_count
        per_group = HEADS // seq_count
        group_cols = per_group * HD
        w_rows = w_query.shape[0]
        own_rows = D // (seq_count * fsdp_count)

        def gather_sequence(own, then=()):
            far = tie(swap_x(own), then)
            theirs = swap_c(own)
            return [own, far, theirs, swap_c(tie(far, theirs))]

        def gather_plane(own):
            return [own, swap_x(own), swap_y(own), swap_xy(own)]

        def scatter_plane(terms, then=()):
            came = trade(terms.reshape(4, tok_rows, D), ("x", "y"))
            return jnp.sum(tie(came, then).astype(F32), axis=0)

        wide = group_cols + 2 * HD
        small_rows = jnp.stack(
            [
                jnp.pad(vector, (0, wide + group_cols - vector.shape[0]))
                for vector in (gain_attn, gain_mlp, bias_query, bias_key, bias_value)
            ]
        )
        small_rows = jnp.pad(small_rows, ((0, 11), (0, 0)))
        attn_own = jnp.concatenate(
            [
                lax.dynamic_slice_in_dim(w_query, s * group_cols, group_cols, 1),
                lax.dynamic_slice_in_dim(w_key, x * HD, HD, 1),
                lax.dynamic_slice_in_dim(w_value, x * HD, HD, 1),
                lax.dynamic_slice_in_dim(w_output, s * group_cols, group_cols, 1),
            ],
            axis=1,
        )
        attn_payload = jnp.concatenate([attn_own, small_rows], axis=0)
        chunk_places = []
        for low, high in CHUNKS:
            table = []
            for start, (first, end) in zip(CHIP_STARTS, CHIP_VALID):
                edge = 1 if low == 0 and first > 0 else 0
                edge = 2 if high > end * LANE else edge
                table.append((start * LANE + low, edge))
            table = jnp.array(table, jnp.int32)
            chunk_places.append((table[2 * x + y], table[2 * x + 1 - y]))

        def cut(chunk, whose, then):
            low, high = CHUNKS[chunk]
            return cut_columns(tie(chunk_places[chunk][whose], then), gate_up, w_down, high - low)

        sent = cut(0, 1, ())
        attn_payload = tie(attn_payload, sent)
        token_far = swap_x(tokens[0])
        token_pieces = [tokens[0], token_far, swap_c(tokens[0])]
        attn_pieces = ring_gather(attn_payload, token_pieces[2])
        first_back = along + 1
        attn_theirs = [swap_y(tie(attn_pieces[0], attn_pieces[1]))]
        attn_theirs += [swap_y(piece) for piece in attn_pieces[1:-1]]

        came, kept = send_rows(sent), cut(0, 0, attn_payload)
        cuts = [(cut(1, 1, kept), cut(1, 0, kept))]
        kept, came = tie(
            (kept, came), attn_pieces[1:], attn_theirs[first_back], token_pieces[1:3], cuts
        )
        payloads = [jnp.where(c == y, kept, came)]
        token_pieces.append(swap_c(tie(token_far, payloads[0])))
        attn_theirs.append(swap_y(tie(attn_pieces[-1], payloads[0])))
        own_swapped = swap_c(tie(payloads[0], attn_theirs))
        for sent, kept in cuts:
            came = send_rows(tie(sent, attn_theirs))
            payloads.append(jnp.where(c == y, kept, came))
        chunk_pieces = [ring_gather(payloads[0])]
        cot_x = swap_x(tie(cotangent[0], cuts))
        cot_y = swap_y(tie(cotangent[0], attn_theirs))

        seq_positions = positions[0]
        cosine, sine = rope_tables(seq_positions)
        first_keys = (jnp.arange(length, dtype=jnp.int32) - seq_positions)[:, None]
        (
            normed_attn_t,
            queries,
            keys,
            values,
            attended_t,
            *out_terms,
            attn_weights,
            gains,
            tokens_all,
        ) = attention_in(
            behind,
            own_place,
            attn_pieces,
            attn_theirs,
            tie(token_pieces, cot_x),
            cosine,
            sine,
            first_keys,
            group_cols,
        )
        inputs = tokens[0].astype(F32)
        out_terms, queries, keys, values, attended_t, gains = tie(
            (out_terms, queries, keys, values, attended_t, gains),
            chunk_pieces[0][1 : along + 2],
            came,
            cot_y,
            own_swapped,
        )

        def scatter_sequence(near, far, other_near, other_far, then=()):
            leaves = (far.astype(F32) + swap_c(other_far).astype(F32)).astype(BF)
            leaves = tie(leaves, *then)
            back = swap_x(leaves)
            stays = near.astype(F32) + swap_c(other_near).astype(F32)
            return stays + back.astype(F32), leaves, back

        gain_a, gain_m = gains[0], gains[1]
        branch_attn, out_leaves, _ = scatter_sequence(*out_terms)
        cot_pieces = [cotangent[0], cot_x, cot_y, swap_y(tie(cot_x, out_terms))]
        hidden = inputs + tie(branch_attn, cot_pieces[3])
        factor_mlp = rms_factor(hidden)
        normed_own = (hidden * factor_mlp * gain_m).astype(BF)
        normed = gather_plane(normed_own)
        chunk_theirs = [[own_swapped] + [swap_c(piece) for piece in chunk_pieces[0][1:-1]], []]
        chunk_theirs[0].append(swap_c(tie(chunk_pieces[0][-1], normed[1:])))
        chunk_pieces.append(ring_gather(tie(payloads[1], normed_own)))

        def plane_ahead(steps):
            return ring_order[(ring_place[z] + steps) % planes]

        class RingScatter:
            def __init__(self, block, first=None):
                self.block = block
                self.own = block(z)
                self.first = first or [
                    block(plane_ahead(sign * steps)).astype(BF)
                    for steps, sign in ((along, 1), (against, -1))
                    if steps
                ]

            def go(self, then=(), together=False, parts=False):
                self.arrived, self.second, self.last = [], [], []
                firsts = list(self.first)
                for steps, sign, move in ((along, 1, ring), (against, -1, ring_back)):
                    then = (then, self.last) if together else then
                    if steps:
                        running = firsts.pop(0)
                        for left in range(steps - 1, 0, -1):
                            came = tie(move(running), then)
                            self.arrived.append(came)
                            running = self.block(plane_ahead(sign * left)) + came.astype(F32)
                            running = running.astype(BF)
                            self.second.append(running)
                        if parts and sign < 0:
                            self.parts = [move(running[:2]), move(running[2:])]
                            came = self.parts
                        else:
                            came = move(running)
                        self.arrived.append(came)
                        self.last.append(came)
                return self

            def total(self, then=()):
                total = self.own
                for came in tie(self.last, then):
                    came = jnp.concatenate(came, axis=0) if isinstance(came, list) else came
                    total = total + came.astype(F32)
                return total.astype(BF)

        def chunk_scatter(keep, send, then):
            def by_plane(piece):
                return piece.reshape(piece.shape[:-2] + (planes, 2 * own_rows, piece.shape[-1]))

            if isinstance(send, (list, tuple)):
                away = [swap_c(piece) for piece in send]
                first = None
                if along and against and 2 * own_rows % 16 == 0:
                    where = jnp.stack([plane_ahead(along), plane_ahead(-against)]).astype(jnp.int32)
                    first = add_planes(keep, away, 2 * own_rows, where)
                away = [by_plane(piece) for piece in away]
                keep = [by_plane(piece) for piece in keep]

                def block(plane):
                    return jnp.stack(
                        [
                            pick(ours, plane, 1).astype(F32) + pick(theirs, plane, 1).astype(F32)
                            for ours, theirs in zip(keep, away)
                        ]
                    )

            else:
                first = None
                away = by_plane(tie(swap_c(send), then))
                keep = by_plane(keep)

                def block(plane):
                    return pick(keep, plane, 2).astype(F32) + pick(away, plane, 2).astype(F32)

            return RingScatter(block, first)

        before = [(), None]
        beside = [chunk_pieces[1][1 : along + 2]]
        totals = None
        scatters = []
        for chunk in range(len(CHUNKS)):
            last = chunk == len(CHUNKS) - 1
            results = feed_forward(
                behind,
                core,
                chunk_pieces[chunk],
                chunk_theirs[chunk],
                tie(normed, before[chunk]),
                cot_pieces,
                totals,
                last,
            )
            if last:
                results = tie(results, scatters[0].arrived[along])
                totals = results[3:]
                pieces = last_weights(core, turned, results[:3])
                keep, send = pieces[:3], pieces[3:]
            else:
                results = tie(results, beside[chunk])
                keep, send = results[:2]
                turned, totals = results[2:4], results[4:]
                own = tie(chunk_pieces[1][0], send)
                chunk_theirs[1] = [swap_c(piece) for piece in [own] + chunk_pieces[1][1:]]
            then = () if last else chunk_theirs[1][:-1]
            scatters.append(chunk_scatter(keep, send, then))
            if not last:
                scatters[0].go(parts=True)
                before[1] = scatters[0].first
        last_sent = (keep, send)

        grad_out = cotangent[0].astype(F32)
        grad_hidden_norm, grad_gain_mlp = rms_backward(
            hidden, factor_mlp, gain_m, scatter_plane(totals[0], (last_sent, scatters[0].second))
        )
        grad_hidden = grad_out + grad_hidden_norm
        grad_pieces = gather_sequence(
            grad_hidden.astype(BF), (scatters[0].parts[0], scatters[0].last[0])
        )
        grad_q, grad_kv, d_early = attention_out(
            own_place,
            tie(grad_pieces, scatters[1].first),
            attn_weights,
            queries,
            keys,
            values,
            cosine,
            sine,
            first_keys,
            normed_attn_t,
            attended_t,
        )
        scatters[1].go()

        branch = trade(tie(totals[1], grad_pieces[1]).reshape(4, tok_rows, D), ("x", "y"))

        def owner_rows(partial):
            rows = partial.reshape(2, 2, planes, 2, own_rows, partial.shape[1])
            return pick(rows, 1 - y, 3), pick(rows, y, 3)

        grad_kv_theirs = swap_c(grad_kv)
        early_rows = owner_rows(d_early)
        kv_rows = KV * HD // (seq_count * fsdp_count)
        d_late, *in_terms = projection_out(
            own_rows,
            kv_rows,
            own_place,
            tie(grad_q, branch),
            grad_kv,
            grad_kv_theirs,
            attn_weights,
            normed_attn_t,
            cosine,
            sine,
            tokens_all,
            grad_gain_mlp[None],
        )
        def owner_scatter(away, stays, then=()):
            def block(plane):
                return pick(stays, plane, 2).astype(F32) + pick(away, plane, 2).astype(F32)

            return RingScatter(block).go(then, True)

        def chunk_sum(scatter, then):
            total = scatter.total(then).reshape(3, 2, 2, own_rows, -1)
            return total.transpose(1, 2, 0, 3, 4).reshape(4, 3, own_rows, -1)

        early_away = tie(swap_y(early_rows[0]), d_late)
        d_late, in_terms = tie((d_late, in_terms), scatters[1].arrived[along])
        late_leaves, late_stays = owner_rows(d_late)
        grad_normed_attn, in_leaves, in_back = scatter_sequence(*in_terms, (early_away, late_leaves))
        grad_input_norm, _ = rms_backward(
            inputs,
            rms_factor(inputs),
            gain_a,
            grad_normed_attn,
        )
        grad_input = grad_hidden + grad_input_norm
        result = hidden + jnp.sum(tie(branch, in_leaves).astype(F32), axis=0)
        result = result.astype(BF)
        first_sum = chunk_sum(scatters[0], in_leaves)
        gathered = [trade(first_sum, ("x", "y"))]

        late_away = tie(swap_y(late_leaves), in_back, scatters[1].last[-1])
        early = owner_scatter(early_away, early_rows[1], (in_back, gathered[0], scatters[1].last[0]))
        late = owner_scatter(late_away, late_stays)
        second_sum = chunk_sum(scatters[1], (early.first, late.first))
        gathered.append(trade(second_sum, ("x", "y")))
        d_gate_up, d_w_down = assemble(gathered)
        owned = [early.total(gathered), late.total(gathered)]
        owned = jnp.concatenate(owned, axis=-1).reshape(4, own_rows, -1)
        owned = trade(owned, ("x", "c")).astype(F32)
        early, late = owned[..., : 2 * group_cols], owned[..., 2 * group_cols :]
        d_w_output = jnp.concatenate([early[i, :, :group_cols] for i in range(4)], axis=1)
        d_w_query = jnp.concatenate([early[i, :, group_cols:] for i in range(4)], axis=1)
        d_w_key = jnp.concatenate([late[0, :, :HD], late[2, :, :HD]], axis=1)
        d_w_value = jnp.concatenate([late[1, :, :HD], late[3, :, :HD]], axis=1)
        sums = jnp.sum(late[:, :, HD:], axis=0)
        d_gain_attn, d_gain_mlp, d_bias_query = sums[:, 0], sums[:, 1], sums[:, 2]
        kv_sums = late[:, :kv_rows, HD + 3]
        d_bias_key = kv_sums[0] + kv_sums[2]
        d_bias_value = kv_sums[1] + kv_sums[3]
        return (
            result[None],
            grad_input[None],
            d_w_query,
            d_w_key,
            d_w_value,
            d_w_output,
            d_gate_up,
            d_w_down,
            d_bias_query,
            d_bias_key,
            d_bias_value,
            d_gain_attn,
            d_gain_mlp,
        )

    return local


def solution(mesh):
    seq, fsdp = mesh.shape["seq"], mesh.shape["fsdp"]
    grid = jax.sharding.Mesh(mesh.devices.reshape(seq // 2, 2, fsdp // 2, 2), ("x", "c", "z", "y"))
    by_rows, by_owner = ("z", "y"), ("x", "c", "z", "y")
    tokens = P(by_rows, ("x", "c"), None)
    rows, vector = P(by_rows, None), P(by_rows)
    owner, owner_vector = P(by_owner, None), P(by_owner)
    return jax.shard_map(
        build(seq, fsdp),
        mesh=grid,
        in_specs=(
            tokens,
            rows,
            rows,
            rows,
            rows,
            rows,
            P(by_rows, None, None),
            rows,
            vector,
            vector,
            vector,
            vector,
            vector,
            tokens,
        ),
        out_specs=(
            tokens,
            tokens,
            owner,
            owner,
            owner,
            owner,
            P(by_owner, None, None),
            owner,
            owner_vector,
            owner_vector,
            owner_vector,
            owner_vector,
            owner_vector,
        ),
        check_vma=False,
    )
```
